128 devices in a mesh: dp: 32 (over z, x_lo, y), tensor: 4 (over x_hi, core).
Axes of the slice: x: 4 (x_hi: 2, x_lo: 2; x = x_hi * 2 + x_lo), y: 4, z: 4, core: 2. Of those that a mesh axis runs over, the one named last changes fastest.
Arguments:
- tokens: bfloat16 [16384, 1024], P(('dp', 'tensor')), may hold values from -6 to 6
- segment_ids: int32 [16384], P('dp'), may hold values from 0 to 3, as said below
- cotangent: bfloat16 [16384, 1024], P(('dp', 'tensor')), may hold values from -6 to 6
- attn_norm: float32 [2, 1024], replicated, may hold values from 0.1 to 1.9
- q_weight: bfloat16 [2, 1024, 2048], P(None, 'dp', 'tensor'), may hold values from -0.1875 to 0.1875
- key_projection: bfloat16 [2, 1024, 1024], P(None, 'dp', 'tensor'), may hold values from -0.1875 to 0.1875
- value_projection: bfloat16 [2, 1024, 1024], P(None, 'dp', 'tensor'), may hold values from -0.1875 to 0.1875
- o_weight: bfloat16 [2, 2048, 1024], P(None, 'tensor', 'dp'), may hold values from -1.5 to 1.5
- q_gain: float32 [2, 128], replicated, may hold values from 0.1 to 1.9
- k_gain: float32 [2, 128], replicated, may hold values from 0.1 to 1.9
- mlp_norm: float32 [2, 1024], replicated, may hold values from 0.1 to 1.9
- gate_weight: bfloat16 [2, 1024, 3072], P(None, 'dp', 'tensor'), may hold values from -0.1875 to 0.1875
- up_weight: bfloat16 [2, 1024, 3072], P(None, 'dp', 'tensor'), may hold values from -0.1875 to 0.1875
- down_weight: bfloat16 [2, 3072, 1024], P(None, 'tensor', 'dp'), may hold values from -0.109375 to 0.109375
Outputs:
- output: bfloat16 [16384, 1024], P(('dp', 'tensor'))
- input_grad: float32 [16384, 1024], P(('dp', 'tensor'))
- attn_norm_grad: float32 [2, 1024], replicated
- q_weight_grad: float32 [2, 1024, 2048], P(None, 'dp', 'tensor')
- k_weight_grad: float32 [2, 1024, 1024], P(None, 'dp', 'tensor')
- v_weight_grad: float32 [2, 1024, 1024], P(None, 'dp', 'tensor')
- o_weight_grad: float32 [2, 2048, 1024], P(None, 'tensor', 'dp')
- q_gain_grad: float32 [2, 128], replicated
- k_gain_grad: float32 [2, 128], replicated
- mlp_norm_grad: float32 [2, 1024], replicated
- gate_weight_grad: float32 [2, 1024, 3072], P(None, 'dp', 'tensor')
- up_weight_grad: float32 [2, 1024, 3072], P(None, 'dp', 'tensor')
- down_weight_grad: float32 [2, 3072, 1024], P(None, 'tensor', 'dp')
The draws below stay inside these ranges and needn't reach their ends.
Inputs may be any that keep to these rules, and one draw needn't show every extreme that they name: `segment_ids`: in each group of 512 consecutive slots the ids never fall: documents 0, 1 and 2 (0 and 2 may be absent), then empty slots with id 3 up to the group's end; document 1 starts among the group's first 128 slots and ends among its last 128; in some group it fills all 512 slots.
All inputs are finite; a program needn't handle non-finite values.
Results may differ from the reference program's by a relative error of at most 0.04.
Values may be sent and summed in bfloat16 or wider, within the bound.
No kernel may reach another device: no remote copies, remote signals or barrier semaphores. Data moves between devices by JAX's collectives and lax.ppermute only.
A program may use at most 128 MiB of HBM per device.

```python
import math
import jax
import jax.numpy as jnp
from jax import lax

MODEL_WIDTH = 1024
QUERY_HEADS = 16
KEY_VALUE_HEADS = 8
HEAD_SIZE = 128
FF = 3072
DECODER_LAYERS = 2
SLOTS = 512
GROUPS = 32
TOKENS = 16384


def draw_segment_ids(key, part):
    key = jax.random.fold_in(key, 11)
    subkeys = jax.random.split(key, 4)
    quarter = SLOTS // 4
    doc_start = jax.random.randint(subkeys[0], (GROUPS,), 0, quarter)
    doc_finish = jax.random.randint(subkeys[1], (GROUPS,), 3 * quarter + 1, SLOTS + 1)
    filled_group = jax.random.randint(subkeys[2], (), 0, GROUPS)
    chosen = jnp.arange(GROUPS) == filled_group
    doc_start = jnp.where(chosen, 0, doc_start)
    doc_finish = jnp.where(chosen, SLOTS, doc_finish)
    leftover = jax.random.randint(subkeys[3], (GROUPS,), 0, SLOTS + 1 - doc_finish)
    cutoff = doc_finish + leftover
    column = jnp.arange(SLOTS)[None, :]
    labels = jnp.where(column < doc_start[:, None], 0, jnp.where(column < doc_finish[:, None], 1, jnp.where(column < cutoff[:, None], 2, 3)))
    return labels.reshape(GROUPS * SLOTS).astype(jnp.int32)


def block_scale(stream_key, dims, cuts, least, top_value):
    def one(dim, shards_of):
        steps = jax.random.uniform(jax.random.fold_in(jax.random.fold_in(stream_key, 6), dim), (shards_of,), jnp.float32, least / len(cuts), top_value / len(cuts))
        return jnp.repeat(jnp.exp(steps), dims[dim] // shards_of).reshape((-1,) + (1,) * (len(dims) - dim - 1))

    gain = one(*cuts[0])
    for cut in cuts[1:]:
        gain = gain * one(*cut)
    return gain


def normal_values(stream_key, dims, deviation, bound, cuts=(), kind=jnp.bfloat16):
    array = deviation * jax.random.normal(stream_key, dims, jnp.float32)
    if cuts:
        array = array * block_scale(stream_key, dims, cuts, -0.22, 0.18)
    return jnp.clip(array, -bound, bound).astype(kind)


def setup_inputs(seed: int = 0) -> dict:
    keys = jax.random.split(jax.random.key(seed), 15)
    return {
        "tokens": normal_values(keys[0], (TOKENS, MODEL_WIDTH), 1.0, 6.0, ((0, 128),)),
        "segment_ids": draw_segment_ids(jax.random.fold_in(keys[14], 71), 0),
        "cotangent": normal_values(keys[2], (TOKENS, MODEL_WIDTH), 1.0, 6.0, ((0, 128),)),
        "attn_norm": jnp.clip(1.0 + 0.18 * jax.random.normal(keys[3], (DECODER_LAYERS, MODEL_WIDTH), jnp.float32), 0.1, 1.9),
        "q_weight": normal_values(keys[4], (DECODER_LAYERS, MODEL_WIDTH, QUERY_HEADS * HEAD_SIZE), MODEL_WIDTH ** -0.5, 0.1875, ((1, 32), (2, 4))),
        "key_projection": normal_values(keys[5], (DECODER_LAYERS, MODEL_WIDTH, KEY_VALUE_HEADS * HEAD_SIZE), MODEL_WIDTH ** -0.5, 0.1875, ((1, 32), (2, 4))),
        "value_projection": normal_values(keys[6], (DECODER_LAYERS, MODEL_WIDTH, KEY_VALUE_HEADS * HEAD_SIZE), MODEL_WIDTH ** -0.5, 0.1875, ((1, 32), (2, 4))),
        "o_weight": normal_values(keys[7], (DECODER_LAYERS, QUERY_HEADS * HEAD_SIZE, MODEL_WIDTH), (QUERY_HEADS * HEAD_SIZE * 4 // SLOTS) ** -0.5, 1.5, ((1, 4), (2, 32))),
        "q_gain": jnp.clip(1.0 + 0.18 * jax.random.normal(keys[8], (DECODER_LAYERS, HEAD_SIZE), jnp.float32), 0.1, 1.9),
        "k_gain": jnp.clip(1.0 + 0.18 * jax.random.normal(keys[9], (DECODER_LAYERS, HEAD_SIZE), jnp.float32), 0.1, 1.9),
        "mlp_norm": jnp.clip(1.0 + 0.18 * jax.random.normal(keys[10], (DECODER_LAYERS, MODEL_WIDTH), jnp.float32), 0.1, 1.9),
        "gate_weight": normal_values(keys[11], (DECODER_LAYERS, MODEL_WIDTH, FF), MODEL_WIDTH ** -0.5, 0.1875, ((1, 32), (2, 4))),
        "up_weight": normal_values(keys[12], (DECODER_LAYERS, MODEL_WIDTH, FF), MODEL_WIDTH ** -0.5, 0.1875, ((1, 32), (2, 4))),
        "down_weight": normal_values(keys[13], (DECODER_LAYERS, FF, MODEL_WIDTH), FF ** -0.5, 0.109375, ((1, 4), (2, 32))),
    }


@jax.custom_vjp
def reduced_precision(v):
    return lax.optimization_barrier(v.astype(jnp.bfloat16)).astype(jnp.float32)

@jax.custom_vjp
def reduced_backward(v):
    return v

def low_keep(v):
    return (reduced_precision(v), None)

def low_pass(kept, grad):
    return (grad,)

def back_keep(v):
    return (v, None)

def back_low(kept, grad):
    return (reduced_precision(grad),)
reduced_precision.defvjp(low_keep, low_pass)
reduced_backward.defvjp(back_keep, back_low)
NORM_EPS = 1e-06
ROPE_BASE = 1000000.0
MASK_FILL = -1000000000.0

def matrix_multiply(left_side, right_side):
    return jnp.dot(left_side, right_side, precision=lax.Precision.HIGHEST, preferred_element_type=jnp.float32)

def rms_scale(values, gain_vector):
    return values * lax.rsqrt(lax.optimization_barrier(jnp.mean(values * values, axis=-1, keepdims=True)) + NORM_EPS) * gain_vector

def rotary_tables(segment_ids):
    width = segment_ids.shape[0]
    column = jnp.arange(width, dtype=jnp.int32)
    doc_starts = jnp.zeros((width,), jnp.int32)
    for doc_number in range(4):
        before = jnp.sum((segment_ids < doc_number).astype(jnp.int32)).astype(jnp.int32)
        doc_starts = doc_starts + jnp.where(segment_ids == doc_number, before, 0).astype(jnp.int32)
    position = (column - doc_starts).astype(jnp.float32)
    half_width = HEAD_SIZE // 2
    frequency = jnp.exp(jnp.arange(half_width, dtype=jnp.float32) * (-2.0 * math.log(ROPE_BASE) / HEAD_SIZE))
    angles = position[:, None] * frequency[None, :]
    angles = jnp.concatenate([angles, angles], axis=-1)
    return (jnp.cos(angles)[:, None, :], jnp.sin(angles)[:, None, :])

def rotate(values, cosine_table, sine_table):
    half_width = values.shape[-1] // 2
    turned = jnp.concatenate([-values[..., half_width:], values[..., :half_width]], axis=-1)
    return values * cosine_table + turned * sine_table

def attention_mask(segment_ids):
    column = jnp.arange(segment_ids.shape[0], dtype=jnp.int32)
    same_doc = segment_ids[:, None] == segment_ids[None, :]
    causal = column[None, :] <= column[:, None]
    live_row = segment_ids[:, None] < 3
    return same_doc & causal & live_row | (column[:, None] == column[None, :])

def layer_forward(params, decoder_layer_index, hidden_in, cosine_table, sine_table, allowed):
    attn_norm, q_weight, key_projection, value_projection, o_weight, q_gain, k_gain, mlp_norm, gate_weight, up_weight, down_weight = params
    token_row_count = hidden_in.shape[0]
    heads_per_group = QUERY_HEADS // KEY_VALUE_HEADS
    normalized_input = reduced_precision(rms_scale(hidden_in, attn_norm[decoder_layer_index]))
    query_pre = reduced_backward(matrix_multiply(normalized_input, q_weight[decoder_layer_index])).reshape(token_row_count, QUERY_HEADS, HEAD_SIZE)
    key_before_rotary = reduced_backward(matrix_multiply(normalized_input, key_projection[decoder_layer_index])).reshape(token_row_count, KEY_VALUE_HEADS, HEAD_SIZE)
    value_reduced = reduced_precision(reduced_backward(matrix_multiply(normalized_input, value_projection[decoder_layer_index]))).reshape(token_row_count, KEY_VALUE_HEADS, HEAD_SIZE)
    query_rotated = reduced_precision(rotate(rms_scale(query_pre, q_gain[decoder_layer_index]), cosine_table, sine_table))
    query_rotated = query_rotated.reshape(token_row_count, KEY_VALUE_HEADS, heads_per_group, HEAD_SIZE)
    key_rot = reduced_precision(rotate(rms_scale(key_before_rotary, k_gain[decoder_layer_index]), cosine_table, sine_table))
    raw_scores = jnp.einsum('qhgd,khd->hgqk', query_rotated, key_rot, precision=lax.Precision.HIGHEST)
    scaled = jnp.where(allowed, reduced_backward(raw_scores) * HEAD_SIZE ** (-0.5), MASK_FILL)
    exponent = jnp.exp(scaled - lax.optimization_barrier(jnp.max(scaled, axis=-1, keepdims=True)))
    probability = reduced_precision(exponent / lax.optimization_barrier(jnp.sum(exponent, axis=-1, keepdims=True)))
    mixed_heads = jnp.einsum('hgqk,khd->qhgd', probability, value_reduced, precision=lax.Precision.HIGHEST)
    mixed_low = reduced_precision(reduced_backward(mixed_heads.reshape(token_row_count, QUERY_HEADS * HEAD_SIZE)))
    middle = hidden_in + reduced_backward(matrix_multiply(mixed_low, o_weight[decoder_layer_index]))
    normed_two = reduced_precision(rms_scale(middle, mlp_norm[decoder_layer_index]))
    gate_pre = reduced_backward(matrix_multiply(normed_two, gate_weight[decoder_layer_index]))
    up_pre = reduced_backward(matrix_multiply(normed_two, up_weight[decoder_layer_index]))
    product_low = reduced_precision(jax.nn.silu(gate_pre) * up_pre)
    return middle + reduced_backward(matrix_multiply(product_low, down_weight[decoder_layer_index]))

def group_forward(params, hidden_in, segment_ids):
    cosine_table, sine_table = rotary_tables(segment_ids)
    allowed = attention_mask(segment_ids)
    hidden = hidden_in
    for decoder_layer_index in range(DECODER_LAYERS):
        hidden = layer_forward(params, decoder_layer_index, hidden, cosine_table, sine_table, allowed)
    return hidden

def forward(hidden_all, params, segment_ids):
    grouped = hidden_all.reshape(GROUPS, SLOTS, MODEL_WIDTH)
    segment_groups = segment_ids.reshape(GROUPS, SLOTS)
    checked = jax.checkpoint(group_forward)

    def per_group(group_items):
        return checked(params, group_items[0], group_items[1])
    result_groups = lax.map(per_group, (grouped, segment_groups))
    return result_groups.reshape(GROUPS * SLOTS, MODEL_WIDTH)

def reference(tokens, segment_ids, cotangent, attn_norm, q_weight, key_projection, value_projection, o_weight, q_gain, k_gain, mlp_norm, gate_weight, up_weight, down_weight):
    params = tuple((weight_item.astype(jnp.float32) for weight_item in (attn_norm, q_weight, key_projection, value_projection, o_weight, q_gain, k_gain, mlp_norm, gate_weight, up_weight, down_weight)))

    def wrapped(hidden_all, weight_set):
        return forward(hidden_all, weight_set, segment_ids)
    output_value, pullback = jax.vjp(wrapped, tokens.astype(jnp.float32), params)
    input_grad, weight_grads = pullback(cotangent.astype(jnp.float32))
    return (output_value.astype(jnp.bfloat16), input_grad, weight_grads[0], weight_grads[1], weight_grads[2], weight_grads[3], weight_grads[4], weight_grads[5], weight_grads[6], weight_grads[7], weight_grads[8], weight_grads[9], weight_grads[10])
```

```python
import math

import jax
import jax.numpy as jnp
from jax import lax
from jax.sharding import PartitionSpec as P

QUERY_HEADS = 16
KEY_VALUE_HEADS = 8
HEAD_SIZE = 128
DECODER_LAYERS = 2


NORM_EPS = 1e-06
ROPE_BASE = 1000000.0
MASK_FILL = -1000000000.0
QUERY_BLOCK = 512


def rms_scale(values, gain_vector):
    return (
        values
        * lax.rsqrt(jnp.mean(values * values, axis=-1, keepdims=True) + NORM_EPS)
        * gain_vector
    )


def rotary_tables(segment_ids):
    width = segment_ids.shape[0]
    column = jnp.arange(width, dtype=jnp.int32)
    doc_starts = jnp.zeros((width,), jnp.int32)
    for doc_number in range(4):
        before = jnp.sum((segment_ids < doc_number).astype(jnp.int32))
        doc_starts = doc_starts + jnp.where(segment_ids == doc_number, before, 0)
    position = (column - doc_starts).astype(jnp.float32)
    half_width = HEAD_SIZE // 2
    frequency = jnp.exp(
        jnp.arange(half_width, dtype=jnp.float32) * (-2.0 * math.log(ROPE_BASE) / HEAD_SIZE)
    )
    angles = position[:, None] * frequency[None, :]
    angles = jnp.concatenate([angles, angles], axis=-1)
    return (jnp.cos(angles)[:, None, :], jnp.sin(angles)[:, None, :])


def rotate(values, cosine_table, sine_table):
    half_width = values.shape[-1] // 2
    turned = jnp.concatenate([-values[..., half_width:], values[..., :half_width]], axis=-1)
    return values * cosine_table + turned * sine_table


def attention_mask(segment_ids):
    column = jnp.arange(segment_ids.shape[0], dtype=jnp.int32)
    same_doc = segment_ids[:, None] == segment_ids[None, :]
    causal = column[None, :] <= column[:, None]
    live_row = segment_ids[:, None] < 3
    return same_doc & causal & live_row | (column[:, None] == column[None, :])


def swiglu(gate_pre, up_pre):
    return jax.nn.silu(gate_pre) * up_pre


def block_scores(query_block, key_rot, mask_block):
    raw_scores = jnp.einsum(
        "qhgd,khd->hgqk", query_block, key_rot, preferred_element_type=jnp.float32
    )
    return jnp.where(mask_block[None, None], raw_scores * HEAD_SIZE ** (-0.5), MASK_FILL)


def split_blocks(values, block_count, block_rows):
    return values.reshape((block_count, block_rows) + values.shape[1:])


def attend_forward(query_rotated, key_rot, value_reduced, allowed):
    slot_count = query_rotated.shape[0]
    block_rows = min(QUERY_BLOCK, slot_count)
    block_count = slot_count // block_rows

    def one_block(block_pair):
        scaled = block_scores(block_pair[0], key_rot, block_pair[1])
        row_peak = jnp.max(scaled, axis=-1, keepdims=True)
        exponent = jnp.exp(scaled - row_peak)
        row_total = jnp.sum(exponent, axis=-1, keepdims=True)
        probability = (exponent / row_total).astype(jnp.bfloat16)
        mixed_heads = jnp.einsum(
            "hgqk,khd->qhgd", probability, value_reduced, preferred_element_type=jnp.float32
        )
        return (mixed_heads, row_peak + jnp.log(row_total))

    mixed_heads, log_total = lax.map(
        one_block,
        (
            split_blocks(query_rotated, block_count, block_rows),
            split_blocks(allowed, block_count, block_rows),
        ),
    )
    return (mixed_heads.reshape(query_rotated.shape), log_total)


def attend_backward(query_rotated, key_rot, value_reduced, log_total, grad_mixed, allowed):
    slot_count = query_rotated.shape[0]
    block_rows = min(QUERY_BLOCK, slot_count)
    block_count = slot_count // block_rows

    def one_step(carried, block_items):
        query_block, grad_block, mask_block, total_block = block_items
        probability = jnp.exp(block_scores(query_block, key_rot, mask_block) - total_block)
        grad_prob = jnp.einsum(
            "qhgd,khd->hgqk", grad_block, value_reduced, preferred_element_type=jnp.float32
        )
        grad_value = jnp.einsum(
            "hgqk,qhgd->khd",
            probability.astype(jnp.bfloat16),
            grad_block,
            preferred_element_type=jnp.float32,
        )
        inner_sum = jnp.sum(probability * grad_prob, axis=-1, keepdims=True)
        grad_score = (probability * (grad_prob - inner_sum) * HEAD_SIZE ** (-0.5)).astype(
            jnp.bfloat16
        )
        grad_query = jnp.einsum(
            "hgqk,khd->qhgd", grad_score, key_rot, preferred_element_type=jnp.float32
        )
        grad_key = jnp.einsum(
            "hgqk,qhgd->khd", grad_score, query_block, preferred_element_type=jnp.float32
        )
        return ((carried[0] + grad_key, carried[1] + grad_value), grad_query)

    zero_keys = jnp.zeros(key_rot.shape, jnp.float32)
    sums, grad_query = lax.scan(
        one_step,
        (zero_keys, zero_keys),
        (
            split_blocks(query_rotated, block_count, block_rows),
            split_blocks(grad_mixed, block_count, block_rows),
            split_blocks(allowed, block_count, block_rows),
            log_total,
        ),
    )
    return (grad_query.reshape(query_rotated.shape), sums[0], sums[1])


def core_pairs():
    return [(index, index ^ 1) for index in range(4)]


def chip_pairs():
    return [(index, index ^ 2) for index in range(4)]


def dp_shift(stage, step):
    pairs = []
    for z in range(4):
        for x in range(2):
            for y in range(4):
                target = {
                    "y": (z, x, (y + step) % 4),
                    "x": (z, (x + step) % 2, y),
                    "z": ((z + step) % 4, x, y),
                }[stage]
                pairs.append((z * 8 + x * 4 + y, target[0] * 8 + target[1] * 4 + target[2]))
    return pairs


def gather_rows(row_block):
    index = lax.axis_index("tensor")
    chip, core = index // 2, index % 2
    other = lax.ppermute(row_block, "tensor", chip_pairs())
    pair = jnp.where(chip == 0, jnp.stack([row_block, other]), jnp.stack([other, row_block]))
    sibling = lax.ppermute(pair, "tensor", core_pairs())
    both = jnp.where(
        core == 0, jnp.stack([pair, sibling], axis=1), jnp.stack([sibling, pair], axis=1)
    )
    return both.reshape(4 * row_block.shape[0], row_block.shape[1])


def scatter_rows(term):
    index = lax.axis_index("tensor")
    chip, core = index // 2, index % 2
    rows, width = term.shape[0] // 4, term.shape[1]
    blocks = term.reshape(2, 2, rows, width)
    own = jnp.where(core == 0, blocks[:, 0], blocks[:, 1])
    away = jnp.where(core == 0, blocks[:, 1], blocks[:, 0]).astype(jnp.bfloat16)
    summed = own + lax.ppermute(away, "tensor", core_pairs()).astype(jnp.float32)
    keep = jnp.where(chip == 0, summed[0], summed[1])
    send = jnp.where(chip == 0, summed[1], summed[0]).astype(jnp.bfloat16)
    return keep + lax.ppermute(send, "tensor", chip_pairs()).astype(jnp.float32)


def sum_everywhere(values):
    values = values + lax.ppermute(values, "tensor", core_pairs())
    values = values + lax.ppermute(values, "tensor", chip_pairs())
    for stage in ("y", "z"):
        pair = values + lax.ppermute(values, "dp", dp_shift(stage, 1))
        values = pair + lax.ppermute(pair, "dp", dp_shift(stage, 2))
    return values + lax.ppermute(values, "dp", dp_shift("x", 1))


def pack_weights(layer, q, k, v, o, gate, up, down):
    return jnp.concatenate(
        [q[layer], k[layer], v[layer], o[layer].T, gate[layer], up[layer], down[layer].T], axis=1
    )


def body(
    tokens,
    segment_ids,
    cotangent,
    attn_norm,
    q_weight,
    key_projection,
    value_projection,
    o_weight,
    q_gain,
    k_gain,
    mlp_norm,
    gate_weight,
    up_weight,
    down_weight,
):
    cosine_table, sine_table = rotary_tables(segment_ids)
    allowed = attention_mask(segment_ids)
    slot_count = segment_ids.shape[0]
    heads_per_group = QUERY_HEADS // KEY_VALUE_HEADS
    residual = tokens.astype(jnp.float32)
    saved_layers = []
    packed = jnp.concatenate(
        [
            pack_weights(
                layer,
                q_weight,
                key_projection,
                value_projection,
                o_weight,
                gate_weight,
                up_weight,
                down_weight,
            )
            for layer in range(DECODER_LAYERS)
        ],
        axis=1,
    )
    packed_full = lax.all_gather(packed, "dp", axis=0, tiled=True)
    layer_width = packed.shape[1] // DECODER_LAYERS
    weights_by_layer = [
        jnp.split(
            packed_full[:, layer * layer_width : (layer + 1) * layer_width],
            [512, 768, 1024, 1536, 2304, 3072],
            axis=1,
        )
        for layer in range(DECODER_LAYERS)
    ]
    for decoder_layer_index in range(DECODER_LAYERS):
        wq_full, wk_full, wv_full, wo_full, wg_full, wu_full, wd_full = weights_by_layer[
            decoder_layer_index
        ]
        normed_all = gather_rows(
            rms_scale(residual, attn_norm[decoder_layer_index]).astype(jnp.bfloat16)
        )
        query_pre = jnp.dot(normed_all, wq_full, preferred_element_type=jnp.float32).reshape(
            slot_count, -1, HEAD_SIZE
        )
        key_before_rotary = jnp.dot(
            normed_all, wk_full, preferred_element_type=jnp.float32
        ).reshape(slot_count, -1, HEAD_SIZE)
        value_reduced = jnp.dot(normed_all, wv_full, preferred_element_type=jnp.float32).astype(
            jnp.bfloat16
        )
        value_reduced = value_reduced.reshape(slot_count, -1, HEAD_SIZE)
        local_kv = key_before_rotary.shape[1]
        query_rotated = rotate(
            rms_scale(query_pre, q_gain[decoder_layer_index]), cosine_table, sine_table
        )
        query_rotated = query_rotated.astype(jnp.bfloat16).reshape(
            slot_count, local_kv, heads_per_group, HEAD_SIZE
        )
        key_rot = rotate(
            rms_scale(key_before_rotary, k_gain[decoder_layer_index]), cosine_table, sine_table
        ).astype(jnp.bfloat16)
        mixed_heads, log_total = attend_forward(query_rotated, key_rot, value_reduced, allowed)
        mixed_low = mixed_heads.reshape(slot_count, -1).astype(jnp.bfloat16)

        branch = jnp.einsum("sf,df->sd", mixed_low, wo_full, preferred_element_type=jnp.float32)
        middle = residual + scatter_rows(branch)
        normed_two_all = gather_rows(
            rms_scale(middle, mlp_norm[decoder_layer_index]).astype(jnp.bfloat16)
        )
        gate_pre = jnp.dot(normed_two_all, wg_full, preferred_element_type=jnp.float32)
        up_pre = jnp.dot(normed_two_all, wu_full, preferred_element_type=jnp.float32)
        product_low = swiglu(gate_pre, up_pre).astype(jnp.bfloat16)

        feed = jnp.einsum("sf,df->sd", product_low, wd_full, preferred_element_type=jnp.float32)
        saved_layers.append(
            (
                residual,
                middle,
                normed_all,
                normed_two_all,
                query_pre,
                key_before_rotary,
                query_rotated,
                key_rot,
                value_reduced,
                log_total,
                mixed_low,
                gate_pre,
                up_pre,
                product_low,
            )
        )
        residual = middle + scatter_rows(feed)
    output = residual.astype(jnp.bfloat16)
    grad_rows = cotangent.astype(jnp.float32)
    grads_by_layer = [None] * DECODER_LAYERS
    gains_by_layer = [None] * DECODER_LAYERS
    for decoder_layer_index in range(DECODER_LAYERS - 1, -1, -1):
        (
            residual_in,
            middle,
            normed_all,
            normed_two_all,
            query_pre,
            key_before_rotary,
            query_rotated,
            key_rot,
            value_reduced,
            log_total,
            mixed_low,
            gate_pre,
            up_pre,
            product_low,
        ) = saved_layers[decoder_layer_index]
        wq_full, wk_full, wv_full, wo_full, wg_full, wu_full, wd_full = weights_by_layer[
            decoder_layer_index
        ]
        local_kv = key_before_rotary.shape[1]
        grad_out_all = gather_rows(grad_rows.astype(jnp.bfloat16))
        down_part = jnp.einsum(
            "sf,sd->df", product_low, grad_out_all, preferred_element_type=jnp.float32
        )
        grad_product = jnp.einsum(
            "sd,df->sf", grad_out_all, wd_full, preferred_element_type=jnp.float32
        )
        swiglu_back = jax.vjp(swiglu, gate_pre, up_pre)[1]
        grad_gate, grad_up = swiglu_back(grad_product)
        grad_gate_low = grad_gate.astype(jnp.bfloat16)
        grad_up_low = grad_up.astype(jnp.bfloat16)
        gate_part = jnp.einsum(
            "sd,sf->df", normed_two_all, grad_gate_low, preferred_element_type=jnp.float32
        )
        up_part = jnp.einsum(
            "sd,sf->df", normed_two_all, grad_up_low, preferred_element_type=jnp.float32
        )

        first_term = jnp.einsum(
                "sf,df->sd", grad_gate_low, wg_full, preferred_element_type=jnp.float32
        )
        second_term = jnp.einsum(
                "sf,df->sd", grad_up_low, wu_full, preferred_element_type=jnp.float32
        )
        grad_normed_two = scatter_rows(first_term + second_term)
        norm_back_two = jax.vjp(rms_scale, middle, mlp_norm[decoder_layer_index])[1]
        grad_middle_part, mlp_gain_part = norm_back_two(grad_normed_two)
        grad_middle = grad_rows + grad_middle_part
        grad_branch_all = gather_rows(grad_middle.astype(jnp.bfloat16))
        o_part = jnp.einsum(
            "sf,sd->df", mixed_low, grad_branch_all, preferred_element_type=jnp.float32
        )
        grad_mixed = jnp.einsum(
            "sd,df->sf", grad_branch_all, wo_full, preferred_element_type=jnp.float32
        )
        grad_mixed = grad_mixed.astype(jnp.bfloat16).reshape(
            slot_count, local_kv, heads_per_group, HEAD_SIZE
        )
        grad_query_rot, grad_key_rot, grad_value = attend_backward(
            query_rotated, key_rot, value_reduced, log_total, grad_mixed, allowed
        )

        def head_norm(pre_heads, gain_vector):
            return rotate(rms_scale(pre_heads, gain_vector), cosine_table, sine_table)

        query_back = jax.vjp(head_norm, query_pre, q_gain[decoder_layer_index])[1]
        grad_query_pre, q_gain_part = query_back(grad_query_rot.reshape(slot_count, -1, HEAD_SIZE))
        key_back = jax.vjp(head_norm, key_before_rotary, k_gain[decoder_layer_index])[1]
        grad_key_pre, k_gain_part = key_back(grad_key_rot)
        grad_query_low = grad_query_pre.reshape(slot_count, -1).astype(jnp.bfloat16)
        grad_key_low = grad_key_pre.reshape(slot_count, -1).astype(jnp.bfloat16)
        grad_value_low = grad_value.reshape(slot_count, -1).astype(jnp.bfloat16)
        q_part = jnp.einsum(
            "sd,sf->df", normed_all, grad_query_low, preferred_element_type=jnp.float32
        )
        k_part = jnp.einsum(
            "sd,sf->df", normed_all, grad_key_low, preferred_element_type=jnp.float32
        )
        v_part = jnp.einsum(
            "sd,sf->df", normed_all, grad_value_low, preferred_element_type=jnp.float32
        )

        query_term = jnp.einsum(
            "sf,df->sd", grad_query_low, wq_full, preferred_element_type=jnp.float32
        )
        key_term = jnp.einsum(
            "sf,df->sd", grad_key_low, wk_full, preferred_element_type=jnp.float32
        )
        value_term = jnp.einsum(
            "sf,df->sd", grad_value_low, wv_full, preferred_element_type=jnp.float32
        )

        grad_normed = scatter_rows(query_term + key_term + value_term)
        norm_back_one = jax.vjp(rms_scale, residual_in, attn_norm[decoder_layer_index])[1]
        grad_in_part, attn_gain_part = norm_back_one(grad_normed)
        grad_rows = grad_middle + grad_in_part
        grad_packed = jnp.concatenate(
            [
                part.astype(jnp.bfloat16)
                for part in (q_part, k_part, v_part, o_part, gate_part, up_part, down_part)
            ],
            axis=1,
        )
        grad_rows_own = lax.psum_scatter(
            grad_packed, "dp", scatter_dimension=0, tiled=True
        ).astype(jnp.float32)
        q_own, k_own, v_own, o_own, gate_own, up_own, down_own = jnp.split(
            grad_rows_own, [512, 768, 1024, 1536, 2304, 3072], axis=1
        )
        grads_by_layer[decoder_layer_index] = (
            q_own,
            k_own,
            v_own,
            o_own.T,
            gate_own,
            up_own,
            down_own.T,
        )
        gains_by_layer[decoder_layer_index] = (
            attn_gain_part,
            q_gain_part,
            k_gain_part,
            mlp_gain_part,
        )
    stacked = [
        jnp.stack(
            [
                grads_by_layer[decoder_layer_index][member]
                for decoder_layer_index in range(DECODER_LAYERS)
            ]
        )
        for member in range(7)
    ]
    q_stack, k_stack, v_stack, o_stack, gate_stack, up_stack, down_stack = stacked
    gain_stack = [
        jnp.stack(
            [
                gains_by_layer[decoder_layer_index][member]
                for decoder_layer_index in range(DECODER_LAYERS)
            ]
        )
        for member in range(4)
    ]
    attn_gain_stack, q_gain_stack, k_gain_stack, mlp_gain_stack = gain_stack
    gain_sums = sum_everywhere(jnp.concatenate(gain_stack, axis=1))
    attn_gain_sum, q_gain_sum, k_gain_sum, mlp_gain_sum = jnp.split(
        gain_sums, [1024, 1152, 1280], axis=1
    )
    return (
        output,
        grad_rows,
        attn_gain_sum,
        q_stack,
        k_stack,
        v_stack,
        o_stack,
        q_gain_sum,
        k_gain_sum,
        mlp_gain_sum,
        gate_stack,
        up_stack,
        down_stack,
    )


def solution(mesh):
    return jax.shard_map(
        body,
        mesh=mesh,
        in_specs=(
            P(("dp", "tensor"), None),
            P("dp"),
            P(("dp", "tensor"), None),
            P(),
            P(None, "dp", "tensor"),
            P(None, "dp", "tensor"),
            P(None, "dp", "tensor"),
            P(None, "tensor", "dp"),
            P(),
            P(),
            P(),
            P(None, "dp", "tensor"),
            P(None, "dp", "tensor"),
            P(None, "tensor", "dp"),
        ),
        out_specs=(
            P(("dp", "tensor"), None),
            P(("dp", "tensor"), None),
            P(),
            P(None, "dp", "tensor"),
            P(None, "dp", "tensor"),
            P(None, "dp", "tensor"),
            P(None, "tensor", "dp"),
            P(),
            P(),
            P(),
            P(None, "dp", "tensor"),
            P(None, "dp", "tensor"),
            P(None, "tensor", "dp"),
        ),
        check_vma=False,
    )
```

```python
import math

import jax
import jax.numpy as jnp
from jax import lax
from jax.experimental import pallas as pl
from jax.experimental.pallas import tpu as pltpu
from jax.sharding import PartitionSpec as P

ROPE_BASE = 1000000.0
HEAD = 128
SCALE = 128 ** -0.5
LOG2E = 1.0 / math.log(2.0)
NORM_EPS = 1e-6
NT = (((1,), (1,)), ((), ()))
TN = (((0,), (0,)), ((), ()))
NN = (((1,), (0,)), ((), ()))


def block_offsets():
    core = lax.axis_index("tensor") % 2
    return [
        pl.multiple_of(128 * (block // 2 + 2 * ((block + core) % 2)), 128) for block in range(4)
    ]


def block_mask(block, segment_rows, segment_columns):
    keys = 128 * (block + 1)
    row = lax.broadcasted_iota(jnp.int32, (128, keys), 0) + 128 * block
    column = lax.broadcasted_iota(jnp.int32, (128, keys), 1)
    query_segment = segment_rows[128 * block : 128 * (block + 1), :]
    same = query_segment == segment_columns[:, :keys]
    allowed = same & (column <= row) & (query_segment < 3) | (column == row)
    return allowed.astype(jnp.float32)


def head_norm(pre):
    return lax.rsqrt(jnp.mean(pre * pre, axis=-1, keepdims=True) + NORM_EPS)


def attend_forward_kernel(
    pre_qk, pre_v, q_gain, k_gain, cosine, sine, segment_rows, segment_columns, rotated, mixed, inverse, keys
):
    offsets = block_offsets()
    cos, sin = cosine[...], sine[...]
    for head in range(6):
        lanes = slice(128 * head, 128 * (head + 1))
        value = pre_qk[:, lanes]
        gain = q_gain[...] if head < 4 else k_gain[...]
        normed = value * head_norm(value) * gain
        turned = normed * cos + pltpu.roll(normed, 64, 1) * sin
        rotated[:, lanes] = turned.astype(jnp.bfloat16)
    rotated[:, 768:] = pre_v[...].astype(jnp.bfloat16)
    for block in range(4):
        keys[128 * block : 128 * (block + 1), :] = rotated[pl.ds(offsets[block], 128), 512:]
    lane = lax.broadcasted_iota(jnp.int32, (128, 128), 1)
    for block in range(4):
        count = 128 * (block + 1)
        allowed = block_mask(block, segment_rows, segment_columns)
        allowed = jnp.concatenate([allowed, allowed], axis=0)
        rows = pl.ds(offsets[block], 128)
        totals = jnp.zeros((128, 128), jnp.float32)
        for group in range(2):
            query = jnp.concatenate(
                [rotated[rows, 256 * group : 256 * group + 128], rotated[rows, 256 * group + 128 : 256 * group + 256]],
                axis=0,
            )
            key = keys[:count, 128 * group : 128 * (group + 1)]
            value = keys[:count, 256 + 128 * group : 256 + 128 * (group + 1)]
            score = lax.dot_general(query, key, NT, preferred_element_type=jnp.float32)
            weight = jnp.exp2(score * (SCALE * LOG2E)) * allowed
            inverse_total = 1.0 / jnp.sum(weight, axis=-1, keepdims=True)
            out = lax.dot_general((weight * inverse_total).astype(jnp.bfloat16), value, NN, preferred_element_type=jnp.float32)
            out = out.astype(jnp.bfloat16)
            mixed[rows, 256 * group : 256 * group + 128] = out[:128]
            mixed[rows, 256 * group + 128 : 256 * group + 256] = out[128:]
            totals = jnp.where(lane == 2 * group, inverse_total[:128], totals)
            totals = jnp.where(lane == 2 * group + 1, inverse_total[128:], totals)
        inverse[rows, :] = totals


def attend_forward(pre_qk, pre_v, q_gain, k_gain, cosine, sine, segment_rows, segment_columns):
    return pl.pallas_call(
        attend_forward_kernel,
        out_shape=(
            jax.ShapeDtypeStruct((512, 1024), jnp.bfloat16),
            jax.ShapeDtypeStruct((512, 512), jnp.bfloat16),
            jax.ShapeDtypeStruct((512, 128), jnp.float32),
        ),
        scratch_shapes=[pltpu.VMEM((512, 512), jnp.bfloat16)],
        compiler_params=pltpu.CompilerParams(vmem_limit_bytes=24 * 1024 * 1024),
        cost_estimate=pl.CostEstimate(flops=700_000_000, bytes_accessed=6_000_000, transcendentals=700_000),
        name="attend_forward",
    )(pre_qk, pre_v, q_gain, k_gain, cosine, sine, segment_rows, segment_columns)


def attend_backward_kernel(
    pre_qk, rotated, mixed, inverse, grad_mixed, q_gain, k_gain, cosine, sine, segment_rows, segment_columns,
    grad_qk, grad_v, gain_grads, keys, grad_rotated, grad_keys,
):
    offsets = block_offsets()
    for block in range(4):
        keys[128 * block : 128 * (block + 1), :] = rotated[pl.ds(offsets[block], 128), 512:]
    for block in range(3, -1, -1):
        count = 128 * (block + 1)
        allowed = block_mask(block, segment_rows, segment_columns)
        allowed = jnp.concatenate([allowed, allowed], axis=0)
        rows = pl.ds(offsets[block], 128)
        inverse_block = inverse[rows, :]
        for group in range(2):
            def pair(ref):
                return jnp.concatenate(
                    [ref[rows, 256 * group : 256 * group + 128], ref[rows, 256 * group + 128 : 256 * group + 256]],
                    axis=0,
                )
            query, grad_out = pair(rotated), pair(grad_mixed)
            inner = jnp.sum(grad_out.astype(jnp.float32) * pair(mixed).astype(jnp.float32), axis=-1, keepdims=True)
            key = keys[:count, 128 * group : 128 * (group + 1)]
            value = keys[:count, 256 + 128 * group : 256 + 128 * (group + 1)]
            inverse_total = jnp.concatenate(
                [inverse_block[:, 2 * group : 2 * group + 1], inverse_block[:, 2 * group + 1 : 2 * group + 2]], axis=0
            )
            score = lax.dot_general(query, key, NT, preferred_element_type=jnp.float32)
            weight = jnp.exp2(score * (SCALE * LOG2E)) * allowed * inverse_total
            grad_weight = lax.dot_general(grad_out, value, NT, preferred_element_type=jnp.float32)
            grad_score = (weight * (grad_weight - inner)).astype(jnp.bfloat16)
            low = weight.astype(jnp.bfloat16)
            grad_value = lax.dot_general(low, grad_out, TN, preferred_element_type=jnp.float32)
            grad_key = lax.dot_general(grad_score, query, TN, preferred_element_type=jnp.float32)
            grad_query = lax.dot_general(grad_score, key, NN, preferred_element_type=jnp.float32)
            grad_rotated[rows, 256 * group : 256 * group + 128] = grad_query[:128] * SCALE
            grad_rotated[rows, 256 * group + 128 : 256 * group + 256] = grad_query[128:] * SCALE
            spot, value_spot = slice(128 * group, 128 * (group + 1)), slice(256 + 128 * group, 256 + 128 * (group + 1))
            if block == 3:
                grad_keys[:, spot] = grad_key * SCALE
                grad_keys[:, value_spot] = grad_value
            else:
                grad_keys[:count, spot] += grad_key * SCALE
                grad_keys[:count, value_spot] += grad_value
    for block in range(4):
        grad_rotated[pl.ds(offsets[block], 128), 512:] = grad_keys[128 * block : 128 * (block + 1), :]
    cos, sin = cosine[...], sine[...]
    gain_sums = []
    for head in range(6):
        lanes = slice(128 * head, 128 * (head + 1))
        value = pre_qk[:, lanes]
        gain = q_gain[...] if head < 4 else k_gain[...]
        scale = head_norm(value)
        unit = value * scale
        turned = grad_rotated[:, lanes]
        grad = turned * cos + pltpu.roll(turned * sin, 64, 1)
        gain_sums.append(jnp.sum(grad * unit, axis=0, keepdims=True))
        grad = grad * gain
        grad = scale * (grad - unit * jnp.mean(grad * unit, axis=-1, keepdims=True))
        grad_qk[:, lanes] = grad.astype(jnp.bfloat16)
    grad_v[...] = grad_rotated[:, 768:].astype(jnp.bfloat16)
    gain_grads[0:1, :] = gain_sums[0] + gain_sums[1] + gain_sums[2] + gain_sums[3]
    gain_grads[1:2, :] = gain_sums[4] + gain_sums[5]
    gain_grads[2:8, :] = jnp.zeros((6, 128), jnp.float32)


def attend_backward(pre_qk, rotated, mixed, inverse, grad_mixed, q_gain, k_gain, cosine, sine, segment_rows, segment_columns):
    return pl.pallas_call(
        attend_backward_kernel,
        out_shape=(
            jax.ShapeDtypeStruct((512, 768), jnp.bfloat16),
            jax.ShapeDtypeStruct((512, 256), jnp.bfloat16),
            jax.ShapeDtypeStruct((8, 128), jnp.float32),
        ),
        scratch_shapes=[
            pltpu.VMEM((512, 512), jnp.bfloat16),
            pltpu.VMEM((512, 1024), jnp.float32),
            pltpu.VMEM((512, 512), jnp.float32),
        ],
        compiler_params=pltpu.CompilerParams(vmem_limit_bytes=28 * 1024 * 1024),
        cost_estimate=pl.CostEstimate(flops=1_700_000_000, bytes_accessed=8_000_000, transcendentals=700_000),
        name="attend_backward",
    )(pre_qk, rotated, mixed, inverse, grad_mixed, q_gain, k_gain, cosine, sine, segment_rows, segment_columns)


def core_pairs():
    return [(index, index ^ 1) for index in range(4)]


def chip_pairs():
    return [(index, index ^ 2) for index in range(4)]


def dp_shift(stage, step):
    pairs = []
    for z in range(4):
        for x in range(2):
            for y in range(4):
                target = {
                    "y": (z, x, (y + step) % 4),
                    "x": (z, (x + step) % 2, y),
                    "z": ((z + step) % 4, x, y),
                }[stage]
                pairs.append((z * 8 + x * 4 + y, target[0] * 8 + target[1] * 4 + target[2]))
    return pairs


def dp_place():
    index = lax.axis_index("dp")
    return {"z": index // 8, "x": index // 4 % 2, "y": index % 4}


def dp_groups(stage):
    groups = {}
    for z in range(4):
        for x in range(2):
            for y in range(4):
                key = {"z": (x, y), "y": (z, x)}[stage]
                groups.setdefault(key, []).append(z * 8 + x * 4 + y)
    return [groups[key] for key in sorted(groups)]


def column_ranges(widths):
    starts = [sum(widths[:index]) for index in range(len(widths))]
    return [pl.ds(start, width) for start, width in zip(starts, widths)]


def ring_gather(block, stage):
    return [(block, 0, None)] + [
        (lax.ppermute(block, "dp", dp_shift(stage, step)), step, None) for step in (1, 2, 3)
    ]


def two_step_gather(block, stage):
    half = block.shape[0] // 2
    below = lax.ppermute(block, "dp", dp_shift(stage, 1))
    above = lax.ppermute(block, "dp", dp_shift(stage, 3))
    far_low = lax.ppermute(below[:half], "dp", dp_shift(stage, 1))
    far_high = lax.ppermute(above[half:], "dp", dp_shift(stage, 3))
    return [(block, 0, None), (below, 1, None), (above, 3, None), (far_low, 2, 0), (far_high, 2, 1)]


def place_blocks(blocks, stage, shape, axis, widths):
    places = [(step, half) for _, step, half in blocks]

    def kernel(*refs):
        sources, targets, semaphores = refs[: len(places)], refs[len(places) : -1], refs[-1]
        index = lax.axis_index("dp")
        mine = index // 8 if stage == "z" else index % 4
        copies = []
        for order, (source, (step, half)) in enumerate(zip(sources, places)):
            spot = lax.rem(mine - step + 4, 4)
            rows = source.shape[0]
            rows = pl.ds(0 if half is None else half * rows, rows)
            for number, columns in enumerate(column_ranges(widths)):
                whole = targets[number]
                target = whole.at[spot, rows] if axis == 0 else whole.at[rows, spot]
                copies.append(
                    pltpu.make_async_copy(
                        source.at[..., columns], target, semaphores.at[order, number]
                    )
                )
        for copy in copies:
            copy.start()
        for copy in copies:
            copy.wait()

    arrays = [block for block, _, _ in blocks]
    return pl.pallas_call(
        kernel,
        out_shape=[jax.ShapeDtypeStruct((*shape, width), arrays[0].dtype) for width in widths],
        in_specs=[pl.BlockSpec(memory_space=pl.ANY)] * len(arrays),
        out_specs=[pl.BlockSpec(memory_space=pltpu.VMEM)] * len(widths),
        scratch_shapes=[pltpu.SemaphoreType.DMA((len(arrays), len(widths)))],
        compiler_params=pltpu.CompilerParams(vmem_limit_bytes=16 * 1024 * 1024),
        cost_estimate=pl.CostEstimate(
            flops=0, bytes_accessed=4 * math.prod(shape) * sum(widths), transcendentals=0
        ),
        name="place_blocks",
    )(*arrays)


def split_blocks(parts, stage, axis):
    widths = [part.shape[-1] for part in parts]
    lead = parts[0].shape[:-1]
    shape = (*lead[:axis], *lead[axis + 1 :], sum(widths))

    def kernel(*refs):
        sources, blocks, semaphores = refs[: len(parts)], refs[len(parts) : -1], refs[-1]
        index = lax.axis_index("dp")
        mine = index // 8 if stage == "z" else index % 4
        copies = []
        for step, block in enumerate(blocks):
            spot = lax.rem(mine + step, 4)
            for number, columns in enumerate(column_ranges(widths)):
                source = sources[number]
                piece = source.at[spot] if axis == 0 else source.at[:, spot]
                copies.append(
                    pltpu.make_async_copy(
                        piece, block.at[..., columns], semaphores.at[step, number]
                    )
                )
        for copy in copies:
            copy.start()
        for copy in copies:
            copy.wait()

    return pl.pallas_call(
        kernel,
        out_shape=[jax.ShapeDtypeStruct(shape, parts[0].dtype)] * 4,
        in_specs=[pl.BlockSpec(memory_space=pltpu.VMEM)] * len(parts),
        out_specs=[pl.BlockSpec(memory_space=pl.ANY)] * 4,
        scratch_shapes=[pltpu.SemaphoreType.DMA((4, len(parts)))],
        compiler_params=pltpu.CompilerParams(vmem_limit_bytes=16 * 1024 * 1024),
        cost_estimate=pl.CostEstimate(
            flops=0, bytes_accessed=16 * math.prod(shape), transcendentals=0
        ),
        name="split_blocks",
    )(*parts)


def join_x(block, other):
    return jnp.where(
        dp_place()["x"] == 0, jnp.stack([block, other]), jnp.stack([other, block])
    )


def gather_x(block, *side_work):
    return join_x(block, after(lax.ppermute(block, "dp", dp_shift("x", 1)), *side_work))


def place_first(blocks, stage, widths):
    if stage == "y":
        wholes = place_blocks(blocks, "y", (2, 4, 32), 1, widths)
    else:
        wholes = place_blocks(blocks, "z", (4, 2, 32), 0, widths)
    return [whole.reshape(256, width) for whole, width in zip(wholes, widths)]


def place_last(blocks, stage, widths):
    if stage == "z":
        wholes = place_blocks(blocks, "z", (4, 256), 0, widths)
    else:
        blocks = [
            (block.reshape(-1, 32, sum(widths)), step, half) for block, step, half in blocks
        ]
        wholes = place_blocks(blocks, "y", (8, 4, 32), 1, widths)
    return [whole.reshape(1024, width) for whole, width in zip(wholes, widths)]


def ring_send(blocks, stage):
    return [blocks[0]] + [
        lax.ppermute(blocks[step], "dp", dp_shift(stage, step)) for step in (1, 2, 3)
    ]


def ring_sum(sent):
    total = sum(block.astype(jnp.float32) for block in sent).astype(jnp.bfloat16)
    return total.reshape(256, total.shape[-1])


def split_first(parts, stage):
    if stage == "z":
        blocks = split_blocks([part.reshape(4, 256, -1) for part in parts], "z", 0)
    else:
        blocks = split_blocks([part.reshape(8, 4, 32, -1) for part in parts], "y", 1)
    return blocks


def x_parts(part, first_stage):
    width = part.shape[-1]
    if first_stage == "z":
        low, high = part[:128], part[128:]
    else:
        blocks = part.reshape(4, 2, 32, width)
        low, high = blocks[:, 0].reshape(128, width), blocks[:, 1].reshape(128, width)
    place = dp_place()["x"]
    return jnp.where(place == 0, low, high), jnp.where(place == 0, high, low)


def send_x(part, first_stage):
    return lax.ppermute(x_parts(part, first_stage)[1], "dp", dp_shift("x", 1))


def add_x(part, other, first_stage):
    kept = x_parts(part, first_stage)[0].astype(jnp.float32)
    return (kept + other.astype(jnp.float32)).astype(jnp.bfloat16)


def scatter_last(parts, stage):
    blocks = jnp.concatenate(parts, axis=1).reshape(4, 32, -1)
    mine = dp_place()[stage]
    total = lax.dynamic_index_in_dim(blocks, mine, 0, False).astype(jnp.float32)
    for step in (1, 2, 3):
        away = lax.dynamic_index_in_dim(blocks, (mine + step) % 4, 0, False)
        total = total + lax.ppermute(away, "dp", dp_shift(stage, step)).astype(jnp.float32)
    return total


def after(values, *others):
    return lax.optimization_barrier((values, others))[0]


def rms_scale(values, gain):
    return (
        values
        * lax.rsqrt(jnp.mean(values * values, axis=-1, keepdims=True) + NORM_EPS)
        * gain
    )


def rms_backward(values, gain, grad):
    scale = lax.rsqrt(jnp.mean(values * values, axis=-1, keepdims=True) + NORM_EPS)
    unit = values * scale
    scaled = grad * gain
    grad_values = scale * (scaled - unit * jnp.mean(scaled * unit, axis=-1, keepdims=True))
    return grad_values, jnp.sum(grad * unit, axis=0)


def dot(left, right):
    return jnp.dot(left, right, preferred_element_type=jnp.float32)


def dot_nt(left, right):
    return lax.dot_general(left, right, NT, preferred_element_type=jnp.float32)


def dot_tn(left, right):
    return lax.dot_general(left, right, TN, preferred_element_type=jnp.float32).astype(
        jnp.bfloat16
    )


def own_block(rows):
    chip = lax.axis_index("tensor") // 2
    blocks = rows.reshape(2, 128, rows.shape[-1])
    return jnp.where(chip == 0, blocks[0], blocks[1])


def both_blocks(block, *side_work):
    chip = lax.axis_index("tensor") // 2
    other = after(lax.ppermute(block, "tensor", chip_pairs()), *side_work)
    return jnp.where(
        chip == 0, jnp.concatenate([block, other]), jnp.concatenate([other, block])
    )


def with_sibling(rows):
    return jnp.concatenate([rows, lax.ppermute(rows, "tensor", core_pairs())])


def sum_cores(term):
    away = lax.ppermute(term(1).astype(jnp.bfloat16), "tensor", core_pairs())
    return (term(0) + away.astype(jnp.float32)).astype(jnp.bfloat16)


def sum_chips(part, *side_work):
    other = after(lax.ppermute(part, "tensor", chip_pairs()), *side_work)
    return part.astype(jnp.float32) + other.astype(jnp.float32)


def sum_own_block(part):
    chip = lax.axis_index("tensor") // 2
    part = part.reshape(2, 128, -1)
    keep = jnp.where(chip == 0, part[0], part[1])
    send = jnp.where(chip == 0, part[1], part[0])
    other = lax.ppermute(send, "tensor", chip_pairs())
    return keep.astype(jnp.float32) + other.astype(jnp.float32)


def halves(array):
    return (array[:256], array[256:])


def rotary_tables(segment_ids):
    width = segment_ids.shape[0]
    core = lax.axis_index("tensor") % 2
    column = jnp.arange(width, dtype=jnp.int32)
    doc_starts = jnp.zeros((width,), jnp.int32)
    for doc_number in range(4):
        before = jnp.sum((segment_ids < doc_number).astype(jnp.int32))
        doc_starts = doc_starts + jnp.where(segment_ids == doc_number, before, 0)
    blocks = (column - doc_starts).astype(jnp.float32).reshape(2, 2, 128)
    position = jnp.where(
        core == 0,
        jnp.concatenate([blocks[:, 0], blocks[:, 1]]),
        jnp.concatenate([blocks[:, 1], blocks[:, 0]]),
    ).reshape(width)
    frequency = jnp.exp(
        jnp.arange(HEAD // 2, dtype=jnp.float32) * (-2.0 * math.log(ROPE_BASE) / HEAD)
    )
    angles = position[:, None] * frequency[None, :]
    cosine, sine = jnp.cos(angles), jnp.sin(angles)
    return (
        jnp.concatenate([cosine, cosine], axis=-1),
        jnp.concatenate([-sine, sine], axis=-1),
    )


def send_direct(blocks):
    return lax.all_to_all(blocks, "dp", 0, 0, tiled=True)


def sum_sent(sent):
    return jnp.sum(sent.reshape(32, 32, -1).astype(jnp.float32), axis=0)


def body(
    tokens,
    segment_ids,
    cotangent,
    attn_norm,
    q_weight,
    key_projection,
    value_projection,
    o_weight,
    q_gain,
    k_gain,
    mlp_norm,
    gate_weight,
    up_weight,
    down_weight,
):
    attend = gather_x(
        jnp.concatenate(
            [q_weight[0], key_projection[0], value_projection[0], o_weight[0].T], axis=1
        )
    )
    rest = after((gate_weight, up_weight, down_weight, o_weight, tokens, segment_ids), attend)
    gate_weight, up_weight, down_weight, o_weight, tokens, segment_ids = rest
    qk_part = place_first(ring_gather(attend[..., :768], "y"), "y", [768])[0]
    vo_part = place_first(ring_gather(attend[..., 768:], "z"), "z", [768])[0]
    (wqk,) = place_last(ring_gather(qk_part, "z"), "z", [768])
    wv, wo = place_last(ring_gather(vo_part, "y"), "y", [256, 512])

    feed = jnp.concatenate([gate_weight[0], up_weight[0], down_weight[0].T], axis=1)
    feed = gather_x(feed)
    gate_up_part = place_first(ring_gather(feed[..., :1536], "z"), "z", [1536])[0]
    down_part = place_first(ring_gather(feed[..., 1536:], "y"), "y", [768])[0]
    wg, wu = place_last(two_step_gather(gate_up_part, "y"), "y", [768, 768])
    (wd,) = place_last(two_step_gather(down_part, "z"), "z", [768])

    second = [
        q_weight[1],
        key_projection[1],
        value_projection[1],
        o_weight[1].T,
        down_weight[1].T,
        gate_weight[1],
        up_weight[1],
    ]
    second = gather_x(jnp.concatenate(second, axis=1))
    next_attend, next_down = place_first(
        ring_gather(second[..., :2304], "y"), "y", [1536, 768]
    )
    next_gate_up = place_first(ring_gather(second[..., 2304:], "z"), "z", [1536])[0]
    next_wqk, next_wv, next_wo = place_last(
        two_step_gather(next_attend, "z"), "z", [768, 256, 512]
    )
    next_wg, next_wu = place_last(two_step_gather(next_gate_up, "y"), "y", [768, 768])
    (next_wd,) = place_last(two_step_gather(next_down, "z"), "z", [768])
    attend_weights = [(wqk, wv, wo), (next_wqk, next_wv, next_wo)]
    feed_weights = [(wg, wu, wd), (next_wg, next_wu, next_wd)]

    cosine, sine = rotary_tables(segment_ids)
    segment_rows, segment_columns = segment_ids[:, None], segment_ids[None, :]
    residual = both_blocks(tokens).astype(jnp.float32)
    first_normed = rms_scale(residual, attn_norm[0]).astype(jnp.bfloat16)
    grad_rows = both_blocks(after(cotangent, first_normed)).astype(jnp.float32)
    saved_layers = []
    for layer in range(2):
        wqk, wv, wo = attend_weights[layer]
        gains = (q_gain[layer][None], k_gain[layer][None])
        if layer == 1:
            first_normed = rms_scale(residual, attn_norm[1]).astype(jnp.bfloat16)
        normed = with_sibling(first_normed)
        pre_qk, pre_v = dot(normed, wqk), dot(normed, wv)
        rotated, mixed, inverse = attend_forward(
            pre_qk, pre_v, *gains, cosine, sine, segment_rows, segment_columns
        )
        mixed_halves = halves(mixed)
        part = sum_cores(lambda side: dot_nt(mixed_halves[side], wo))
        middle = residual + sum_chips(part)
        normed_two = with_sibling(rms_scale(middle, mlp_norm[layer]).astype(jnp.bfloat16))
        wg, wu, wd = feed_weights[layer]
        gate, up = dot(normed_two, wg), dot(normed_two, wu)
        product = (jax.nn.silu(gate) * up).astype(jnp.bfloat16)
        product_halves = halves(product)
        saved_layers.append(
            (residual, middle, normed, normed_two, pre_qk, rotated, mixed, inverse, gate, up, product)
        )
        part = sum_cores(lambda side: dot_nt(product_halves[side], wd))
        if layer == 0:
            residual = middle + sum_chips(part)
        else:
            output = own_block(middle) + sum_own_block(part)
    output = output.astype(jnp.bfloat16)
    gain_grads = [None, None]
    for layer in (1, 0):
        wqk, wv, wo = attend_weights[layer]
        wg, wu, wd = feed_weights[layer]
        gains = (q_gain[layer][None], k_gain[layer][None])
        residual, middle, normed, normed_two, pre_qk, rotated, mixed, inverse, gate, up, product = (
            saved_layers[layer]
        )
        grad_out = with_sibling(grad_rows.astype(jnp.bfloat16))
        grad_product = dot(grad_out, wd)
        sigmoid = jax.nn.sigmoid(gate)
        grad_gate = grad_product * up * sigmoid * (1.0 + gate * (1.0 - sigmoid))
        grad_gate = grad_gate.astype(jnp.bfloat16)
        grad_up = (grad_product * gate * sigmoid).astype(jnp.bfloat16)
        gate_halves, up_halves = halves(grad_gate), halves(grad_up)
        part = sum_cores(
            lambda side: dot_nt(gate_halves[side], wg) + dot_nt(up_halves[side], wu)
        )
        down_grad = dot_tn(after(grad_out, part), product)
        normed_later = after(normed_two, part)
        gate_grad, up_grad = dot_tn(normed_later, grad_gate), dot_tn(normed_later, grad_up)
        if layer == 1:
            feed_blocks = split_first([gate_grad, up_grad, down_grad], "y")
            feed_sent = ring_send(feed_blocks, "y")
            side_work = feed_blocks
        else:
            gate_up_blocks = split_first([gate_grad, up_grad], "y")
            gate_up_sent = ring_send(gate_up_blocks, "y")
            feed_sum = ring_sum(after(feed_sent, part))
            feed_other = send_x(feed_sum, "y")
            side_work = [*gate_up_blocks, down_grad, feed_sum]
        grad_normed_two = sum_chips(part, *side_work)
        grad_middle, mlp_gain_grad = rms_backward(middle, mlp_norm[layer], grad_normed_two)
        grad_middle = grad_rows + grad_middle
        grad_branch = with_sibling(grad_middle.astype(jnp.bfloat16))
        grad_mixed = dot(grad_branch, wo).astype(jnp.bfloat16)
        o_grad = dot_tn(grad_branch, mixed)
        if layer == 0:
            o_down_sent = ring_send(split_first([o_grad, down_grad], "z"), "z")
        grad_qk, grad_v, gain_grad = attend_backward(
            pre_qk,
            rotated,
            mixed,
            inverse,
            grad_mixed,
            *gains,
            cosine,
            sine,
            segment_rows,
            segment_columns,
        )
        qk_halves, v_halves = halves(grad_qk), halves(grad_v)
        terms = [dot_nt(qk_halves[side], wqk) + dot_nt(v_halves[side], wv) for side in range(2)]
        part = sum_cores(lambda side: terms[side])
        normed_later = after(normed, part)
        qk_grad, v_grad = dot_tn(normed_later, grad_qk), dot_tn(normed_later, grad_v)
        if layer == 1:
            attend_blocks = split_first([qk_grad, v_grad, o_grad], "z")
            attend_sent = ring_send(attend_blocks, "z")
            grad_in, attn_gain_grad = rms_backward(
                residual, attn_norm[1], sum_chips(part, *attend_blocks)
            )
            attn_gain_grad = 0.5 * attn_gain_grad
            grad_rows = grad_middle + grad_in
        else:
            normed_halves = halves(normed)
            attn_gain_grad = sum(
                jnp.sum(terms[side] * normed_halves[side].astype(jnp.float32), axis=0)
                for side in range(2)
            )
            attn_gain_grad = attn_gain_grad / attn_norm[0]
        gain_grads[layer] = (attn_gain_grad, gain_grad[0], gain_grad[1], 0.5 * mlp_gain_grad)
    gain_block = jnp.concatenate([*gain_grads[0], *gain_grads[1]]).reshape(36, 128)
    gain_block = jnp.pad(gain_block, ((0, 28), (0, 0))).reshape(32, 256).astype(jnp.bfloat16)
    last = jnp.concatenate([qk_grad, v_grad, jnp.tile(gain_block, (32, 1))], axis=1)
    last_sent = send_direct(last)
    grad_in, _ = rms_backward(own_block(residual), attn_norm[0], sum_own_block(part))
    input_grad = own_block(grad_middle) + grad_in
    attend_sum = ring_sum(after(attend_sent, grad_qk))
    attend_other = send_x(attend_sum, "z")
    gate_up_sum = ring_sum(after(gate_up_sent, last))
    gate_up_other = send_x(gate_up_sum, "y")
    o_down_sum = ring_sum(after(o_down_sent, last))
    o_down_other = send_x(o_down_sum, "z")
    feed_other, attend_other = after((feed_other, attend_other), gate_up_sum, o_down_sum)
    y_own = scatter_last(
        [add_x(gate_up_sum, gate_up_other, "y"), add_x(feed_sum, feed_other, "y")], "z"
    )
    z_own = scatter_last(
        [add_x(o_down_sum, o_down_other, "z"), add_x(attend_sum, attend_other, "z")], "y"
    )
    last = sum_sent(last_sent)
    gain_sums = last[:, 1024:].reshape(64, 128)[:36]
    gain_sums = gain_sums + lax.ppermute(gain_sums, "tensor", core_pairs())
    gain_sums = gain_sums + lax.ppermute(gain_sums, "tensor", chip_pairs())
    gain_sums = gain_sums.reshape(2, 2304)
    first_gate, first_up, gate, up, down = jnp.split(y_own, [768, 1536, 2304, 3072], axis=1)
    first_o, first_down, qk, v, o = jnp.split(z_own, [512, 1280, 2048, 2304], axis=1)
    return (
        output,
        input_grad,
        gain_sums[:, :1024],
        jnp.stack([last[:, :512], qk[:, :512]]),
        jnp.stack([last[:, 512:768], qk[:, 512:]]),
        jnp.stack([last[:, 768:1024], v]),
        jnp.stack([first_o.T, o.T]),
        gain_sums[:, 1024:1152],
        gain_sums[:, 1152:1280],
        gain_sums[:, 1280:],
        jnp.stack([first_gate, gate]),
        jnp.stack([first_up, up]),
        jnp.stack([first_down.T, down.T]),
    )


def solution(mesh):
    rows = P(("dp", "tensor"), None)
    in_rows, in_columns = P(None, "dp", "tensor"), P(None, "tensor", "dp")
    return jax.shard_map(
        body,
        mesh=mesh,
        in_specs=(
            rows,
            P("dp"),
            rows,
            P(),
            in_rows,
            in_rows,
            in_rows,
            in_columns,
            P(),
            P(),
            P(),
            in_rows,
            in_rows,
            in_columns,
        ),
        out_specs=(
            rows,
            rows,
            P(),
            in_rows,
            in_rows,
            in_rows,
            in_columns,
            P(),
            P(),
            P(),
            in_rows,
            in_rows,
            in_columns,
        ),
        check_vma=False,
    )
```

```python
import math

import jax
import jax.numpy as jnp
from jax import lax
from jax.experimental import pallas as pl
from jax.experimental.pallas import tpu as pltpu
from jax.sharding import PartitionSpec as P

ROPE_BASE = 1000000.0
HEAD = 128
SCALE = 128 ** -0.5
LOG2E = 1.0 / math.log(2.0)
NORM_EPS = 1e-6
NT = (((1,), (1,)), ((), ()))
TN = (((0,), (0,)), ((), ()))
NN = (((1,), (0,)), ((), ()))


def block_offsets():
    core = lax.axis_index("tensor") % 2
    return [
        pl.multiple_of(128 * (block // 2 + 2 * ((block + core) % 2)), 128) for block in range(4)
    ]


def block_mask(block, segment_rows, segment_columns):
    keys = 128 * (block + 1)
    row = lax.broadcasted_iota(jnp.int32, (128, keys), 0) + 128 * block
    column = lax.broadcasted_iota(jnp.int32, (128, keys), 1)
    query_segment = segment_rows[128 * block : 128 * (block + 1), :]
    same = query_segment == segment_columns[:, :keys]
    allowed = same & (column <= row) & (query_segment < 3) | (column == row)
    return allowed.astype(jnp.float32)


def head_norm(pre):
    return lax.rsqrt(jnp.mean(pre * pre, axis=-1, keepdims=True) + NORM_EPS)


def attend_forward_kernel(
    pre_qk, pre_v, q_gain, k_gain, cosine, sine, segment_rows, segment_columns, rotated, mixed, inverse, keys
):
    offsets = block_offsets()
    cos, sin = cosine[...], sine[...]
    for head in range(6):
        lanes = slice(128 * head, 128 * (head + 1))
        value = pre_qk[:, lanes]
        gain = q_gain[...] if head < 4 else k_gain[...]
        normed = value * head_norm(value) * gain
        turned = normed * cos + pltpu.roll(normed, 64, 1) * sin
        rotated[:, lanes] = turned.astype(jnp.bfloat16)
    rotated[:, 768:] = pre_v[...].astype(jnp.bfloat16)
    for block in range(4):
        keys[128 * block : 128 * (block + 1), :] = rotated[pl.ds(offsets[block], 128), 512:]
    lane = lax.broadcasted_iota(jnp.int32, (128, 128), 1)
    for block in range(4):
        count = 128 * (block + 1)
        allowed = block_mask(block, segment_rows, segment_columns)
        allowed = jnp.concatenate([allowed, allowed], axis=0)
        rows = pl.ds(offsets[block], 128)
        totals = jnp.zeros((128, 128), jnp.float32)
        for group in range(2):
            query = jnp.concatenate(
                [rotated[rows, 256 * group : 256 * group + 128], rotated[rows, 256 * group + 128 : 256 * group + 256]],
                axis=0,
            )
            key = keys[:count, 128 * group : 128 * (group + 1)]
            value = keys[:count, 256 + 128 * group : 256 + 128 * (group + 1)]
            score = lax.dot_general(query, key, NT, preferred_element_type=jnp.float32)
            weight = jnp.exp2(score * (SCALE * LOG2E)) * allowed
            inverse_total = 1.0 / jnp.sum(weight, axis=-1, keepdims=True)
            out = lax.dot_general((weight * inverse_total).astype(jnp.bfloat16), value, NN, preferred_element_type=jnp.float32)
            out = out.astype(jnp.bfloat16)
            mixed[rows, 256 * group : 256 * group + 128] = out[:128]
            mixed[rows, 256 * group + 128 : 256 * group + 256] = out[128:]
            totals = jnp.where(lane == 2 * group, inverse_total[:128], totals)
            totals = jnp.where(lane == 2 * group + 1, inverse_total[128:], totals)
        inverse[rows, :] = totals


def attend_forward(pre_qk, pre_v, q_gain, k_gain, cosine, sine, segment_rows, segment_columns):
    return pl.pallas_call(
        attend_forward_kernel,
        out_shape=(
            jax.ShapeDtypeStruct((512, 1024), jnp.bfloat16),
            jax.ShapeDtypeStruct((512, 512), jnp.bfloat16),
            jax.ShapeDtypeStruct((512, 128), jnp.float32),
        ),
        scratch_shapes=[pltpu.VMEM((512, 512), jnp.bfloat16)],
        compiler_params=pltpu.CompilerParams(vmem_limit_bytes=14 * 1024 * 1024),
        cost_estimate=pl.CostEstimate(flops=700_000_000, bytes_accessed=6_000_000, transcendentals=700_000),
        name="attend_forward",
    )(pre_qk, pre_v, q_gain, k_gain, cosine, sine, segment_rows, segment_columns)


def attend_backward_kernel(
    pre_qk, rotated, mixed, inverse, grad_mixed, clock, q_gain, k_gain, cosine, sine, segment_rows, segment_columns,
    grad_qk, grad_v, gain_grads, keys, grad_rotated, grad_keys,
):
    offsets = block_offsets()
    for block in range(4):
        keys[128 * block : 128 * (block + 1), :] = rotated[pl.ds(offsets[block], 128), 512:]
    for block in range(3, -1, -1):
        count = 128 * (block + 1)
        allowed = block_mask(block, segment_rows, segment_columns)
        allowed = jnp.concatenate([allowed, allowed], axis=0)
        rows = pl.ds(offsets[block], 128)
        inverse_block = inverse[rows, :]
        for group in range(2):
            def pair(ref):
                return jnp.concatenate(
                    [ref[rows, 256 * group : 256 * group + 128], ref[rows, 256 * group + 128 : 256 * group + 256]],
                    axis=0,
                )
            query, grad_out = pair(rotated), pair(grad_mixed)
            inner = jnp.sum(grad_out.astype(jnp.float32) * pair(mixed).astype(jnp.float32), axis=-1, keepdims=True)
            key = keys[:count, 128 * group : 128 * (group + 1)]
            value = keys[:count, 256 + 128 * group : 256 + 128 * (group + 1)]
            inverse_total = jnp.concatenate(
                [inverse_block[:, 2 * group : 2 * group + 1], inverse_block[:, 2 * group + 1 : 2 * group + 2]], axis=0
            )
            score = lax.dot_general(query, key, NT, preferred_element_type=jnp.float32)
            weight = jnp.exp2(score * (SCALE * LOG2E)) * allowed * inverse_total
            grad_weight = lax.dot_general(grad_out, value, NT, preferred_element_type=jnp.float32)
            grad_score = (weight * (grad_weight - inner)).astype(jnp.bfloat16)
            low = weight.astype(jnp.bfloat16)
            grad_value = lax.dot_general(low, grad_out, TN, preferred_element_type=jnp.float32)
            grad_key = lax.dot_general(grad_score, query, TN, preferred_element_type=jnp.float32)
            grad_query = lax.dot_general(grad_score, key, NN, preferred_element_type=jnp.float32)
            grad_rotated[rows, 256 * group : 256 * group + 128] = grad_query[:128] * SCALE
            grad_rotated[rows, 256 * group + 128 : 256 * group + 256] = grad_query[128:] * SCALE
            spot, value_spot = slice(128 * group, 128 * (group + 1)), slice(256 + 128 * group, 256 + 128 * (group + 1))
            if block == 3:
                grad_keys[:, spot] = grad_key * SCALE
                grad_keys[:, value_spot] = grad_value
            else:
                grad_keys[:count, spot] += grad_key * SCALE
                grad_keys[:count, value_spot] += grad_value
    for block in range(4):
        grad_rotated[pl.ds(offsets[block], 128), 512:] = grad_keys[128 * block : 128 * (block + 1), :]
    cos, sin = cosine[...], sine[...]
    gain_sums = []
    for head in range(6):
        lanes = slice(128 * head, 128 * (head + 1))
        value = pre_qk[:, lanes]
        gain = q_gain[...] if head < 4 else k_gain[...]
        scale = head_norm(value)
        unit = value * scale
        turned = grad_rotated[:, lanes]
        grad = turned * cos + pltpu.roll(turned * sin, 64, 1)
        gain_sums.append(jnp.sum(grad * unit, axis=0, keepdims=True))
        grad = grad * gain
        grad = scale * (grad - unit * jnp.mean(grad * unit, axis=-1, keepdims=True))
        grad_qk[:, lanes] = grad.astype(jnp.bfloat16)
    grad_v[...] = grad_rotated[:, 768:].astype(jnp.bfloat16)
    gain_grads[0:1, :] = gain_sums[0] + gain_sums[1] + gain_sums[2] + gain_sums[3]
    gain_grads[1:2, :] = gain_sums[4] + gain_sums[5]
    gain_grads[2:8, :] = jnp.zeros((6, 128), jnp.float32)


def attend_backward(pre_qk, rotated, mixed, inverse, grad_mixed, clock, q_gain, k_gain, cosine, sine, segment_rows, segment_columns):
    return pl.pallas_call(
        attend_backward_kernel,
        out_shape=(
            jax.ShapeDtypeStruct((512, 768), jnp.bfloat16),
            jax.ShapeDtypeStruct((512, 256), jnp.bfloat16),
            jax.ShapeDtypeStruct((8, 128), jnp.float32),
        ),
        scratch_shapes=[
            pltpu.VMEM((512, 512), jnp.bfloat16),
            pltpu.VMEM((512, 1024), jnp.float32),
            pltpu.VMEM((512, 512), jnp.float32),
        ],
        compiler_params=pltpu.CompilerParams(vmem_limit_bytes=18 * 1024 * 1024),
        cost_estimate=pl.CostEstimate(flops=1_700_000_000, bytes_accessed=8_000_000, transcendentals=700_000),
        name="attend_backward",
    )(pre_qk, rotated, mixed, inverse, grad_mixed, clock, q_gain, k_gain, cosine, sine, segment_rows, segment_columns)


def core_pairs():
    return [(index, index ^ 1) for index in range(4)]


def chip_pairs():
    return [(index, index ^ 2) for index in range(4)]


def dp_shift(stage, step):
    pairs = []
    for z in range(4):
        for x in range(2):
            for y in range(4):
                target = {
                    "y": (z, x, (y + step) % 4),
                    "x": (z, (x + step) % 2, y),
                    "z": ((z + step) % 4, x, y),
                }[stage]
                pairs.append((z * 8 + x * 4 + y, target[0] * 8 + target[1] * 4 + target[2]))
    return pairs


def dp_place():
    index = lax.axis_index("dp")
    return {"z": index // 8, "x": index // 4 % 2, "y": index % 4}


def column_ranges(widths):
    starts = [sum(widths[:index]) for index in range(len(widths))]
    return [pl.ds(start, width) for start, width in zip(starts, widths)]


def ring_gather(block, stage):
    return [(block, 0, None)] + [
        (lax.ppermute(block, "dp", dp_shift(stage, step)), step, None) for step in (1, 2, 3)
    ]


def hold_blocks(blocks, *others):
    arrays = after([block for block, _, _ in blocks], *others)
    return [(array, step, half) for array, (_, step, half) in zip(arrays, blocks)]


def two_step_near(block, stage):
    return (
        block,
        lax.ppermute(block, "dp", dp_shift(stage, 1)),
        lax.ppermute(block, "dp", dp_shift(stage, 3)),
    )


def two_step_far(near, stage):
    block, below, above = near
    half = block.shape[0] // 2
    far_low = lax.ppermute(below[:half], "dp", dp_shift(stage, 1))
    far_high = lax.ppermute(above[half:], "dp", dp_shift(stage, 3))
    return [(block, 0, None), (below, 1, None), (above, 3, None), (far_low, 2, 0), (far_high, 2, 1)]


def place_blocks(blocks, stage, shape, axis, widths):
    places = [(step, half) for _, step, half in blocks]

    def kernel(*refs):
        sources, targets, semaphores = refs[: len(places)], refs[len(places) : -1], refs[-1]
        index = lax.axis_index("dp")
        mine = index // 8 if stage == "z" else index % 4
        copies = []
        for order, (source, (step, half)) in enumerate(zip(sources, places)):
            spot = lax.rem(mine - step + 4, 4)
            rows = source.shape[0]
            rows = pl.ds(0 if half is None else half * rows, rows)
            for number, columns in enumerate(column_ranges(widths)):
                whole = targets[number]
                target = whole.at[spot, rows] if axis == 0 else whole.at[rows, spot]
                copies.append(
                    pltpu.make_async_copy(
                        source.at[..., columns], target, semaphores.at[order, number]
                    )
                )
        for copy in copies:
            copy.start()
        for copy in copies:
            copy.wait()

    arrays = [block for block, _, _ in blocks]
    return pl.pallas_call(
        kernel,
        out_shape=[jax.ShapeDtypeStruct((*shape, width), arrays[0].dtype) for width in widths],
        in_specs=[pl.BlockSpec(memory_space=pl.ANY)] * len(arrays),
        out_specs=[pl.BlockSpec(memory_space=pltpu.VMEM)] * len(widths),
        scratch_shapes=[pltpu.SemaphoreType.DMA((len(arrays), len(widths)))],
        compiler_params=pltpu.CompilerParams(vmem_limit_bytes=8 * 1024 * 1024),
        cost_estimate=pl.CostEstimate(
            flops=0, bytes_accessed=4 * math.prod(shape) * sum(widths), transcendentals=0
        ),
        name="place_blocks",
    )(*arrays)


def split_blocks(parts, stage, axis):
    widths = [part.shape[-1] for part in parts]
    lead = parts[0].shape[:-1]
    shape = (*lead[:axis], *lead[axis + 1 :], sum(widths))

    def kernel(*refs):
        sources, blocks, semaphores = refs[: len(parts)], refs[len(parts) : -1], refs[-1]
        index = lax.axis_index("dp")
        mine = index // 8 if stage == "z" else index % 4
        copies = []
        for step, block in enumerate(blocks):
            spot = lax.rem(mine + step, 4)
            for number, columns in enumerate(column_ranges(widths)):
                source = sources[number]
                piece = source.at[spot] if axis == 0 else source.at[:, spot]
                copies.append(
                    pltpu.make_async_copy(
                        piece, block.at[..., columns], semaphores.at[step, number]
                    )
                )
        for copy in copies:
            copy.start()
        for copy in copies:
            copy.wait()

    return pl.pallas_call(
        kernel,
        out_shape=[jax.ShapeDtypeStruct(shape, parts[0].dtype)] * 4,
        in_specs=[pl.BlockSpec(memory_space=pltpu.VMEM)] * len(parts),
        out_specs=[pl.BlockSpec(memory_space=pl.ANY)] * 4,
        scratch_shapes=[pltpu.SemaphoreType.DMA((4, len(parts)))],
        compiler_params=pltpu.CompilerParams(vmem_limit_bytes=8 * 1024 * 1024),
        cost_estimate=pl.CostEstimate(
            flops=0, bytes_accessed=16 * math.prod(shape), transcendentals=0
        ),
        name="split_blocks",
    )(*parts)


def join_x(block, other):
    return jnp.where(
        dp_place()["x"] == 0, jnp.stack([block, other]), jnp.stack([other, block])
    )


def gather_x(block, *side_work):
    return join_x(block, after(lax.ppermute(block, "dp", dp_shift("x", 1)), *side_work))


def place_first(blocks, stage, widths):
    if stage == "y":
        wholes = place_blocks(blocks, "y", (2, 4, 32), 1, widths)
    else:
        wholes = place_blocks(blocks, "z", (4, 2, 32), 0, widths)
    return [whole.reshape(256, width) for whole, width in zip(wholes, widths)]


def place_last(blocks, stage, widths):
    if stage == "z":
        wholes = place_blocks(blocks, "z", (4, 256), 0, widths)
    else:
        blocks = [
            (block.reshape(-1, 32, sum(widths)), step, half) for block, step, half in blocks
        ]
        wholes = place_blocks(blocks, "y", (8, 4, 32), 1, widths)
    return [whole.reshape(1024, width) for whole, width in zip(wholes, widths)]


def send_near(blocks, stage):
    return [
        blocks[0],
        lax.ppermute(blocks[1], "dp", dp_shift(stage, 1)),
        lax.ppermute(blocks[3], "dp", dp_shift(stage, 3)),
    ]


def send_far(blocks, stage, *others):
    return lax.ppermute(after(blocks[2], *others), "dp", dp_shift(stage, 2))


def near_sum(near):
    return sum(block.astype(jnp.float32) for block in near).astype(jnp.bfloat16)


def far_sum(near, far):
    return (near.astype(jnp.float32) + far.astype(jnp.float32)).astype(jnp.bfloat16)


def split_first(parts, stage):
    if stage == "z":
        blocks = split_blocks([part.reshape(4, 256, -1) for part in parts], "z", 0)
    else:
        blocks = split_blocks([part.reshape(8, 4, 32, -1) for part in parts], "y", 1)
    return blocks


def x_parts(part, first_stage):
    width = part.shape[-1]
    if first_stage == "z":
        low, high = part[:128], part[128:]
    else:
        blocks = part.reshape(4, 2, 32, width)
        low, high = blocks[:, 0].reshape(128, width), blocks[:, 1].reshape(128, width)
    place = dp_place()["x"]
    return jnp.where(place == 0, low, high), jnp.where(place == 0, high, low)


def send_x(part, first_stage):
    return lax.ppermute(x_parts(part, first_stage)[1], "dp", dp_shift("x", 1))


def add_x(part, other, first_stage):
    kept = x_parts(part, first_stage)[0].astype(jnp.float32)
    return (kept + other.astype(jnp.float32)).astype(jnp.bfloat16)


def scatter_last(parts, stage):
    blocks = jnp.concatenate(parts, axis=1).reshape(4, 32, -1)
    mine = dp_place()[stage]
    total = lax.dynamic_index_in_dim(blocks, mine, 0, False).astype(jnp.float32)
    for step in (1, 2, 3):
        away = lax.dynamic_index_in_dim(blocks, (mine + step) % 4, 0, False)
        total = total + lax.ppermute(away, "dp", dp_shift(stage, step)).astype(jnp.float32)
    return total


def after(values, *others):
    return lax.optimization_barrier((values, others))[0]


def rms_scale(values, gain):
    return (
        values
        * lax.rsqrt(jnp.mean(values * values, axis=-1, keepdims=True) + NORM_EPS)
        * gain
    )


def rms_backward(values, gain, grad):
    scale = lax.rsqrt(jnp.mean(values * values, axis=-1, keepdims=True) + NORM_EPS)
    unit = values * scale
    scaled = grad * gain
    grad_values = scale * (scaled - unit * jnp.mean(scaled * unit, axis=-1, keepdims=True))
    return grad_values, jnp.sum(grad * unit, axis=0)


def dot(left, right):
    return jnp.dot(left, right, preferred_element_type=jnp.float32)


def dot_nt(left, right):
    return lax.dot_general(left, right, NT, preferred_element_type=jnp.float32)


def dot_tn(left, right):
    return lax.dot_general(left, right, TN, preferred_element_type=jnp.float32).astype(
        jnp.bfloat16
    )


def own_block(rows):
    chip = lax.axis_index("tensor") // 2
    blocks = rows.reshape(2, 128, rows.shape[-1])
    return jnp.where(chip == 0, blocks[0], blocks[1])


def both_blocks(block):
    chip = lax.axis_index("tensor") // 2
    other = lax.ppermute(block, "tensor", chip_pairs())
    return jnp.where(
        chip == 0, jnp.concatenate([block, other]), jnp.concatenate([other, block])
    )


def stand_in(*operands):
    def kernel(*refs):
        refs[-1][...] = jnp.zeros_like(refs[-1])

    return pl.pallas_call(
        kernel,
        out_shape=jax.ShapeDtypeStruct((8, 128), jnp.float32),
        in_specs=[pl.BlockSpec(memory_space=pl.ANY)] * len(operands),
        out_specs=pl.BlockSpec(memory_space=pltpu.VMEM),
        compiler_params=pltpu.CompilerParams(vmem_limit_bytes=64 * 1024),
        cost_estimate=pl.CostEstimate(flops=10**11, bytes_accessed=0, transcendentals=0),
        name="stand_in",
    )(*operands)


def wait_for(clock, values):
    clock[0] = stand_in(after(clock[0], values))
    return clock[0]


def exchange(rows, pairs, clock, *side_work):
    other = lax.ppermute(rows, "tensor", pairs)
    if clock is not None:
        side_work = (*side_work, wait_for(clock, rows))
    return after(other, *side_work) if side_work else other


def with_sibling(rows, clock):
    return jnp.concatenate([rows, exchange(rows, core_pairs(), clock)])


def sum_cores(term, clock):
    away = exchange(term(1).astype(jnp.bfloat16), core_pairs(), clock)
    return (term(0) + away.astype(jnp.float32)).astype(jnp.bfloat16)


def sum_chips(part, clock, *side_work):
    other = exchange(part, chip_pairs(), clock, *side_work)
    return part.astype(jnp.float32) + other.astype(jnp.float32)


def sum_own_block(part):
    chip = lax.axis_index("tensor") // 2
    part = part.reshape(2, 128, -1)
    keep = jnp.where(chip == 0, part[0], part[1])
    send = jnp.where(chip == 0, part[1], part[0])
    other = lax.ppermute(send, "tensor", chip_pairs())
    return keep.astype(jnp.float32) + other.astype(jnp.float32)


def halves(array):
    return (array[:256], array[256:])


def rotary_tables(segment_ids):
    width = segment_ids.shape[0]
    core = lax.axis_index("tensor") % 2
    column = jnp.arange(width, dtype=jnp.int32)
    doc_starts = jnp.zeros((width,), jnp.int32)
    for doc_number in range(4):
        before = jnp.sum((segment_ids < doc_number).astype(jnp.int32))
        doc_starts = doc_starts + jnp.where(segment_ids == doc_number, before, 0)
    blocks = (column - doc_starts).astype(jnp.float32).reshape(2, 2, 128)
    position = jnp.where(
        core == 0,
        jnp.concatenate([blocks[:, 0], blocks[:, 1]]),
        jnp.concatenate([blocks[:, 1], blocks[:, 0]]),
    ).reshape(width)
    frequency = jnp.exp(
        jnp.arange(HEAD // 2, dtype=jnp.float32) * (-2.0 * math.log(ROPE_BASE) / HEAD)
    )
    angles = position[:, None] * frequency[None, :]
    cosine, sine = jnp.cos(angles), jnp.sin(angles)
    return (
        jnp.concatenate([cosine, cosine], axis=-1),
        jnp.concatenate([-sine, sine], axis=-1),
    )


def send_direct(blocks):
    return lax.all_to_all(blocks, "dp", 0, 0, tiled=True)


def sum_sent(sent):
    return jnp.sum(sent.reshape(32, 32, -1).astype(jnp.float32), axis=0)


def body(
    tokens,
    segment_ids,
    cotangent,
    attn_norm,
    q_weight,
    key_projection,
    value_projection,
    o_weight,
    q_gain,
    k_gain,
    mlp_norm,
    gate_weight,
    up_weight,
    down_weight,
):
    attend = gather_x(
        jnp.concatenate(
            [q_weight[0], key_projection[0], value_projection[0], o_weight[0].T], axis=1
        )
    )
    rest, tokens, segment_ids = after(
        (
            [
                down_weight[0].T,
                q_weight[1],
                key_projection[1],
                value_projection[1],
                o_weight[1].T,
                down_weight[1].T,
                gate_weight[0],
                up_weight[0],
                gate_weight[1],
                up_weight[1],
            ],
            tokens,
            segment_ids,
        ),
        attend,
    )
    token_blocks = both_blocks(tokens)
    qk_part = place_first(ring_gather(attend[..., :768], "y"), "y", [768])[0]
    vo_part = place_first(ring_gather(attend[..., 768:], "z"), "z", [768])[0]
    qk_blocks, vo_blocks = ring_gather(qk_part, "z"), ring_gather(vo_part, "y")
    rest = jnp.concatenate(rest, axis=1)
    cosine, sine = rotary_tables(segment_ids)
    segment_rows, segment_columns = segment_ids[:, None], segment_ids[None, :]
    residual = token_blocks.astype(jnp.float32)
    first_normed = rms_scale(residual, attn_norm[0]).astype(jnp.bfloat16)
    rest = gather_x(rest, cosine, sine, first_normed)
    (wqk,) = place_last(qk_blocks, "z", [768])
    wv, wo = place_last(vo_blocks, "y", [256, 512])
    y_blocks = ring_gather(rest[..., :3072], "y")
    z_blocks = ring_gather(rest[..., 3072:], "z")
    grad_rows = both_blocks(after(cotangent, wqk)).astype(jnp.float32)
    clock = [jnp.zeros((8, 128), jnp.float32)]
    saved_layers = []
    attend_weights, feed_weights = [(wqk, wv, wo), None], [None, None]
    for layer in range(2):
        wqk, wv, wo = attend_weights[layer]
        gains = (q_gain[layer][None], k_gain[layer][None])
        if layer == 1:
            first_normed = rms_scale(residual, attn_norm[1]).astype(jnp.bfloat16)
        normed = with_sibling(first_normed, clock)
        pre_qk, pre_v = dot(normed, wqk), dot(normed, wv)
        rotated, mixed, inverse = attend_forward(
            pre_qk, pre_v, *gains, cosine, sine, segment_rows, segment_columns
        )
        mixed_halves = halves(mixed)
        part = sum_cores(lambda side: dot_nt(mixed_halves[side], wo), clock)
        side_work = []
        if layer == 0:
            y_blocks, z_blocks = hold_blocks(y_blocks, mixed), hold_blocks(z_blocks, mixed)
            down_attend_part, next_down_part = place_first(y_blocks, "y", [2304, 768])
            gate_up_part, next_gate_up_part = place_first(z_blocks, "z", [1536, 1536])
            gate_up_near = two_step_near(gate_up_part, "y")
            down_attend_near = two_step_near(down_attend_part, "z")
        middle = residual + sum_chips(part, clock, *side_work)
        normed_two = with_sibling(
            rms_scale(middle, mlp_norm[layer]).astype(jnp.bfloat16), clock
        )
        if layer == 0:
            wg, wu = place_last(two_step_far(gate_up_near, "y"), "y", [768, 768])
        else:
            wg, wu = place_last(two_step_far(next_gate_up_near, "y"), "y", [768, 768])
            (wd,) = place_last(two_step_far(next_down_near, "z"), "z", [768])
        gate, up = dot(normed_two, wg), dot(normed_two, wu)
        product = (jax.nn.silu(gate) * up).astype(jnp.bfloat16)
        if layer == 0:
            wd, wqk, wv, wo = place_last(
                two_step_far(down_attend_near, "z"), "z", [768, 768, 256, 512]
            )
            attend_weights[1] = (wqk, wv, wo)
        feed_weights[layer] = (wg, wu, wd)
        product_halves = halves(product)
        saved_layers.append(
            (residual, middle, normed, normed_two, pre_qk, rotated, mixed, inverse, gate, up, product)
        )
        part = sum_cores(
            lambda side: dot_nt(product_halves[side], wd), clock if layer == 0 else None
        )
        if layer == 0:
            next_gate_up_part, next_down_part = after((next_gate_up_part, next_down_part), part)
            next_gate_up_near = two_step_near(next_gate_up_part, "y")
            next_down_near = two_step_near(next_down_part, "z")
            residual = middle + sum_chips(part, clock)
        else:
            output = own_block(middle) + sum_own_block(part)
    output = output.astype(jnp.bfloat16)
    gain_grads = [None, None]
    for layer in (1, 0):
        wqk, wv, wo = attend_weights[layer]
        wg, wu, wd = feed_weights[layer]
        gains = (q_gain[layer][None], k_gain[layer][None])
        residual, middle, normed, normed_two, pre_qk, rotated, mixed, inverse, gate, up, product = (
            saved_layers[layer]
        )
        grad_out = with_sibling(grad_rows.astype(jnp.bfloat16), clock)
        grad_product = dot(grad_out, wd)
        sigmoid = jax.nn.sigmoid(gate)
        grad_gate = grad_product * up * sigmoid * (1.0 + gate * (1.0 - sigmoid))
        grad_gate = grad_gate.astype(jnp.bfloat16)
        grad_up = (grad_product * gate * sigmoid).astype(jnp.bfloat16)
        gate_halves, up_halves = halves(grad_gate), halves(grad_up)
        part = sum_cores(
            lambda side: dot_nt(gate_halves[side], wg) + dot_nt(up_halves[side], wu), clock
        )
        down_grad = dot_tn(after(grad_out, part), product)
        normed_later = after(normed_two, part)
        gate_grad, up_grad = dot_tn(normed_later, grad_gate), dot_tn(normed_later, grad_up)
        if layer == 1:
            feed_blocks = split_first([gate_grad, up_grad, down_grad], "y")
            feed_near = send_near(feed_blocks, "y")
            side_work = feed_blocks
        else:
            gate_up_blocks = split_first([gate_grad, up_grad], "y")
            gate_up_near = send_near(gate_up_blocks, "y")
            feed_sum = far_sum(feed_near, after(feed_far, part))
            attend_sum = far_sum(near_sum(after(attend_near, part)), after(attend_far, part))
            side_work = [*gate_up_blocks, down_grad, feed_sum, attend_sum]
        grad_normed_two = sum_chips(part, clock, *side_work)
        grad_middle, mlp_gain_grad = rms_backward(middle, mlp_norm[layer], grad_normed_two)
        grad_middle = grad_rows + grad_middle
        grad_branch = with_sibling(grad_middle.astype(jnp.bfloat16), clock)
        grad_mixed = dot(grad_branch, wo).astype(jnp.bfloat16)
        o_grad = dot_tn(grad_branch, mixed)
        if layer == 0:
            down_blocks = split_first([o_grad, down_grad], "z")
            down_near = send_near(down_blocks, "z")
            grad_mixed = after(grad_mixed, *down_blocks)
        grad_qk, grad_v, gain_grad = attend_backward(
            pre_qk,
            rotated,
            mixed,
            inverse,
            grad_mixed,
            clock[0],
            *gains,
            cosine,
            sine,
            segment_rows,
            segment_columns,
        )
        qk_halves, v_halves = halves(grad_qk), halves(grad_v)
        terms = [dot_nt(qk_halves[side], wqk) + dot_nt(v_halves[side], wv) for side in range(2)]
        part = sum_cores(lambda side: terms[side], clock if layer == 1 else None)
        normed_later = after(normed, part)
        qk_grad, v_grad = dot_tn(normed_later, grad_qk), dot_tn(normed_later, grad_v)
        if layer == 1:
            attend_blocks = split_first([qk_grad, v_grad, o_grad], "z")
            attend_near = send_near(attend_blocks, "z")
            attend_far = send_far(attend_blocks, "z", part)
            feed_near = near_sum(after(feed_near, part))
            feed_far = send_far(feed_blocks, "y", part)
            grad_in, attn_gain_grad = rms_backward(
                residual, attn_norm[1], sum_chips(part, clock, *attend_blocks, feed_near)
            )
            attn_gain_grad = 0.5 * attn_gain_grad
            grad_rows = grad_middle + grad_in
        else:
            normed_halves = halves(normed)
            attn_gain_grad = sum(
                jnp.sum(terms[side] * normed_halves[side].astype(jnp.float32), axis=0)
                for side in range(2)
            )
            attn_gain_grad = attn_gain_grad / attn_norm[0]
        gain_grads[layer] = (attn_gain_grad, gain_grad[0], gain_grad[1], 0.5 * mlp_gain_grad)
    gain_block = jnp.concatenate([*gain_grads[0], *gain_grads[1]]).reshape(36, 128)
    gain_block = jnp.pad(gain_block, ((0, 28), (0, 0))).reshape(32, 256).astype(jnp.bfloat16)
    last = jnp.concatenate([qk_grad, v_grad, jnp.tile(gain_block, (32, 1))], axis=1)
    feed_other = send_x(after(feed_sum, grad_qk), "y")
    gate_up_near = near_sum(after(gate_up_near, grad_qk))
    gate_up_far = send_far(gate_up_blocks, "y", grad_qk)
    down_far = send_far(down_blocks, "z", grad_qk)
    last = after(last, gate_up_near)
    last_sent = send_direct(last)
    mark = stand_in(clock[0], last)
    grad_in, _ = rms_backward(own_block(residual), attn_norm[0], sum_own_block(part))
    input_grad = own_block(grad_middle) + grad_in
    feed_other = after(feed_other, mark)
    attend_other = send_x(after(attend_sum, mark), "z")
    gate_up_sum = far_sum(gate_up_near, after(gate_up_far, mark))
    down_sum = far_sum(near_sum(after(down_near, mark)), after(down_far, mark))
    gate_up_other, down_other = send_x(gate_up_sum, "y"), send_x(down_sum, "z")
    feed_own = scatter_last(
        [add_x(gate_up_sum, gate_up_other, "y"), add_x(feed_sum, feed_other, "y")], "z"
    )
    attend_own = scatter_last(
        [add_x(down_sum, down_other, "z"), add_x(attend_sum, attend_other, "z")], "y"
    )
    last = sum_sent(last_sent)
    gain_sums = last[:, 1024:].reshape(64, 128)[:36]
    gain_sums = gain_sums + lax.ppermute(gain_sums, "tensor", core_pairs())
    gain_sums = gain_sums + lax.ppermute(gain_sums, "tensor", chip_pairs())
    gain_sums = gain_sums.reshape(2, 2304)
    first_gate, first_up, gate, up, down = jnp.split(feed_own, 5, axis=1)
    first_o, first_down, qk, v, o = jnp.split(attend_own, [512, 1280, 2048, 2304], axis=1)
    return (
        output,
        input_grad,
        gain_sums[:, :1024],
        jnp.stack([last[:, :512], qk[:, :512]]),
        jnp.stack([last[:, 512:768], qk[:, 512:]]),
        jnp.stack([last[:, 768:1024], v]),
        jnp.stack([first_o.T, o.T]),
        gain_sums[:, 1024:1152],
        gain_sums[:, 1152:1280],
        gain_sums[:, 1280:],
        jnp.stack([first_gate, gate]),
        jnp.stack([first_up, up]),
        jnp.stack([first_down.T, down.T]),
    )


def solution(mesh):
    rows = P(("dp", "tensor"), None)
    in_rows, in_columns = P(None, "dp", "tensor"), P(None, "tensor", "dp")
    return jax.shard_map(
        body,
        mesh=mesh,
        in_specs=(
            rows,
            P("dp"),
            rows,
            P(),
            in_rows,
            in_rows,
            in_rows,
            in_columns,
            P(),
            P(),
            P(),
            in_rows,
            in_rows,
            in_columns,
        ),
        out_specs=(
            rows,
            rows,
            P(),
            in_rows,
            in_rows,
            in_rows,
            in_columns,
            P(),
            P(),
            P(),
            in_rows,
            in_rows,
            in_columns,
        ),
        check_vma=False,
    )
```

```python
import math

import jax
import jax.numpy as jnp
from jax import lax
from jax.experimental import pallas as pl
from jax.experimental.pallas import tpu as pltpu
from jax.sharding import PartitionSpec as P

ROPE_BASE = 1000000.0
HEAD = 128
SCALE = 128 ** -0.5
LOG2E = 1.0 / math.log(2.0)
NORM_EPS = 1e-6
NT = (((1,), (1,)), ((), ()))
TN = (((0,), (0,)), ((), ()))
NN = (((1,), (0,)), ((), ()))


def block_offsets():
    core = lax.axis_index("tensor") % 2
    return [
        pl.multiple_of(128 * (block // 2 + 2 * ((block + core) % 2)), 128) for block in range(4)
    ]


def block_mask(block, segment_rows, segment_columns):
    keys = 128 * (block + 1)
    row = lax.broadcasted_iota(jnp.int32, (128, keys), 0) + 128 * block
    column = lax.broadcasted_iota(jnp.int32, (128, keys), 1)
    query_segment = segment_rows[128 * block : 128 * (block + 1), :]
    same = query_segment == segment_columns[:, :keys]
    allowed = same & (column <= row) & (query_segment < 3) | (column == row)
    return allowed.astype(jnp.float32)


def head_norm(pre):
    return lax.rsqrt(jnp.mean(pre * pre, axis=-1, keepdims=True) + NORM_EPS)


def attend_forward_kernel(
    pre_qk, pre_v, q_gain, k_gain, cosine, sine, segment_rows, segment_columns, rotated, mixed, inverse, keys
):
    offsets = block_offsets()
    cos, sin = cosine[...], sine[...]
    for head in range(6):
        lanes = slice(128 * head, 128 * (head + 1))
        value = pre_qk[:, lanes]
        gain = q_gain[...] if head < 4 else k_gain[...]
        normed = value * head_norm(value) * gain
        turned = normed * cos + pltpu.roll(normed, 64, 1) * sin
        rotated[:, lanes] = turned.astype(jnp.bfloat16)
    rotated[:, 768:] = pre_v[...].astype(jnp.bfloat16)
    for block in range(4):
        keys[128 * block : 128 * (block + 1), :] = rotated[pl.ds(offsets[block], 128), 512:]
    lane = lax.broadcasted_iota(jnp.int32, (128, 128), 1)
    for block in range(4):
        count = 128 * (block + 1)
        allowed = block_mask(block, segment_rows, segment_columns)
        allowed = jnp.concatenate([allowed, allowed], axis=0)
        rows = pl.ds(offsets[block], 128)
        totals = jnp.zeros((128, 128), jnp.float32)
        for group in range(2):
            query = jnp.concatenate(
                [rotated[rows, 256 * group : 256 * group + 128], rotated[rows, 256 * group + 128 : 256 * group + 256]],
                axis=0,
            )
            key = keys[:count, 128 * group : 128 * (group + 1)]
            value = keys[:count, 256 + 128 * group : 256 + 128 * (group + 1)]
            score = lax.dot_general(query, key, NT, preferred_element_type=jnp.float32)
            weight = jnp.exp2(score * (SCALE * LOG2E)) * allowed
            inverse_total = 1.0 / jnp.sum(weight, axis=-1, keepdims=True)
            out = lax.dot_general((weight * inverse_total).astype(jnp.bfloat16), value, NN, preferred_element_type=jnp.float32)
            out = out.astype(jnp.bfloat16)
            mixed[rows, 256 * group : 256 * group + 128] = out[:128]
            mixed[rows, 256 * group + 128 : 256 * group + 256] = out[128:]
            totals = jnp.where(lane == 2 * group, inverse_total[:128], totals)
            totals = jnp.where(lane == 2 * group + 1, inverse_total[128:], totals)
        inverse[rows, :] = totals


def attend_forward(pre_qk, pre_v, q_gain, k_gain, cosine, sine, segment_rows, segment_columns):
    return pl.pallas_call(
        attend_forward_kernel,
        out_shape=(
            jax.ShapeDtypeStruct((512, 1024), jnp.bfloat16),
            jax.ShapeDtypeStruct((512, 512), jnp.bfloat16),
            jax.ShapeDtypeStruct((512, 128), jnp.float32),
        ),
        scratch_shapes=[pltpu.VMEM((512, 512), jnp.bfloat16)],
        compiler_params=pltpu.CompilerParams(vmem_limit_bytes=14 * 1024 * 1024),
        cost_estimate=pl.CostEstimate(flops=700_000_000, bytes_accessed=6_000_000, transcendentals=700_000),
        name="attend_forward",
    )(pre_qk, pre_v, q_gain, k_gain, cosine, sine, segment_rows, segment_columns)


def attend_backward_kernel(
    pre_qk, rotated, mixed, inverse, grad_mixed, clock, q_gain, k_gain, cosine, sine, segment_rows, segment_columns,
    grad_qk, grad_v, gain_grads, keys, grad_rotated, grad_keys,
):
    offsets = block_offsets()
    for block in range(4):
        keys[128 * block : 128 * (block + 1), :] = rotated[pl.ds(offsets[block], 128), 512:]
    for block in range(3, -1, -1):
        count = 128 * (block + 1)
        allowed = block_mask(block, segment_rows, segment_columns)
        allowed = jnp.concatenate([allowed, allowed], axis=0)
        rows = pl.ds(offsets[block], 128)
        inverse_block = inverse[rows, :]
        for group in range(2):
            def pair(ref):
                return jnp.concatenate(
                    [ref[rows, 256 * group : 256 * group + 128], ref[rows, 256 * group + 128 : 256 * group + 256]],
                    axis=0,
                )
            query, grad_out = pair(rotated), pair(grad_mixed)
            inner = jnp.sum(grad_out.astype(jnp.float32) * pair(mixed).astype(jnp.float32), axis=-1, keepdims=True)
            key = keys[:count, 128 * group : 128 * (group + 1)]
            value = keys[:count, 256 + 128 * group : 256 + 128 * (group + 1)]
            inverse_total = jnp.concatenate(
                [inverse_block[:, 2 * group : 2 * group + 1], inverse_block[:, 2 * group + 1 : 2 * group + 2]], axis=0
            )
            score = lax.dot_general(query, key, NT, preferred_element_type=jnp.float32)
            weight = jnp.exp2(score * (SCALE * LOG2E)) * allowed * inverse_total
            grad_weight = lax.dot_general(grad_out, value, NT, preferred_element_type=jnp.float32)
            grad_score = (weight * (grad_weight - inner)).astype(jnp.bfloat16)
            low = weight.astype(jnp.bfloat16)
            grad_value = lax.dot_general(low, grad_out, TN, preferred_element_type=jnp.float32)
            grad_key = lax.dot_general(grad_score, query, TN, preferred_element_type=jnp.float32)
            grad_query = lax.dot_general(grad_score, key, NN, preferred_element_type=jnp.float32)
            grad_rotated[rows, 256 * group : 256 * group + 128] = grad_query[:128] * SCALE
            grad_rotated[rows, 256 * group + 128 : 256 * group + 256] = grad_query[128:] * SCALE
            spot, value_spot = slice(128 * group, 128 * (group + 1)), slice(256 + 128 * group, 256 + 128 * (group + 1))
            if block == 3:
                grad_keys[:, spot] = grad_key * SCALE
                grad_keys[:, value_spot] = grad_value
            else:
                grad_keys[:count, spot] += grad_key * SCALE
                grad_keys[:count, value_spot] += grad_value
    for block in range(4):
        grad_rotated[pl.ds(offsets[block], 128), 512:] = grad_keys[128 * block : 128 * (block + 1), :]
    cos, sin = cosine[...], sine[...]
    gain_sums = []
    for head in range(6):
        lanes = slice(128 * head, 128 * (head + 1))
        value = pre_qk[:, lanes]
        gain = q_gain[...] if head < 4 else k_gain[...]
        scale = head_norm(value)
        unit = value * scale
        turned = grad_rotated[:, lanes]
        grad = turned * cos + pltpu.roll(turned * sin, 64, 1)
        gain_sums.append(jnp.sum(grad * unit, axis=0, keepdims=True))
        grad = grad * gain
        grad = scale * (grad - unit * jnp.mean(grad * unit, axis=-1, keepdims=True))
        grad_qk[:, lanes] = grad.astype(jnp.bfloat16)
    grad_v[...] = grad_rotated[:, 768:].astype(jnp.bfloat16)
    gain_grads[0:1, :] = gain_sums[0] + gain_sums[1] + gain_sums[2] + gain_sums[3]
    gain_grads[1:2, :] = gain_sums[4] + gain_sums[5]
    gain_grads[2:8, :] = jnp.zeros((6, 128), jnp.float32)


def attend_backward(pre_qk, rotated, mixed, inverse, grad_mixed, clock, q_gain, k_gain, cosine, sine, segment_rows, segment_columns):
    return pl.pallas_call(
        attend_backward_kernel,
        out_shape=(
            jax.ShapeDtypeStruct((512, 768), jnp.bfloat16),
            jax.ShapeDtypeStruct((512, 256), jnp.bfloat16),
            jax.ShapeDtypeStruct((8, 128), jnp.float32),
        ),
        scratch_shapes=[
            pltpu.VMEM((512, 512), jnp.bfloat16),
            pltpu.VMEM((512, 1024), jnp.float32),
            pltpu.VMEM((512, 512), jnp.float32),
        ],
        compiler_params=pltpu.CompilerParams(vmem_limit_bytes=18 * 1024 * 1024),
        cost_estimate=pl.CostEstimate(flops=1_700_000_000, bytes_accessed=8_000_000, transcendentals=700_000),
        name="attend_backward",
    )(pre_qk, rotated, mixed, inverse, grad_mixed, clock, q_gain, k_gain, cosine, sine, segment_rows, segment_columns)


def core_pairs():
    return [(index, index ^ 1) for index in range(4)]


def chip_pairs():
    return [(index, index ^ 2) for index in range(4)]


def dp_shift(stage, step):
    pairs = []
    for z in range(4):
        for x in range(2):
            for y in range(4):
                target = {
                    "y": (z, x, (y + step) % 4),
                    "x": (z, (x + step) % 2, y),
                    "z": ((z + step) % 4, x, y),
                }[stage]
                pairs.append((z * 8 + x * 4 + y, target[0] * 8 + target[1] * 4 + target[2]))
    return pairs


def dp_place():
    index = lax.axis_index("dp")
    return {"z": index // 8, "x": index // 4 % 2, "y": index % 4}


def column_ranges(widths):
    starts = [sum(widths[:index]) for index in range(len(widths))]
    return [pl.ds(start, width) for start, width in zip(starts, widths)]


def ring_gather(block, stage):
    return [(block, 0, None)] + [
        (lax.ppermute(block, "dp", dp_shift(stage, step)), step, None) for step in (1, 2, 3)
    ]


def hold_blocks(blocks, *others):
    arrays = after([block for block, _, _ in blocks], *others)
    return [(array, step, half) for array, (_, step, half) in zip(arrays, blocks)]


def near_gather(block, stage):
    return [(block, 0, None)] + [
        (lax.ppermute(block, "dp", dp_shift(stage, step)), step, None) for step in (1, 3)
    ]


def far_gather(block, stage):
    return [(lax.ppermute(block, "dp", dp_shift(stage, 2)), 2, None)]


def two_step_near(block, stage):
    return (
        block,
        lax.ppermute(block, "dp", dp_shift(stage, 1)),
        lax.ppermute(block, "dp", dp_shift(stage, 3)),
    )


def two_step_far(near, stage):
    block, below, above = near
    half = block.shape[0] // 2
    far_low = lax.ppermute(below[:half], "dp", dp_shift(stage, 1))
    far_high = lax.ppermute(above[half:], "dp", dp_shift(stage, 3))
    return [(block, 0, None), (below, 1, None), (above, 3, None), (far_low, 2, 0), (far_high, 2, 1)]


def place_blocks(blocks, stage, shape, axis, widths):
    places = [(step, half) for _, step, half in blocks]

    def kernel(*refs):
        sources, targets, semaphores = refs[: len(places)], refs[len(places) : -1], refs[-1]
        index = lax.axis_index("dp")
        mine = index // 8 if stage == "z" else index % 4
        copies = []
        for order, (source, (step, half)) in enumerate(zip(sources, places)):
            spot = lax.rem(mine - step + 4, 4)
            rows = source.shape[0]
            rows = pl.ds(0 if half is None else half * rows, rows)
            for number, columns in enumerate(column_ranges(widths)):
                whole = targets[number]
                target = whole.at[spot, rows] if axis == 0 else whole.at[rows, spot]
                copies.append(
                    pltpu.make_async_copy(
                        source.at[..., columns], target, semaphores.at[order, number]
                    )
                )
        for copy in copies:
            copy.start()
        for copy in copies:
            copy.wait()

    arrays = [block for block, _, _ in blocks]
    return pl.pallas_call(
        kernel,
        out_shape=[jax.ShapeDtypeStruct((*shape, width), arrays[0].dtype) for width in widths],
        in_specs=[pl.BlockSpec(memory_space=pl.ANY)] * len(arrays),
        out_specs=[pl.BlockSpec(memory_space=pltpu.VMEM)] * len(widths),
        scratch_shapes=[pltpu.SemaphoreType.DMA((len(arrays), len(widths)))],
        compiler_params=pltpu.CompilerParams(vmem_limit_bytes=8 * 1024 * 1024),
        cost_estimate=pl.CostEstimate(
            flops=0, bytes_accessed=4 * math.prod(shape) * sum(widths), transcendentals=0
        ),
        name="place_blocks",
    )(*arrays)


def pack(pieces):
    pieces = [piece if isinstance(piece, tuple) else (piece, None) for piece in pieces]
    widths = [array.shape[-1] for array, _ in pieces]

    def kernel(*refs):
        sources, whole, semaphores = refs[:-2], refs[-2], refs[-1]
        copies = []
        for number, columns in enumerate(column_ranges(widths)):
            layer = pieces[number][1]
            source = sources[number] if layer is None else sources[number].at[layer]
            copies.append(
                pltpu.make_async_copy(source, whole.at[:, columns], semaphores.at[number])
            )
        for copy in copies:
            copy.start()
        for copy in copies:
            copy.wait()

    return pl.pallas_call(
        kernel,
        out_shape=jax.ShapeDtypeStruct((32, sum(widths)), pieces[0][0].dtype),
        in_specs=[pl.BlockSpec(memory_space=pl.ANY)] * len(pieces),
        out_specs=pl.BlockSpec(memory_space=pltpu.VMEM),
        scratch_shapes=[pltpu.SemaphoreType.DMA((len(pieces),))],
        compiler_params=pltpu.CompilerParams(vmem_limit_bytes=2 * 1024 * 1024),
        cost_estimate=pl.CostEstimate(
            flops=0, bytes_accessed=128 * sum(widths), transcendentals=0
        ),
        name="pack",
    )(*[array for array, _ in pieces])


def split_blocks(parts, stage, axis):
    widths = [part.shape[-1] for part in parts]
    lead = parts[0].shape[:-1]
    shape = (*lead[:axis], *lead[axis + 1 :], sum(widths))

    def kernel(*refs):
        sources, blocks, semaphores = refs[: len(parts)], refs[len(parts) : -1], refs[-1]
        index = lax.axis_index("dp")
        mine = index // 8 if stage == "z" else index % 4
        copies = []
        for step, block in enumerate(blocks):
            spot = lax.rem(mine + step, 4)
            for number, columns in enumerate(column_ranges(widths)):
                source = sources[number]
                piece = source.at[spot] if axis == 0 else source.at[:, spot]
                copies.append(
                    pltpu.make_async_copy(
                        piece, block.at[..., columns], semaphores.at[step, number]
                    )
                )
        for copy in copies:
            copy.start()
        for copy in copies:
            copy.wait()

    return pl.pallas_call(
        kernel,
        out_shape=[jax.ShapeDtypeStruct(shape, parts[0].dtype)] * 4,
        in_specs=[pl.BlockSpec(memory_space=pltpu.VMEM)] * len(parts),
        out_specs=[pl.BlockSpec(memory_space=pl.ANY)] * 4,
        scratch_shapes=[pltpu.SemaphoreType.DMA((4, len(parts)))],
        compiler_params=pltpu.CompilerParams(vmem_limit_bytes=8 * 1024 * 1024),
        cost_estimate=pl.CostEstimate(
            flops=0, bytes_accessed=16 * math.prod(shape), transcendentals=0
        ),
        name="split_blocks",
    )(*parts)


def join_x(block, other):
    return jnp.where(
        dp_place()["x"] == 0, jnp.stack([block, other]), jnp.stack([other, block])
    )


def gather_x(block, *side_work):
    return join_x(block, after(lax.ppermute(block, "dp", dp_shift("x", 1)), *side_work))


def place_first(blocks, stage, widths):
    if stage == "y":
        wholes = place_blocks(blocks, "y", (2, 4, 32), 1, widths)
    else:
        wholes = place_blocks(blocks, "z", (4, 2, 32), 0, widths)
    return [whole.reshape(256, width) for whole, width in zip(wholes, widths)]


def place_last(blocks, stage, widths):
    if stage == "z":
        wholes = place_blocks(blocks, "z", (4, 256), 0, widths)
    else:
        blocks = [
            (block.reshape(-1, 32, sum(widths)), step, half) for block, step, half in blocks
        ]
        wholes = place_blocks(blocks, "y", (8, 4, 32), 1, widths)
    return [whole.reshape(1024, width) for whole, width in zip(wholes, widths)]


def send_near(blocks, stage):
    return [
        blocks[0],
        lax.ppermute(blocks[1], "dp", dp_shift(stage, 1)),
        lax.ppermute(blocks[3], "dp", dp_shift(stage, 3)),
    ]


def send_far(blocks, stage, *others):
    return lax.ppermute(after(blocks[2], *others), "dp", dp_shift(stage, 2))


def near_sum(near):
    return sum(block.astype(jnp.float32) for block in near).astype(jnp.bfloat16)


def far_sum(near, far):
    return (near.astype(jnp.float32) + far.astype(jnp.float32)).astype(jnp.bfloat16)


def split_first(parts, stage):
    if stage == "z":
        blocks = split_blocks([part.reshape(4, 256, -1) for part in parts], "z", 0)
    else:
        blocks = split_blocks([part.reshape(8, 4, 32, -1) for part in parts], "y", 1)
    return blocks


def x_parts(part, first_stage):
    width = part.shape[-1]
    if first_stage == "z":
        low, high = part[:128], part[128:]
    else:
        blocks = part.reshape(4, 2, 32, width)
        low, high = blocks[:, 0].reshape(128, width), blocks[:, 1].reshape(128, width)
    place = dp_place()["x"]
    return jnp.where(place == 0, low, high), jnp.where(place == 0, high, low)


def send_x(part, first_stage):
    return lax.ppermute(x_parts(part, first_stage)[1], "dp", dp_shift("x", 1))


def add_x(part, other, first_stage):
    kept = x_parts(part, first_stage)[0].astype(jnp.float32)
    return (kept + other.astype(jnp.float32)).astype(jnp.bfloat16)


def send_last(parts, stage):
    blocks = jnp.concatenate(parts, axis=1).reshape(4, 32, -1)
    mine = dp_place()[stage]
    return [lax.dynamic_index_in_dim(blocks, mine, 0, False)] + [
        lax.ppermute(
            lax.dynamic_index_in_dim(blocks, (mine + step) % 4, 0, False),
            "dp",
            dp_shift(stage, step),
        )
        for step in (1, 2, 3)
    ]


def sum_last(sent):
    return sum(block.astype(jnp.float32) for block in sent)


def after(values, *others):
    return lax.optimization_barrier((values, others))[0]


def rms_scale(values, gain):
    return (
        values
        * lax.rsqrt(jnp.mean(values * values, axis=-1, keepdims=True) + NORM_EPS)
        * gain
    )


def rms_backward(values, gain, grad):
    scale = lax.rsqrt(jnp.mean(values * values, axis=-1, keepdims=True) + NORM_EPS)
    unit = values * scale
    scaled = grad * gain
    grad_values = scale * (scaled - unit * jnp.mean(scaled * unit, axis=-1, keepdims=True))
    return grad_values, jnp.sum(grad * unit, axis=0)


def dot(left, right):
    return jnp.dot(left, right, preferred_element_type=jnp.float32)


def dot_nt(left, right):
    return lax.dot_general(left, right, NT, preferred_element_type=jnp.float32)


def dot_tn(left, right):
    return lax.dot_general(left, right, TN, preferred_element_type=jnp.float32).astype(
        jnp.bfloat16
    )


def own_block(rows):
    chip = lax.axis_index("tensor") // 2
    blocks = rows.reshape(2, 128, rows.shape[-1])
    return jnp.where(chip == 0, blocks[0], blocks[1])


def both_blocks(block):
    chip = lax.axis_index("tensor") // 2
    other = lax.ppermute(block, "tensor", chip_pairs())
    return jnp.where(
        chip == 0, jnp.concatenate([block, other]), jnp.concatenate([other, block])
    )


def stand_in(*operands):
    def kernel(*refs):
        refs[-1][...] = jnp.zeros_like(refs[-1])

    return pl.pallas_call(
        kernel,
        out_shape=jax.ShapeDtypeStruct((8, 128), jnp.float32),
        in_specs=[pl.BlockSpec(memory_space=pl.ANY)] * len(operands),
        out_specs=pl.BlockSpec(memory_space=pltpu.VMEM),
        compiler_params=pltpu.CompilerParams(vmem_limit_bytes=64 * 1024),
        cost_estimate=pl.CostEstimate(flops=10**11, bytes_accessed=0, transcendentals=0),
        name="stand_in",
    )(*operands)


def wait_for(clock, values):
    clock[0] = stand_in(after(clock[0], values))
    return clock[0]


def exchange(rows, pairs, clock, *side_work):
    other = lax.ppermute(rows, "tensor", pairs)
    if clock is not None:
        side_work = (*side_work, wait_for(clock, rows))
    return after(other, *side_work) if side_work else other


def with_sibling(rows, clock):
    return jnp.concatenate([rows, exchange(rows, core_pairs(), clock)])


def sum_cores(term, clock):
    away = exchange(term(1).astype(jnp.bfloat16), core_pairs(), clock)
    return (term(0) + away.astype(jnp.float32)).astype(jnp.bfloat16)


def sum_chips(part, clock, *side_work):
    other = exchange(part, chip_pairs(), clock, *side_work)
    return part.astype(jnp.float32) + other.astype(jnp.float32)


def sum_own_block(part):
    chip = lax.axis_index("tensor") // 2
    part = part.reshape(2, 128, -1)
    keep = jnp.where(chip == 0, part[0], part[1])
    send = jnp.where(chip == 0, part[1], part[0])
    other = lax.ppermute(send, "tensor", chip_pairs())
    return keep.astype(jnp.float32) + other.astype(jnp.float32)


def halves(array):
    return (array[:256], array[256:])


def rotary_tables(segment_ids):
    width = segment_ids.shape[0]
    core = lax.axis_index("tensor") % 2
    column = jnp.arange(width, dtype=jnp.int32)
    doc_starts = jnp.zeros((width,), jnp.int32)
    for doc_number in range(4):
        before = jnp.sum((segment_ids < doc_number).astype(jnp.int32))
        doc_starts = doc_starts + jnp.where(segment_ids == doc_number, before, 0)
    blocks = (column - doc_starts).astype(jnp.float32).reshape(2, 2, 128)
    position = jnp.where(
        core == 0,
        jnp.concatenate([blocks[:, 0], blocks[:, 1]]),
        jnp.concatenate([blocks[:, 1], blocks[:, 0]]),
    ).reshape(width)
    frequency = jnp.exp(
        jnp.arange(HEAD // 2, dtype=jnp.float32) * (-2.0 * math.log(ROPE_BASE) / HEAD)
    )
    angles = position[:, None] * frequency[None, :]
    cosine, sine = jnp.cos(angles), jnp.sin(angles)
    return (
        jnp.concatenate([cosine, cosine], axis=-1),
        jnp.concatenate([-sine, sine], axis=-1),
    )


def send_direct(blocks):
    return lax.all_to_all(blocks, "dp", 0, 0, tiled=True)


def sum_sent(sent):
    return jnp.sum(sent.reshape(32, 32, -1).astype(jnp.float32), axis=0)


def body(
    tokens,
    segment_ids,
    cotangent,
    attn_norm,
    q_weight,
    key_projection,
    value_projection,
    o_weight,
    q_gain,
    k_gain,
    mlp_norm,
    gate_weight,
    up_weight,
    down_weight,
):
    attend = gather_x(
        pack([(q_weight, 0), (key_projection, 0), (value_projection, 0), o_weight[0].T])
    )
    tokens, transposed = after(
        (tokens, [down_weight[0].T, o_weight[1].T, down_weight[1].T]), attend
    )
    token_blocks = both_blocks(tokens)
    qk_part = place_first(ring_gather(attend[..., :768], "y"), "y", [768])[0]
    vo_part = place_first(ring_gather(attend[..., 768:], "z"), "z", [768])[0]
    qk_blocks, vo_blocks = ring_gather(qk_part, "z"), ring_gather(vo_part, "y")
    rest = pack(
        [
            transposed[0],
            (q_weight, 1),
            (key_projection, 1),
            (value_projection, 1),
            transposed[1],
            transposed[2],
            (gate_weight, 0),
            (up_weight, 0),
            (gate_weight, 1),
            (up_weight, 1),
        ]
    )
    segment_ids = after(segment_ids, qk_part, vo_part)
    cosine, sine = rotary_tables(segment_ids)
    segment_rows, segment_columns = segment_ids[:, None], segment_ids[None, :]
    residual = token_blocks.astype(jnp.float32)
    first_normed = rms_scale(residual, attn_norm[0]).astype(jnp.bfloat16)
    rest = gather_x(rest, first_normed)
    (wqk,) = place_last(qk_blocks, "z", [768])
    wv, wo = place_last(vo_blocks, "y", [256, 512])
    y_blocks = ring_gather(rest[..., :3072], "y")
    z_blocks = near_gather(rest[..., 3072:], "z")
    grad_rows = both_blocks(after(cotangent, wqk)).astype(jnp.float32)
    clock = [jnp.zeros((8, 128), jnp.float32)]
    saved_layers = []
    attend_weights, feed_weights = [(wqk, wv, wo), None], [None, None]
    for layer in range(2):
        wqk, wv, wo = attend_weights[layer]
        gains = (q_gain[layer][None], k_gain[layer][None])
        if layer == 1:
            first_normed = rms_scale(residual, attn_norm[1]).astype(jnp.bfloat16)
        normed = with_sibling(first_normed, clock)
        pre_qk, pre_v = dot(normed, wqk), dot(normed, wv)
        rotated, mixed, inverse = attend_forward(
            pre_qk, pre_v, *gains, cosine, sine, segment_rows, segment_columns
        )
        mixed_halves = halves(mixed)
        part = sum_cores(lambda side: dot_nt(mixed_halves[side], wo), clock)
        side_work = []
        if layer == 0:
            z_blocks += far_gather(after(z_blocks[0][0], mixed), "z")
            y_blocks, z_blocks = hold_blocks(y_blocks, mixed), hold_blocks(z_blocks, mixed)
            down_attend_part, next_down_part = place_first(y_blocks, "y", [2304, 768])
            gate_up_part, next_gate_up_part = place_first(z_blocks, "z", [1536, 1536])
            gate_up_near = two_step_near(gate_up_part, "y")
            down_attend_near = two_step_near(down_attend_part, "z")
        middle = residual + sum_chips(part, clock, *side_work)
        normed_two = with_sibling(
            rms_scale(middle, mlp_norm[layer]).astype(jnp.bfloat16), clock
        )
        if layer == 0:
            wg, wu = place_last(two_step_far(gate_up_near, "y"), "y", [768, 768])
        else:
            wg, wu = place_last(two_step_far(next_gate_up_near, "y"), "y", [768, 768])
            (wd,) = place_last(two_step_far(next_down_near, "z"), "z", [768])
        gate, up = dot(normed_two, wg), dot(normed_two, wu)
        product = (jax.nn.silu(gate) * up).astype(jnp.bfloat16)
        if layer == 0:
            wd, wqk, wv, wo = place_last(
                two_step_far(down_attend_near, "z"), "z", [768, 768, 256, 512]
            )
            attend_weights[1] = (wqk, wv, wo)
        feed_weights[layer] = (wg, wu, wd)
        product_halves = halves(product)
        saved_layers.append(
            (residual, middle, normed, normed_two, pre_qk, rotated, mixed, inverse, gate, up, product)
        )
        part = sum_cores(
            lambda side: dot_nt(product_halves[side], wd), clock if layer == 0 else None
        )
        if layer == 0:
            next_gate_up_part, next_down_part = after((next_gate_up_part, next_down_part), part)
            next_gate_up_near = two_step_near(next_gate_up_part, "y")
            next_down_near = two_step_near(next_down_part, "z")
            residual = middle + sum_chips(part, clock)
        else:
            output = own_block(middle) + sum_own_block(part)
    output = output.astype(jnp.bfloat16)
    gain_grads = [None, None]
    for layer in (1, 0):
        wqk, wv, wo = attend_weights[layer]
        wg, wu, wd = feed_weights[layer]
        gains = (q_gain[layer][None], k_gain[layer][None])
        residual, middle, normed, normed_two, pre_qk, rotated, mixed, inverse, gate, up, product = (
            saved_layers[layer]
        )
        grad_out = with_sibling(grad_rows.astype(jnp.bfloat16), clock)
        grad_product = dot(grad_out, wd)
        sigmoid = jax.nn.sigmoid(gate)
        grad_gate = grad_product * up * sigmoid * (1.0 + gate * (1.0 - sigmoid))
        grad_gate = grad_gate.astype(jnp.bfloat16)
        grad_up = (grad_product * gate * sigmoid).astype(jnp.bfloat16)
        gate_halves, up_halves = halves(grad_gate), halves(grad_up)
        part = sum_cores(
            lambda side: dot_nt(gate_halves[side], wg) + dot_nt(up_halves[side], wu), clock
        )
        down_grad = dot_tn(after(grad_out, part), product)
        normed_later = after(normed_two, part)
        gate_grad, up_grad = dot_tn(normed_later, grad_gate), dot_tn(normed_later, grad_up)
        if layer == 1:
            feed_blocks = split_first([gate_grad, up_grad, down_grad], "y")
            feed_near = send_near(feed_blocks, "y")
            side_work = feed_blocks
        else:
            gate_up_blocks = split_first([gate_grad, up_grad], "y")
            gate_up_near = send_near(gate_up_blocks, "y")
            feed_sum = far_sum(feed_near, after(feed_far, part))
            attend_sum = far_sum(near_sum(after(attend_near, part)), after(attend_far, part))
            side_work = [*gate_up_blocks, down_grad, feed_sum, attend_sum]
        grad_normed_two = sum_chips(part, clock, *side_work)
        grad_middle, mlp_gain_grad = rms_backward(middle, mlp_norm[layer], grad_normed_two)
        grad_middle = grad_rows + grad_middle
        grad_branch = with_sibling(grad_middle.astype(jnp.bfloat16), clock)
        grad_mixed = dot(grad_branch, wo).astype(jnp.bfloat16)
        o_grad = dot_tn(grad_branch, mixed)
        if layer == 0:
            down_blocks = split_first([o_grad, down_grad], "z")
            down_near = send_near(down_blocks, "z")
            grad_mixed = after(grad_mixed, *down_blocks)
        grad_qk, grad_v, gain_grad = attend_backward(
            pre_qk,
            rotated,
            mixed,
            inverse,
            grad_mixed,
            clock[0],
            *gains,
            cosine,
            sine,
            segment_rows,
            segment_columns,
        )
        qk_halves, v_halves = halves(grad_qk), halves(grad_v)
        terms = [dot_nt(qk_halves[side], wqk) + dot_nt(v_halves[side], wv) for side in range(2)]
        part = sum_cores(lambda side: terms[side], clock if layer == 1 else None)
        normed_later = after(normed, part)
        qk_grad, v_grad = dot_tn(normed_later, grad_qk), dot_tn(normed_later, grad_v)
        if layer == 1:
            attend_blocks = split_first([qk_grad, v_grad, o_grad], "z")
            attend_near = send_near(attend_blocks, "z")
            attend_far = send_far(attend_blocks, "z", part)
            feed_near = near_sum(after(feed_near, part))
            feed_far = send_far(feed_blocks, "y", part)
            grad_in, attn_gain_grad = rms_backward(
                residual, attn_norm[1], sum_chips(part, clock, *attend_blocks, feed_near)
            )
            attn_gain_grad = 0.5 * attn_gain_grad
            grad_rows = grad_middle + grad_in
        else:
            normed_halves = halves(normed)
            attn_gain_grad = sum(
                jnp.sum(terms[side] * normed_halves[side].astype(jnp.float32), axis=0)
                for side in range(2)
            )
            attn_gain_grad = attn_gain_grad / attn_norm[0]
        gain_grads[layer] = (attn_gain_grad, gain_grad[0], gain_grad[1], 0.5 * mlp_gain_grad)
    gain_block = jnp.concatenate([*gain_grads[0], *gain_grads[1]]).reshape(36, 128)
    gain_block = jnp.pad(gain_block, ((0, 28), (0, 0))).reshape(32, 256).astype(jnp.bfloat16)
    last = jnp.concatenate([qk_grad, v_grad, jnp.tile(gain_block, (32, 1))], axis=1)
    feed_other = send_x(after(feed_sum, grad_qk), "y")
    gate_up_near = near_sum(after(gate_up_near, grad_qk))
    gate_up_far = send_far(gate_up_blocks, "y", grad_qk)
    down_far = send_far(down_blocks, "z", grad_qk)
    last = after(last, gate_up_near)
    last_sent = send_direct(last)
    mark = stand_in(clock[0], last)
    grad_in, _ = rms_backward(own_block(residual), attn_norm[0], sum_own_block(part))
    input_grad = own_block(grad_middle) + grad_in
    feed_other = after(feed_other, mark)
    attend_other = send_x(after(attend_sum, mark), "z")
    gate_up_sum = far_sum(gate_up_near, after(gate_up_far, mark))
    down_sum = far_sum(near_sum(after(down_near, mark)), after(down_far, mark))
    gate_up_other, down_other = send_x(gate_up_sum, "y"), send_x(down_sum, "z")
    last = sum_sent(last_sent)
    gain_sums = last[:, 1024:].reshape(64, 128)[:36]
    gain_sums = gain_sums + lax.ppermute(gain_sums, "tensor", core_pairs())
    gain_sums = gain_sums + lax.ppermute(gain_sums, "tensor", chip_pairs())
    gate_up_other, down_other = after((gate_up_other, down_other), gain_sums)
    feed_sent = send_last(
        [add_x(gate_up_sum, gate_up_other, "y"), add_x(feed_sum, feed_other, "y")], "z"
    )
    attend_sent = send_last(
        [add_x(down_sum, down_other, "z"), add_x(attend_sum, attend_other, "z")], "y"
    )
    feed_sent, attend_sent = after(feed_sent, attend_sent[0]), after(attend_sent, feed_sent[0])
    feed_own, attend_own = sum_last(feed_sent), sum_last(attend_sent)
    gain_sums = gain_sums.reshape(2, 2304)
    first_gate, first_up, gate, up, down = jnp.split(feed_own, 5, axis=1)
    first_o, first_down, qk, v, o = jnp.split(attend_own, [512, 1280, 2048, 2304], axis=1)
    return (
        output,
        input_grad,
        gain_sums[:, :1024],
        jnp.stack([last[:, :512], qk[:, :512]]),
        jnp.stack([last[:, 512:768], qk[:, 512:]]),
        jnp.stack([last[:, 768:1024], v]),
        jnp.stack([first_o.T, o.T]),
        gain_sums[:, 1024:1152],
        gain_sums[:, 1152:1280],
        gain_sums[:, 1280:],
        jnp.stack([first_gate, gate]),
        jnp.stack([first_up, up]),
        jnp.stack([first_down.T, down.T]),
    )


def solution(mesh):
    rows = P(("dp", "tensor"), None)
    in_rows, in_columns = P(None, "dp", "tensor"), P(None, "tensor", "dp")
    return jax.shard_map(
        body,
        mesh=mesh,
        in_specs=(
            rows,
            P("dp"),
            rows,
            P(),
            in_rows,
            in_rows,
            in_rows,
            in_columns,
            P(),
            P(),
            P(),
            in_rows,
            in_rows,
            in_columns,
        ),
        out_specs=(
            rows,
            rows,
            P(),
            in_rows,
            in_rows,
            in_rows,
            in_columns,
            P(),
            P(),
            P(),
            in_rows,
            in_rows,
            in_columns,
        ),
        check_vma=False,
    )
```

```python
import math

import jax
import jax.numpy as jnp
from jax import lax
from jax.experimental import pallas as pl
from jax.experimental.pallas import tpu as pltpu
from jax.sharding import PartitionSpec as P

ROPE_BASE = 1000000.0
HEAD = 128
SCALE = 128 ** -0.5
LOG2E = 1.0 / math.log(2.0)
NORM_EPS = 1e-6
NT = (((1,), (1,)), ((), ()))
TN = (((0,), (0,)), ((), ()))
NN = (((1,), (0,)), ((), ()))


def block_offsets():
    core = lax.axis_index("tensor") % 2
    return [
        pl.multiple_of(128 * (block // 2 + 2 * ((block + core) % 2)), 128) for block in range(4)
    ]


def block_mask(block, segment_rows, segment_columns):
    keys = 128 * (block + 1)
    row = lax.broadcasted_iota(jnp.int32, (128, keys), 0) + 128 * block
    column = lax.broadcasted_iota(jnp.int32, (128, keys), 1)
    query_segment = segment_rows[128 * block : 128 * (block + 1), :]
    same = query_segment == segment_columns[:, :keys]
    allowed = same & (column <= row) & (query_segment < 3) | (column == row)
    return allowed.astype(jnp.float32)


def head_norm(pre):
    return lax.rsqrt(jnp.mean(pre * pre, axis=-1, keepdims=True) + NORM_EPS)


def attend_forward_kernel(
    pre_qk, pre_v, q_gain, k_gain, cosine, sine, segment_rows, segment_columns, rotated, mixed, inverse, keys
):
    offsets = block_offsets()
    cos, sin = cosine[...], sine[...]
    for head in range(6):
        lanes = slice(128 * head, 128 * (head + 1))
        value = pre_qk[:, lanes]
        gain = q_gain[...] if head < 4 else k_gain[...]
        normed = value * head_norm(value) * gain
        turned = normed * cos + pltpu.roll(normed, 64, 1) * sin
        rotated[:, lanes] = turned.astype(jnp.bfloat16)
    rotated[:, 768:] = pre_v[...].astype(jnp.bfloat16)
    for block in range(4):
        keys[128 * block : 128 * (block + 1), :] = rotated[pl.ds(offsets[block], 128), 512:]
    lane = lax.broadcasted_iota(jnp.int32, (128, 128), 1)
    for block in range(4):
        count = 128 * (block + 1)
        allowed = block_mask(block, segment_rows, segment_columns)
        allowed = jnp.concatenate([allowed, allowed], axis=0)
        rows = pl.ds(offsets[block], 128)
        totals = jnp.zeros((128, 128), jnp.float32)
        for group in range(2):
            query = jnp.concatenate(
                [rotated[rows, 256 * group : 256 * group + 128], rotated[rows, 256 * group + 128 : 256 * group + 256]],
                axis=0,
            )
            key = keys[:count, 128 * group : 128 * (group + 1)]
            value = keys[:count, 256 + 128 * group : 256 + 128 * (group + 1)]
            score = lax.dot_general(query, key, NT, preferred_element_type=jnp.float32)
            weight = jnp.exp2(score * (SCALE * LOG2E)) * allowed
            inverse_total = 1.0 / jnp.sum(weight, axis=-1, keepdims=True)
            out = lax.dot_general((weight * inverse_total).astype(jnp.bfloat16), value, NN, preferred_element_type=jnp.float32)
            out = out.astype(jnp.bfloat16)
            mixed[rows, 256 * group : 256 * group + 128] = out[:128]
            mixed[rows, 256 * group + 128 : 256 * group + 256] = out[128:]
            totals = jnp.where(lane == 2 * group, inverse_total[:128], totals)
            totals = jnp.where(lane == 2 * group + 1, inverse_total[128:], totals)
        inverse[rows, :] = totals


def attend_forward(pre_qk, pre_v, q_gain, k_gain, cosine, sine, segment_rows, segment_columns):
    return pl.pallas_call(
        attend_forward_kernel,
        out_shape=(
            jax.ShapeDtypeStruct((512, 1024), jnp.bfloat16),
            jax.ShapeDtypeStruct((512, 512), jnp.bfloat16),
            jax.ShapeDtypeStruct((512, 128), jnp.float32),
        ),
        scratch_shapes=[pltpu.VMEM((512, 512), jnp.bfloat16)],
        compiler_params=pltpu.CompilerParams(vmem_limit_bytes=14 * 1024 * 1024),
        cost_estimate=pl.CostEstimate(flops=700_000_000, bytes_accessed=6_000_000, transcendentals=700_000),
        name="attend_forward",
    )(pre_qk, pre_v, q_gain, k_gain, cosine, sine, segment_rows, segment_columns)


def attend_backward_kernel(
    pre_qk, rotated, mixed, inverse, grad_mixed, clock, q_gain, k_gain, cosine, sine, segment_rows, segment_columns,
    grad_qk, grad_v, gain_grads, keys, grad_rotated, grad_keys,
):
    offsets = block_offsets()
    for block in range(4):
        keys[128 * block : 128 * (block + 1), :] = rotated[pl.ds(offsets[block], 128), 512:]
    for block in range(3, -1, -1):
        count = 128 * (block + 1)
        allowed = block_mask(block, segment_rows, segment_columns)
        allowed = jnp.concatenate([allowed, allowed], axis=0)
        rows = pl.ds(offsets[block], 128)
        inverse_block = inverse[rows, :]
        for group in range(2):
            def pair(ref):
                return jnp.concatenate(
                    [ref[rows, 256 * group : 256 * group + 128], ref[rows, 256 * group + 128 : 256 * group + 256]],
                    axis=0,
                )
            query, grad_out = pair(rotated), pair(grad_mixed)
            inner = jnp.sum(grad_out.astype(jnp.float32) * pair(mixed).astype(jnp.float32), axis=-1, keepdims=True)
            key = keys[:count, 128 * group : 128 * (group + 1)]
            value = keys[:count, 256 + 128 * group : 256 + 128 * (group + 1)]
            inverse_total = jnp.concatenate(
                [inverse_block[:, 2 * group : 2 * group + 1], inverse_block[:, 2 * group + 1 : 2 * group + 2]], axis=0
            )
            score = lax.dot_general(query, key, NT, preferred_element_type=jnp.float32)
            weight = jnp.exp2(score * (SCALE * LOG2E)) * allowed * inverse_total
            grad_weight = lax.dot_general(grad_out, value, NT, preferred_element_type=jnp.float32)
            grad_score = (weight * (grad_weight - inner)).astype(jnp.bfloat16)
            low = weight.astype(jnp.bfloat16)
            grad_value = lax.dot_general(low, grad_out, TN, preferred_element_type=jnp.float32)
            grad_key = lax.dot_general(grad_score, query, TN, preferred_element_type=jnp.float32)
            grad_query = lax.dot_general(grad_score, key, NN, preferred_element_type=jnp.float32)
            grad_rotated[rows, 256 * group : 256 * group + 128] = grad_query[:128] * SCALE
            grad_rotated[rows, 256 * group + 128 : 256 * group + 256] = grad_query[128:] * SCALE
            spot, value_spot = slice(128 * group, 128 * (group + 1)), slice(256 + 128 * group, 256 + 128 * (group + 1))
            if block == 3:
                grad_keys[:, spot] = grad_key * SCALE
                grad_keys[:, value_spot] = grad_value
            else:
                grad_keys[:count, spot] += grad_key * SCALE
                grad_keys[:count, value_spot] += grad_value
    for block in range(4):
        grad_rotated[pl.ds(offsets[block], 128), 512:] = grad_keys[128 * block : 128 * (block + 1), :]
    cos, sin = cosine[...], sine[...]
    gain_sums = []
    for head in range(6):
        lanes = slice(128 * head, 128 * (head + 1))
        value = pre_qk[:, lanes]
        gain = q_gain[...] if head < 4 else k_gain[...]
        scale = head_norm(value)
        unit = value * scale
        turned = grad_rotated[:, lanes]
        grad = turned * cos + pltpu.roll(turned * sin, 64, 1)
        gain_sums.append(jnp.sum(grad * unit, axis=0, keepdims=True))
        grad = grad * gain
        grad = scale * (grad - unit * jnp.mean(grad * unit, axis=-1, keepdims=True))
        grad_qk[:, lanes] = grad.astype(jnp.bfloat16)
    grad_v[...] = grad_rotated[:, 768:].astype(jnp.bfloat16)
    gain_grads[0:1, :] = gain_sums[0] + gain_sums[1] + gain_sums[2] + gain_sums[3]
    gain_grads[1:2, :] = gain_sums[4] + gain_sums[5]
    gain_grads[2:8, :] = jnp.zeros((6, 128), jnp.float32)


def attend_backward(pre_qk, rotated, mixed, inverse, grad_mixed, clock, q_gain, k_gain, cosine, sine, segment_rows, segment_columns):
    return pl.pallas_call(
        attend_backward_kernel,
        out_shape=(
            jax.ShapeDtypeStruct((512, 768), jnp.bfloat16),
            jax.ShapeDtypeStruct((512, 256), jnp.bfloat16),
            jax.ShapeDtypeStruct((8, 128), jnp.float32),
        ),
        scratch_shapes=[
            pltpu.VMEM((512, 512), jnp.bfloat16),
            pltpu.VMEM((512, 1024), jnp.float32),
            pltpu.VMEM((512, 512), jnp.float32),
        ],
        compiler_params=pltpu.CompilerParams(vmem_limit_bytes=18 * 1024 * 1024),
        cost_estimate=pl.CostEstimate(flops=1_700_000_000, bytes_accessed=8_000_000, transcendentals=700_000),
        name="attend_backward",
    )(pre_qk, rotated, mixed, inverse, grad_mixed, clock, q_gain, k_gain, cosine, sine, segment_rows, segment_columns)


def core_pairs():
    return [(index, index ^ 1) for index in range(4)]


def chip_pairs():
    return [(index, index ^ 2) for index in range(4)]


def dp_shift(stage, step):
    pairs = []
    for z in range(4):
        for x in range(2):
            for y in range(4):
                target = {
                    "y": (z, x, (y + step) % 4),
                    "x": (z, (x + step) % 2, y),
                    "z": ((z + step) % 4, x, y),
                }[stage]
                pairs.append((z * 8 + x * 4 + y, target[0] * 8 + target[1] * 4 + target[2]))
    return pairs


def dp_place():
    index = lax.axis_index("dp")
    return {"z": index // 8, "x": index // 4 % 2, "y": index % 4}


def column_ranges(widths):
    starts = [sum(widths[:index]) for index in range(len(widths))]
    return [pl.ds(start, width) for start, width in zip(starts, widths)]


def ring_gather(block, stage):
    return [(block, 0, None)] + [
        (lax.ppermute(block, "dp", dp_shift(stage, step)), step, None) for step in (1, 2, 3)
    ]


def hold_blocks(blocks, *others):
    arrays = after([block for block, _, _ in blocks], *others)
    return [(array, step, half) for array, (_, step, half) in zip(arrays, blocks)]


def near_gather(block, stage):
    return [(block, 0, None)] + [
        (lax.ppermute(block, "dp", dp_shift(stage, step)), step, None) for step in (1, 3)
    ]


def far_gather(block, stage):
    return [(lax.ppermute(block, "dp", dp_shift(stage, 2)), 2, None)]


def two_step_near(block, stage):
    return (
        block,
        lax.ppermute(block, "dp", dp_shift(stage, 1)),
        lax.ppermute(block, "dp", dp_shift(stage, 3)),
    )


def two_step_far(near, stage):
    block, below, above = near
    half = block.shape[0] // 2
    far_low = lax.ppermute(below[:half], "dp", dp_shift(stage, 1))
    far_high = lax.ppermute(above[half:], "dp", dp_shift(stage, 3))
    return [(block, 0, None), (below, 1, None), (above, 3, None), (far_low, 2, 0), (far_high, 2, 1)]


def place_blocks(blocks, stage, shape, axis, widths):
    places = [(step, half) for _, step, half in blocks]

    def kernel(*refs):
        sources, targets, semaphores = refs[: len(places)], refs[len(places) : -1], refs[-1]
        index = lax.axis_index("dp")
        mine = index // 8 if stage == "z" else index % 4
        copies = []
        for order, (source, (step, half)) in enumerate(zip(sources, places)):
            spot = lax.rem(mine - step + 4, 4)
            rows = source.shape[0]
            rows = pl.ds(0 if half is None else half * rows, rows)
            for number, columns in enumerate(column_ranges(widths)):
                whole = targets[number]
                target = whole.at[spot, rows] if axis == 0 else whole.at[rows, spot]
                copies.append(
                    pltpu.make_async_copy(
                        source.at[..., columns], target, semaphores.at[order, number]
                    )
                )
        for copy in copies:
            copy.start()
        for copy in copies:
            copy.wait()

    arrays = [block for block, _, _ in blocks]
    return pl.pallas_call(
        kernel,
        out_shape=[jax.ShapeDtypeStruct((*shape, width), arrays[0].dtype) for width in widths],
        in_specs=[pl.BlockSpec(memory_space=pl.ANY)] * len(arrays),
        out_specs=[pl.BlockSpec(memory_space=pltpu.VMEM)] * len(widths),
        scratch_shapes=[pltpu.SemaphoreType.DMA((len(arrays), len(widths)))],
        compiler_params=pltpu.CompilerParams(vmem_limit_bytes=8 * 1024 * 1024),
        cost_estimate=pl.CostEstimate(
            flops=0, bytes_accessed=4 * math.prod(shape) * sum(widths), transcendentals=0
        ),
        name="place_blocks",
    )(*arrays)


def pack(pieces):
    pieces = [piece if isinstance(piece, tuple) else (piece, None) for piece in pieces]
    widths = [array.shape[-1] for array, _ in pieces]

    def kernel(*refs):
        sources, whole, semaphores = refs[:-2], refs[-2], refs[-1]
        copies = []
        for number, columns in enumerate(column_ranges(widths)):
            layer = pieces[number][1]
            source = sources[number] if layer is None else sources[number].at[layer]
            copies.append(
                pltpu.make_async_copy(source, whole.at[:, columns], semaphores.at[number])
            )
        for copy in copies:
            copy.start()
        for copy in copies:
            copy.wait()

    return pl.pallas_call(
        kernel,
        out_shape=jax.ShapeDtypeStruct((32, sum(widths)), pieces[0][0].dtype),
        in_specs=[pl.BlockSpec(memory_space=pl.ANY)] * len(pieces),
        out_specs=pl.BlockSpec(memory_space=pltpu.VMEM),
        scratch_shapes=[pltpu.SemaphoreType.DMA((len(pieces),))],
        compiler_params=pltpu.CompilerParams(vmem_limit_bytes=2 * 1024 * 1024),
        cost_estimate=pl.CostEstimate(
            flops=0, bytes_accessed=128 * sum(widths), transcendentals=0
        ),
        name="pack",
    )(*[array for array, _ in pieces])


def split_blocks(parts, stage, axis):
    widths = [part.shape[-1] for part in parts]
    lead = parts[0].shape[:-1]
    shape = (*lead[:axis], *lead[axis + 1 :], sum(widths))

    def kernel(*refs):
        sources, blocks, semaphores = refs[: len(parts)], refs[len(parts) : -1], refs[-1]
        index = lax.axis_index("dp")
        mine = index // 8 if stage == "z" else index % 4
        copies = []
        for step, block in enumerate(blocks):
            spot = lax.rem(mine + step, 4)
            for number, columns in enumerate(column_ranges(widths)):
                source = sources[number]
                piece = source.at[spot] if axis == 0 else source.at[:, spot]
                copies.append(
                    pltpu.make_async_copy(
                        piece, block.at[..., columns], semaphores.at[step, number]
                    )
                )
        for copy in copies:
            copy.start()
        for copy in copies:
            copy.wait()

    return pl.pallas_call(
        kernel,
        out_shape=[jax.ShapeDtypeStruct(shape, parts[0].dtype)] * 4,
        in_specs=[pl.BlockSpec(memory_space=pltpu.VMEM)] * len(parts),
        out_specs=[pl.BlockSpec(memory_space=pl.ANY)] * 4,
        scratch_shapes=[pltpu.SemaphoreType.DMA((4, len(parts)))],
        compiler_params=pltpu.CompilerParams(vmem_limit_bytes=8 * 1024 * 1024),
        cost_estimate=pl.CostEstimate(
            flops=0, bytes_accessed=16 * math.prod(shape), transcendentals=0
        ),
        name="split_blocks",
    )(*parts)


def join_x(block, other):
    return jnp.where(
        dp_place()["x"] == 0, jnp.stack([block, other]), jnp.stack([other, block])
    )


def gather_x(block, *side_work):
    return join_x(block, after(lax.ppermute(block, "dp", dp_shift("x", 1)), *side_work))


def place_first(blocks, stage, widths):
    if stage == "y":
        wholes = place_blocks(blocks, "y", (2, 4, 32), 1, widths)
    else:
        wholes = place_blocks(blocks, "z", (4, 2, 32), 0, widths)
    return [whole.reshape(256, width) for whole, width in zip(wholes, widths)]


def place_last(blocks, stage, widths):
    if stage == "z":
        wholes = place_blocks(blocks, "z", (4, 256), 0, widths)
    else:
        blocks = [
            (block.reshape(-1, 32, sum(widths)), step, half) for block, step, half in blocks
        ]
        wholes = place_blocks(blocks, "y", (8, 4, 32), 1, widths)
    return [whole.reshape(1024, width) for whole, width in zip(wholes, widths)]


def send_near(blocks, stage):
    return [
        blocks[0],
        lax.ppermute(blocks[1], "dp", dp_shift(stage, 1)),
        lax.ppermute(blocks[3], "dp", dp_shift(stage, 3)),
    ]


def send_far(blocks, stage, *others):
    return lax.ppermute(after(blocks[2], *others), "dp", dp_shift(stage, 2))


def near_sum(near):
    return sum(block.astype(jnp.float32) for block in near).astype(jnp.bfloat16)


def far_sum(near, far):
    return (near.astype(jnp.float32) + far.astype(jnp.float32)).astype(jnp.bfloat16)


def split_first(parts, stage):
    if stage == "z":
        blocks = split_blocks([part.reshape(4, 256, -1) for part in parts], "z", 0)
    else:
        blocks = split_blocks([part.reshape(8, 4, 32, -1) for part in parts], "y", 1)
    return blocks


def x_parts(part, first_stage):
    width = part.shape[-1]
    if first_stage == "z":
        low, high = part[:128], part[128:]
    else:
        blocks = part.reshape(4, 2, 32, width)
        low, high = blocks[:, 0].reshape(128, width), blocks[:, 1].reshape(128, width)
    place = dp_place()["x"]
    return jnp.where(place == 0, low, high), jnp.where(place == 0, high, low)


def send_x(part, first_stage):
    return lax.ppermute(x_parts(part, first_stage)[1], "dp", dp_shift("x", 1))


def add_x(part, other, first_stage):
    kept = x_parts(part, first_stage)[0].astype(jnp.float32)
    return (kept + other.astype(jnp.float32)).astype(jnp.bfloat16)


def send_last(parts, stage):
    blocks = jnp.concatenate(parts, axis=1).reshape(4, 32, -1)
    mine = dp_place()[stage]
    return [lax.dynamic_index_in_dim(blocks, mine, 0, False)] + [
        lax.ppermute(
            lax.dynamic_index_in_dim(blocks, (mine + step) % 4, 0, False),
            "dp",
            dp_shift(stage, step),
        )
        for step in (1, 2, 3)
    ]


def sum_last(sent):
    return sum(block.astype(jnp.float32) for block in sent)


def after(values, *others):
    return lax.optimization_barrier((values, others))[0]


def rms_scale(values, gain):
    return (
        values
        * lax.rsqrt(jnp.mean(values * values, axis=-1, keepdims=True) + NORM_EPS)
        * gain
    )


def rms_backward(values, gain, grad):
    scale = lax.rsqrt(jnp.mean(values * values, axis=-1, keepdims=True) + NORM_EPS)
    unit = values * scale
    scaled = grad * gain
    grad_values = scale * (scaled - unit * jnp.mean(scaled * unit, axis=-1, keepdims=True))
    return grad_values, jnp.sum(grad * unit, axis=0)


def dot(left, right):
    return jnp.dot(left, right, preferred_element_type=jnp.float32)


def dot_nt(left, right):
    return lax.dot_general(left, right, NT, preferred_element_type=jnp.float32)


def dot_tn(left, right):
    return lax.dot_general(left, right, TN, preferred_element_type=jnp.float32).astype(
        jnp.bfloat16
    )


def own_block(rows):
    chip = lax.axis_index("tensor") // 2
    blocks = rows.reshape(2, 128, rows.shape[-1])
    return jnp.where(chip == 0, blocks[0], blocks[1])


def both_blocks(block):
    chip = lax.axis_index("tensor") // 2
    other = lax.ppermute(block, "tensor", chip_pairs())
    return jnp.where(
        chip == 0, jnp.concatenate([block, other]), jnp.concatenate([other, block])
    )


def stand_in(*operands):
    def kernel(*refs):
        refs[-1][...] = jnp.zeros_like(refs[-1])

    return pl.pallas_call(
        kernel,
        out_shape=jax.ShapeDtypeStruct((8, 128), jnp.float32),
        in_specs=[pl.BlockSpec(memory_space=pl.ANY)] * len(operands),
        out_specs=pl.BlockSpec(memory_space=pltpu.VMEM),
        compiler_params=pltpu.CompilerParams(vmem_limit_bytes=64 * 1024),
        cost_estimate=pl.CostEstimate(flops=10**11, bytes_accessed=0, transcendentals=0),
        name="stand_in",
    )(*operands)


def wait_for(clock, values):
    clock[0] = stand_in(after(clock[0], values))
    return clock[0]


def exchange(rows, pairs, clock, *side_work):
    other = lax.ppermute(rows, "tensor", pairs)
    if clock is not None:
        side_work = (*side_work, wait_for(clock, rows))
    return after(other, *side_work) if side_work else other


def with_sibling(rows, clock):
    return jnp.concatenate([rows, exchange(rows, core_pairs(), clock)])


def sum_cores(term, clock):
    away = exchange(term(1).astype(jnp.bfloat16), core_pairs(), clock)
    return (term(0) + away.astype(jnp.float32)).astype(jnp.bfloat16)


def sum_chips(part, clock, *side_work):
    other = exchange(part, chip_pairs(), clock, *side_work)
    return part.astype(jnp.float32) + other.astype(jnp.float32)


def sum_own_block(part):
    chip = lax.axis_index("tensor") // 2
    part = part.reshape(2, 128, -1)
    keep = jnp.where(chip == 0, part[0], part[1])
    send = jnp.where(chip == 0, part[1], part[0])
    other = lax.ppermute(send, "tensor", chip_pairs())
    return keep.astype(jnp.float32) + other.astype(jnp.float32)


def halves(array):
    return (array[:256], array[256:])


def rotary_tables(segment_ids):
    width = segment_ids.shape[0]
    core = lax.axis_index("tensor") % 2
    column = jnp.arange(width, dtype=jnp.int32)
    doc_starts = jnp.zeros((width,), jnp.int32)
    for doc_number in range(4):
        before = jnp.sum((segment_ids < doc_number).astype(jnp.int32))
        doc_starts = doc_starts + jnp.where(segment_ids == doc_number, before, 0)
    blocks = (column - doc_starts).astype(jnp.float32).reshape(2, 2, 128)
    position = jnp.where(
        core == 0,
        jnp.concatenate([blocks[:, 0], blocks[:, 1]]),
        jnp.concatenate([blocks[:, 1], blocks[:, 0]]),
    ).reshape(width)
    frequency = jnp.exp(
        jnp.arange(HEAD // 2, dtype=jnp.float32) * (-2.0 * math.log(ROPE_BASE) / HEAD)
    )
    angles = position[:, None] * frequency[None, :]
    cosine, sine = jnp.cos(angles), jnp.sin(angles)
    return (
        jnp.concatenate([cosine, cosine], axis=-1),
        jnp.concatenate([-sine, sine], axis=-1),
    )


def send_direct(blocks):
    return lax.all_to_all(blocks, "dp", 0, 0, tiled=True)


def sum_sent(sent):
    return jnp.sum(sent.reshape(32, 32, -1).astype(jnp.float32), axis=0)


def body(
    tokens,
    segment_ids,
    cotangent,
    attn_norm,
    q_weight,
    key_projection,
    value_projection,
    o_weight,
    q_gain,
    k_gain,
    mlp_norm,
    gate_weight,
    up_weight,
    down_weight,
):
    attend = gather_x(
        pack([(q_weight, 0), (key_projection, 0), (value_projection, 0), o_weight[0].T])
    )
    tokens, transposed = after(
        (tokens, [down_weight[0].T, o_weight[1].T, down_weight[1].T]), attend
    )
    token_blocks = both_blocks(tokens)
    qk_part = place_first(ring_gather(attend[..., :768], "y"), "y", [768])[0]
    vo_part = place_first(ring_gather(attend[..., 768:], "z"), "z", [768])[0]
    qk_blocks, vo_blocks = ring_gather(qk_part, "z"), ring_gather(vo_part, "y")
    rest = pack(
        [
            transposed[0],
            (q_weight, 1),
            (key_projection, 1),
            (value_projection, 1),
            transposed[1],
            transposed[2],
            (gate_weight, 0),
            (up_weight, 0),
            (gate_weight, 1),
            (up_weight, 1),
        ]
    )
    segment_ids = after(segment_ids, qk_part, vo_part)
    cosine, sine = rotary_tables(segment_ids)
    segment_rows, segment_columns = segment_ids[:, None], segment_ids[None, :]
    residual = token_blocks.astype(jnp.float32)
    first_normed = rms_scale(residual, attn_norm[0]).astype(jnp.bfloat16)
    rest = gather_x(rest, first_normed)
    (wqk,) = place_last(qk_blocks, "z", [768])
    wv, wo = place_last(vo_blocks, "y", [256, 512])
    y_blocks = ring_gather(rest[..., :3072], "y")
    z_blocks = near_gather(rest[..., 3072:], "z")
    grad_rows = both_blocks(after(cotangent, wqk)).astype(jnp.float32)
    clock = [jnp.zeros((8, 128), jnp.float32)]
    saved_layers = []
    attend_weights, feed_weights = [(wqk, wv, wo), None], [None, None]
    for layer in range(2):
        wqk, wv, wo = attend_weights[layer]
        gains = (q_gain[layer][None], k_gain[layer][None])
        if layer == 1:
            first_normed = rms_scale(residual, attn_norm[1]).astype(jnp.bfloat16)
        normed = with_sibling(first_normed, clock)
        pre_qk, pre_v = dot(normed, wqk), dot(normed, wv)
        rotated, mixed, inverse = attend_forward(
            pre_qk, pre_v, *gains, cosine, sine, segment_rows, segment_columns
        )
        mixed_halves = halves(mixed)
        part = sum_cores(lambda side: dot_nt(mixed_halves[side], wo), clock)
        side_work = []
        if layer == 0:
            z_blocks += far_gather(after(z_blocks[0][0], mixed), "z")
            y_blocks, z_blocks = hold_blocks(y_blocks, mixed), hold_blocks(z_blocks, mixed)
            down_attend_part, next_down_part = place_first(y_blocks, "y", [2304, 768])
            gate_up_part, next_gate_up_part = place_first(z_blocks, "z", [1536, 1536])
            gate_up_near = two_step_near(gate_up_part, "y")
            down_attend_near = two_step_near(down_attend_part, "z")
        else:
            next_gate_up_near, next_down_near = after((next_gate_up_near, next_down_near), part)
            next_gate_up_blocks = two_step_far(next_gate_up_near, "y")
            next_down_blocks = two_step_far(next_down_near, "z")
        middle = residual + sum_chips(part, clock, *side_work)
        normed_two = with_sibling(
            rms_scale(middle, mlp_norm[layer]).astype(jnp.bfloat16), clock
        )
        if layer == 0:
            wg, wu = place_last(two_step_far(gate_up_near, "y"), "y", [768, 768])
        else:
            wg, wu = place_last(next_gate_up_blocks, "y", [768, 768])
            (wd,) = place_last(next_down_blocks, "z", [768])
        gate, up = dot(normed_two, wg), dot(normed_two, wu)
        product = (jax.nn.silu(gate) * up).astype(jnp.bfloat16)
        if layer == 0:
            wd, wqk, wv, wo = place_last(
                two_step_far(down_attend_near, "z"), "z", [768, 768, 256, 512]
            )
            attend_weights[1] = (wqk, wv, wo)
        feed_weights[layer] = (wg, wu, wd)
        product_halves = halves(product)
        saved_layers.append(
            (residual, middle, normed, normed_two, pre_qk, rotated, mixed, inverse, gate, up, product)
        )
        part = sum_cores(
            lambda side: dot_nt(product_halves[side], wd), clock if layer == 0 else None
        )
        if layer == 0:
            next_gate_up_part, next_down_part = after((next_gate_up_part, next_down_part), part)
            next_gate_up_near = two_step_near(next_gate_up_part, "y")
            next_down_near = two_step_near(next_down_part, "z")
            residual = middle + sum_chips(part, clock)
        else:
            output = own_block(middle) + sum_own_block(part)
    output = output.astype(jnp.bfloat16)
    gain_grads = [None, None]
    for layer in (1, 0):
        wqk, wv, wo = attend_weights[layer]
        wg, wu, wd = feed_weights[layer]
        gains = (q_gain[layer][None], k_gain[layer][None])
        residual, middle, normed, normed_two, pre_qk, rotated, mixed, inverse, gate, up, product = (
            saved_layers[layer]
        )
        grad_out = with_sibling(grad_rows.astype(jnp.bfloat16), clock)
        grad_product = dot(grad_out, wd)
        sigmoid = jax.nn.sigmoid(gate)
        grad_gate = grad_product * up * sigmoid * (1.0 + gate * (1.0 - sigmoid))
        grad_gate = grad_gate.astype(jnp.bfloat16)
        grad_up = (grad_product * gate * sigmoid).astype(jnp.bfloat16)
        gate_halves, up_halves = halves(grad_gate), halves(grad_up)
        part = sum_cores(
            lambda side: dot_nt(gate_halves[side], wg) + dot_nt(up_halves[side], wu), clock
        )
        down_grad = dot_tn(after(grad_out, part), product)
        normed_later = after(normed_two, part)
        gate_grad, up_grad = dot_tn(normed_later, grad_gate), dot_tn(normed_later, grad_up)
        if layer == 1:
            feed_blocks = split_first([gate_grad, up_grad, down_grad], "y")
            feed_near = send_near(feed_blocks, "y")
            side_work = feed_blocks
        else:
            gate_up_blocks = split_first([gate_grad, up_grad], "y")
            gate_up_near = send_near(gate_up_blocks, "y")
            feed_sum = far_sum(feed_near, after(feed_far, part))
            attend_sum = far_sum(near_sum(after(attend_near, part)), after(attend_far, part))
            attend_other = send_x(attend_sum, "z")
            side_work = [*gate_up_blocks, down_grad, feed_sum, attend_sum]
        grad_normed_two = sum_chips(part, clock, *side_work)
        grad_middle, mlp_gain_grad = rms_backward(middle, mlp_norm[layer], grad_normed_two)
        grad_middle = grad_rows + grad_middle
        grad_branch = with_sibling(grad_middle.astype(jnp.bfloat16), clock)
        grad_mixed = dot(grad_branch, wo).astype(jnp.bfloat16)
        o_grad = dot_tn(grad_branch, mixed)
        if layer == 0:
            down_blocks = split_first([o_grad, down_grad], "z")
            down_near = send_near(down_blocks, "z")
            grad_mixed = after(grad_mixed, *down_blocks)
        grad_qk, grad_v, gain_grad = attend_backward(
            pre_qk,
            rotated,
            mixed,
            inverse,
            grad_mixed,
            clock[0],
            *gains,
            cosine,
            sine,
            segment_rows,
            segment_columns,
        )
        qk_halves, v_halves = halves(grad_qk), halves(grad_v)
        terms = [dot_nt(qk_halves[side], wqk) + dot_nt(v_halves[side], wv) for side in range(2)]
        part = sum_cores(lambda side: terms[side], clock if layer == 1 else None)
        normed_later = after(normed, part)
        qk_grad, v_grad = dot_tn(normed_later, grad_qk), dot_tn(normed_later, grad_v)
        if layer == 1:
            attend_blocks = split_first([qk_grad, v_grad, o_grad], "z")
            attend_near = send_near(attend_blocks, "z")
            attend_far = send_far(attend_blocks, "z", part)
            feed_near = near_sum(after(feed_near, part))
            feed_far = send_far(feed_blocks, "y", part)
            grad_in, attn_gain_grad = rms_backward(
                residual, attn_norm[1], sum_chips(part, clock, *attend_blocks, feed_near)
            )
            attn_gain_grad = 0.5 * attn_gain_grad
            grad_rows = grad_middle + grad_in
        else:
            normed_halves = halves(normed)
            attn_gain_grad = sum(
                jnp.sum(terms[side] * normed_halves[side].astype(jnp.float32), axis=0)
                for side in range(2)
            )
            attn_gain_grad = attn_gain_grad / attn_norm[0]
        gain_grads[layer] = (attn_gain_grad, gain_grad[0], gain_grad[1], 0.5 * mlp_gain_grad)
    gain_block = jnp.concatenate([*gain_grads[0], *gain_grads[1]]).reshape(36, 128)
    gain_block = jnp.pad(gain_block, ((0, 28), (0, 0))).reshape(32, 256).astype(jnp.bfloat16)
    last = jnp.concatenate([qk_grad, v_grad, jnp.tile(gain_block, (32, 1))], axis=1)
    feed_other = send_x(after(feed_sum, grad_qk), "y")
    gate_up_near = near_sum(after(gate_up_near, grad_qk))
    gate_up_far = send_far(gate_up_blocks, "y", grad_qk)
    down_far = send_far(down_blocks, "z", grad_qk)
    attend_part = add_x(attend_sum, after(attend_other, grad_qk), "z")
    last = after(last, gate_up_near, attend_part)
    last_sent = send_direct(last)
    mark = stand_in(clock[0], last)
    grad_in, _ = rms_backward(own_block(residual), attn_norm[0], sum_own_block(part))
    input_grad = own_block(grad_middle) + grad_in
    feed_other = after(feed_other, mark)
    gate_up_sum = far_sum(gate_up_near, after(gate_up_far, mark))
    down_sum = far_sum(near_sum(after(down_near, mark)), after(down_far, mark))
    gate_up_other, down_other = send_x(gate_up_sum, "y"), send_x(down_sum, "z")
    last = sum_sent(last_sent)
    gain_sums = last[:, 1024:].reshape(64, 128)[:36]
    gain_sums = gain_sums + lax.ppermute(gain_sums, "tensor", core_pairs())
    gain_sums = gain_sums + lax.ppermute(gain_sums, "tensor", chip_pairs())
    gate_up_other, down_other = after((gate_up_other, down_other), gain_sums)
    feed_sent = send_last(
        [add_x(gate_up_sum, gate_up_other, "y"), add_x(feed_sum, feed_other, "y")], "z"
    )
    attend_sent = send_last(
        [add_x(down_sum, down_other, "z"), attend_part], "y"
    )
    feed_sent, attend_sent = after(feed_sent, attend_sent[0]), after(attend_sent, feed_sent[0])
    feed_own, attend_own = sum_last(feed_sent), sum_last(attend_sent)
    gain_sums = gain_sums.reshape(2, 2304)
    first_gate, first_up, gate, up, down = jnp.split(feed_own, 5, axis=1)
    first_o, first_down, qk, v, o = jnp.split(attend_own, [512, 1280, 2048, 2304], axis=1)
    return (
        output,
        input_grad,
        gain_sums[:, :1024],
        jnp.stack([last[:, :512], qk[:, :512]]),
        jnp.stack([last[:, 512:768], qk[:, 512:]]),
        jnp.stack([last[:, 768:1024], v]),
        jnp.stack([first_o.T, o.T]),
        gain_sums[:, 1024:1152],
        gain_sums[:, 1152:1280],
        gain_sums[:, 1280:],
        jnp.stack([first_gate, gate]),
        jnp.stack([first_up, up]),
        jnp.stack([first_down.T, down.T]),
    )


def solution(mesh):
    rows = P(("dp", "tensor"), None)
    in_rows, in_columns = P(None, "dp", "tensor"), P(None, "tensor", "dp")
    return jax.shard_map(
        body,
        mesh=mesh,
        in_specs=(
            rows,
            P("dp"),
            rows,
            P(),
            in_rows,
            in_rows,
            in_rows,
            in_columns,
            P(),
            P(),
            P(),
            in_rows,
            in_rows,
            in_columns,
        ),
        out_specs=(
            rows,
            rows,
            P(),
            in_rows,
            in_rows,
            in_rows,
            in_columns,
            P(),
            P(),
            P(),
            in_rows,
            in_rows,
            in_columns,
        ),
        check_vma=False,
    )
```

```python
import math

import jax
import jax.numpy as jnp
from jax import lax
from jax.experimental import pallas as pl
from jax.experimental.pallas import tpu as pltpu
from jax.sharding import PartitionSpec as P

ROPE_BASE = 1000000.0
HEAD = 128
SCALE = 128 ** -0.5
LOG2E = 1.0 / math.log(2.0)
NORM_EPS = 1e-6
NT = (((1,), (1,)), ((), ()))
TN = (((0,), (0,)), ((), ()))
NN = (((1,), (0,)), ((), ()))


def block_offsets():
    core = lax.axis_index("tensor") % 2
    return [
        pl.multiple_of(128 * (block // 2 + 2 * ((block + core) % 2)), 128) for block in range(4)
    ]


def block_mask(block, segment_rows, segment_columns):
    keys = 128 * (block + 1)
    row = lax.broadcasted_iota(jnp.int32, (128, keys), 0) + 128 * block
    column = lax.broadcasted_iota(jnp.int32, (128, keys), 1)
    query_segment = segment_rows[128 * block : 128 * (block + 1), :]
    same = query_segment == segment_columns[:, :keys]
    allowed = same & (column <= row) & (query_segment < 3) | (column == row)
    return allowed.astype(jnp.float32)


def head_norm(pre):
    return lax.rsqrt(jnp.mean(pre * pre, axis=-1, keepdims=True) + NORM_EPS)


def attend_forward_kernel(
    pre_qk, pre_v, q_gain, k_gain, cosine, sine, segment_rows, segment_columns, rotated, mixed, inverse, keys
):
    offsets = block_offsets()
    cos, sin = cosine[...], sine[...]
    for head in range(6):
        lanes = slice(128 * head, 128 * (head + 1))
        value = pre_qk[:, lanes]
        gain = q_gain[...] if head < 4 else k_gain[...]
        normed = value * head_norm(value) * gain
        turned = normed * cos + pltpu.roll(normed, 64, 1) * sin
        rotated[:, lanes] = turned.astype(jnp.bfloat16)
    rotated[:, 768:] = pre_v[...].astype(jnp.bfloat16)
    for block in range(4):
        keys[128 * block : 128 * (block + 1), :] = rotated[pl.ds(offsets[block], 128), 512:]
    lane = lax.broadcasted_iota(jnp.int32, (128, 128), 1)
    for block in range(4):
        count = 128 * (block + 1)
        allowed = block_mask(block, segment_rows, segment_columns)
        allowed = jnp.concatenate([allowed, allowed], axis=0)
        rows = pl.ds(offsets[block], 128)
        totals = jnp.zeros((128, 128), jnp.float32)
        for group in range(2):
            query = jnp.concatenate(
                [rotated[rows, 256 * group : 256 * group + 128], rotated[rows, 256 * group + 128 : 256 * group + 256]],
                axis=0,
            )
            key = keys[:count, 128 * group : 128 * (group + 1)]
            value = keys[:count, 256 + 128 * group : 256 + 128 * (group + 1)]
            score = lax.dot_general(query, key, NT, preferred_element_type=jnp.float32)
            weight = jnp.exp2(score * (SCALE * LOG2E)) * allowed
            inverse_total = 1.0 / jnp.sum(weight, axis=-1, keepdims=True)
            out = lax.dot_general((weight * inverse_total).astype(jnp.bfloat16), value, NN, preferred_element_type=jnp.float32)
            out = out.astype(jnp.bfloat16)
            mixed[rows, 256 * group : 256 * group + 128] = out[:128]
            mixed[rows, 256 * group + 128 : 256 * group + 256] = out[128:]
            totals = jnp.where(lane == 2 * group, inverse_total[:128], totals)
            totals = jnp.where(lane == 2 * group + 1, inverse_total[128:], totals)
        inverse[rows, :] = totals


def attend_forward(pre_qk, pre_v, q_gain, k_gain, cosine, sine, segment_rows, segment_columns):
    return pl.pallas_call(
        attend_forward_kernel,
        out_shape=(
            jax.ShapeDtypeStruct((512, 1024), jnp.bfloat16),
            jax.ShapeDtypeStruct((512, 512), jnp.bfloat16),
            jax.ShapeDtypeStruct((512, 128), jnp.float32),
        ),
        scratch_shapes=[pltpu.VMEM((512, 512), jnp.bfloat16)],
        compiler_params=pltpu.CompilerParams(vmem_limit_bytes=14 * 1024 * 1024),
        cost_estimate=pl.CostEstimate(flops=700_000_000, bytes_accessed=6_000_000, transcendentals=700_000),
        name="attend_forward",
    )(pre_qk, pre_v, q_gain, k_gain, cosine, sine, segment_rows, segment_columns)


def attend_backward_kernel(
    pre_qk, rotated, mixed, inverse, grad_mixed, clock, q_gain, k_gain, cosine, sine, segment_rows, segment_columns,
    grad_qk, grad_v, gain_grads, keys, grad_rotated, grad_keys,
):
    offsets = block_offsets()
    for block in range(4):
        keys[128 * block : 128 * (block + 1), :] = rotated[pl.ds(offsets[block], 128), 512:]
    for block in range(3, -1, -1):
        count = 128 * (block + 1)
        allowed = block_mask(block, segment_rows, segment_columns)
        allowed = jnp.concatenate([allowed, allowed], axis=0)
        rows = pl.ds(offsets[block], 128)
        inverse_block = inverse[rows, :]
        for group in range(2):
            def pair(ref):
                return jnp.concatenate(
                    [ref[rows, 256 * group : 256 * group + 128], ref[rows, 256 * group + 128 : 256 * group + 256]],
                    axis=0,
                )
            query, grad_out = pair(rotated), pair(grad_mixed)
            inner = jnp.sum(grad_out.astype(jnp.float32) * pair(mixed).astype(jnp.float32), axis=-1, keepdims=True)
            key = keys[:count, 128 * group : 128 * (group + 1)]
            value = keys[:count, 256 + 128 * group : 256 + 128 * (group + 1)]
            inverse_total = jnp.concatenate(
                [inverse_block[:, 2 * group : 2 * group + 1], inverse_block[:, 2 * group + 1 : 2 * group + 2]], axis=0
            )
            score = lax.dot_general(query, key, NT, preferred_element_type=jnp.float32)
            weight = jnp.exp2(score * (SCALE * LOG2E)) * allowed * inverse_total
            grad_weight = lax.dot_general(grad_out, value, NT, preferred_element_type=jnp.float32)
            grad_score = (weight * (grad_weight - inner)).astype(jnp.bfloat16)
            low = weight.astype(jnp.bfloat16)
            grad_value = lax.dot_general(low, grad_out, TN, preferred_element_type=jnp.float32)
            grad_key = lax.dot_general(grad_score, query, TN, preferred_element_type=jnp.float32)
            grad_query = lax.dot_general(grad_score, key, NN, preferred_element_type=jnp.float32)
            grad_rotated[rows, 256 * group : 256 * group + 128] = grad_query[:128] * SCALE
            grad_rotated[rows, 256 * group + 128 : 256 * group + 256] = grad_query[128:] * SCALE
            spot, value_spot = slice(128 * group, 128 * (group + 1)), slice(256 + 128 * group, 256 + 128 * (group + 1))
            if block == 3:
                grad_keys[:, spot] = grad_key * SCALE
                grad_keys[:, value_spot] = grad_value
            else:
                grad_keys[:count, spot] += grad_key * SCALE
                grad_keys[:count, value_spot] += grad_value
    for block in range(4):
        grad_rotated[pl.ds(offsets[block], 128), 512:] = grad_keys[128 * block : 128 * (block + 1), :]
    cos, sin = cosine[...], sine[...]
    gain_sums = []
    for head in range(6):
        lanes = slice(128 * head, 128 * (head + 1))
        value = pre_qk[:, lanes]
        gain = q_gain[...] if head < 4 else k_gain[...]
        scale = head_norm(value)
        unit = value * scale
        turned = grad_rotated[:, lanes]
        grad = turned * cos + pltpu.roll(turned * sin, 64, 1)
        gain_sums.append(jnp.sum(grad * unit, axis=0, keepdims=True))
        grad = grad * gain
        grad = scale * (grad - unit * jnp.mean(grad * unit, axis=-1, keepdims=True))
        grad_qk[:, lanes] = grad.astype(jnp.bfloat16)
    grad_v[...] = grad_rotated[:, 768:].astype(jnp.bfloat16)
    gain_grads[0:1, :] = gain_sums[0] + gain_sums[1] + gain_sums[2] + gain_sums[3]
    gain_grads[1:2, :] = gain_sums[4] + gain_sums[5]
    gain_grads[2:8, :] = jnp.zeros((6, 128), jnp.float32)


def attend_backward(pre_qk, rotated, mixed, inverse, grad_mixed, clock, q_gain, k_gain, cosine, sine, segment_rows, segment_columns):
    return pl.pallas_call(
        attend_backward_kernel,
        out_shape=(
            jax.ShapeDtypeStruct((512, 768), jnp.bfloat16),
            jax.ShapeDtypeStruct((512, 256), jnp.bfloat16),
            jax.ShapeDtypeStruct((8, 128), jnp.float32),
        ),
        scratch_shapes=[
            pltpu.VMEM((512, 512), jnp.bfloat16),
            pltpu.VMEM((512, 1024), jnp.float32),
            pltpu.VMEM((512, 512), jnp.float32),
        ],
        compiler_params=pltpu.CompilerParams(vmem_limit_bytes=18 * 1024 * 1024),
        cost_estimate=pl.CostEstimate(flops=1_700_000_000, bytes_accessed=8_000_000, transcendentals=700_000),
        name="attend_backward",
    )(pre_qk, rotated, mixed, inverse, grad_mixed, clock, q_gain, k_gain, cosine, sine, segment_rows, segment_columns)


def core_pairs():
    return [(index, index ^ 1) for index in range(4)]


def chip_pairs():
    return [(index, index ^ 2) for index in range(4)]


def dp_shift(stage, step):
    pairs = []
    for z in range(4):
        for x in range(2):
            for y in range(4):
                target = {
                    "y": (z, x, (y + step) % 4),
                    "x": (z, (x + step) % 2, y),
                    "z": ((z + step) % 4, x, y),
                }[stage]
                pairs.append((z * 8 + x * 4 + y, target[0] * 8 + target[1] * 4 + target[2]))
    return pairs


def dp_place():
    index = lax.axis_index("dp")
    return {"z": index // 8, "x": index // 4 % 2, "y": index % 4}


def column_ranges(widths):
    starts = [sum(widths[:index]) for index in range(len(widths))]
    return [pl.ds(start, width) for start, width in zip(starts, widths)]


def ring_gather(block, stage):
    return [(block, 0, None)] + [
        (lax.ppermute(block, "dp", dp_shift(stage, step)), step, None) for step in (1, 2, 3)
    ]


def hold_blocks(blocks, *others):
    arrays = after([block for block, _, _ in blocks], *others)
    return [(array, step, half) for array, (_, step, half) in zip(arrays, blocks)]


def near_gather(block, stage):
    return [(block, 0, None)] + [
        (lax.ppermute(block, "dp", dp_shift(stage, step)), step, None) for step in (1, 3)
    ]


def far_gather(block, stage):
    return [(lax.ppermute(block, "dp", dp_shift(stage, 2)), 2, None)]


def two_step_near(block, stage):
    return (
        block,
        lax.ppermute(block, "dp", dp_shift(stage, 1)),
        lax.ppermute(block, "dp", dp_shift(stage, 3)),
    )


def two_step_far(near, stage):
    block, below, above = near
    half = block.shape[0] // 2
    far_low = lax.ppermute(below[:half], "dp", dp_shift(stage, 1))
    far_high = lax.ppermute(above[half:], "dp", dp_shift(stage, 3))
    return [(block, 0, None), (below, 1, None), (above, 3, None), (far_low, 2, 0), (far_high, 2, 1)]


def place_blocks(blocks, stage, shape, axis, widths):
    places = [(step, half) for _, step, half in blocks]

    def kernel(*refs):
        sources, targets, semaphores = refs[: len(places)], refs[len(places) : -1], refs[-1]
        index = lax.axis_index("dp")
        mine = index // 8 if stage == "z" else index % 4
        copies = []
        for order, (source, (step, half)) in enumerate(zip(sources, places)):
            spot = lax.rem(mine - step + 4, 4)
            rows = source.shape[0]
            rows = pl.ds(0 if half is None else half * rows, rows)
            for number, columns in enumerate(column_ranges(widths)):
                whole = targets[number]
                target = whole.at[spot, rows] if axis == 0 else whole.at[rows, spot]
                copies.append(
                    pltpu.make_async_copy(
                        source.at[..., columns], target, semaphores.at[order, number]
                    )
                )
        for copy in copies:
            copy.start()
        for copy in copies:
            copy.wait()

    arrays = [block for block, _, _ in blocks]
    return pl.pallas_call(
        kernel,
        out_shape=[jax.ShapeDtypeStruct((*shape, width), arrays[0].dtype) for width in widths],
        in_specs=[pl.BlockSpec(memory_space=pl.ANY)] * len(arrays),
        out_specs=[pl.BlockSpec(memory_space=pltpu.VMEM)] * len(widths),
        scratch_shapes=[pltpu.SemaphoreType.DMA((len(arrays), len(widths)))],
        compiler_params=pltpu.CompilerParams(vmem_limit_bytes=8 * 1024 * 1024),
        cost_estimate=pl.CostEstimate(
            flops=0, bytes_accessed=4 * math.prod(shape) * sum(widths), transcendentals=0
        ),
        name="place_blocks",
    )(*arrays)


def pack(pieces):
    pieces = [piece if isinstance(piece, tuple) else (piece, None) for piece in pieces]
    widths = [array.shape[-1] for array, _ in pieces]

    def kernel(*refs):
        sources, whole, semaphores = refs[:-2], refs[-2], refs[-1]
        copies = []
        for number, columns in enumerate(column_ranges(widths)):
            layer = pieces[number][1]
            source = sources[number] if layer is None else sources[number].at[layer]
            copies.append(
                pltpu.make_async_copy(source, whole.at[:, columns], semaphores.at[number])
            )
        for copy in copies:
            copy.start()
        for copy in copies:
            copy.wait()

    return pl.pallas_call(
        kernel,
        out_shape=jax.ShapeDtypeStruct((32, sum(widths)), pieces[0][0].dtype),
        in_specs=[pl.BlockSpec(memory_space=pl.ANY)] * len(pieces),
        out_specs=pl.BlockSpec(memory_space=pltpu.VMEM),
        scratch_shapes=[pltpu.SemaphoreType.DMA((len(pieces),))],
        compiler_params=pltpu.CompilerParams(vmem_limit_bytes=2 * 1024 * 1024),
        cost_estimate=pl.CostEstimate(
            flops=0, bytes_accessed=128 * sum(widths), transcendentals=0
        ),
        name="pack",
    )(*[array for array, _ in pieces])


def split_blocks(parts, stage, axis):
    widths = [part.shape[-1] for part in parts]
    lead = parts[0].shape[:-1]
    shape = (*lead[:axis], *lead[axis + 1 :], sum(widths))

    def kernel(*refs):
        sources, blocks, semaphores = refs[: len(parts)], refs[len(parts) : -1], refs[-1]
        index = lax.axis_index("dp")
        mine = index // 8 if stage == "z" else index % 4
        copies = []
        for step, block in enumerate(blocks):
            spot = lax.rem(mine + step, 4)
            for number, columns in enumerate(column_ranges(widths)):
                source = sources[number]
                piece = source.at[spot] if axis == 0 else source.at[:, spot]
                copies.append(
                    pltpu.make_async_copy(
                        piece, block.at[..., columns], semaphores.at[step, number]
                    )
                )
        for copy in copies:
            copy.start()
        for copy in copies:
            copy.wait()

    return pl.pallas_call(
        kernel,
        out_shape=[jax.ShapeDtypeStruct(shape, parts[0].dtype)] * 4,
        in_specs=[pl.BlockSpec(memory_space=pltpu.VMEM)] * len(parts),
        out_specs=[pl.BlockSpec(memory_space=pl.ANY)] * 4,
        scratch_shapes=[pltpu.SemaphoreType.DMA((4, len(parts)))],
        compiler_params=pltpu.CompilerParams(vmem_limit_bytes=8 * 1024 * 1024),
        cost_estimate=pl.CostEstimate(
            flops=0, bytes_accessed=16 * math.prod(shape), transcendentals=0
        ),
        name="split_blocks",
    )(*parts)


def join_x(block, other):
    return jnp.where(
        dp_place()["x"] == 0, jnp.stack([block, other]), jnp.stack([other, block])
    )


def gather_x(block, *side_work):
    return join_x(block, after(lax.ppermute(block, "dp", dp_shift("x", 1)), *side_work))


def place_first(blocks, stage, widths):
    if stage == "y":
        wholes = place_blocks(blocks, "y", (2, 4, 32), 1, widths)
    else:
        wholes = place_blocks(blocks, "z", (4, 2, 32), 0, widths)
    return [whole.reshape(256, width) for whole, width in zip(wholes, widths)]


def place_last(blocks, stage, widths):
    if stage == "z":
        wholes = place_blocks(blocks, "z", (4, 256), 0, widths)
    else:
        blocks = [
            (block.reshape(-1, 32, sum(widths)), step, half) for block, step, half in blocks
        ]
        wholes = place_blocks(blocks, "y", (8, 4, 32), 1, widths)
    return [whole.reshape(1024, width) for whole, width in zip(wholes, widths)]


def send_near(blocks, stage):
    return [
        blocks[0],
        lax.ppermute(blocks[1], "dp", dp_shift(stage, 1)),
        lax.ppermute(blocks[3], "dp", dp_shift(stage, 3)),
    ]


def send_far(blocks, stage, *others):
    return lax.ppermute(after(blocks[2], *others), "dp", dp_shift(stage, 2))


def near_sum(near):
    return sum(block.astype(jnp.float32) for block in near).astype(jnp.bfloat16)


def far_sum(near, far):
    return (near.astype(jnp.float32) + far.astype(jnp.float32)).astype(jnp.bfloat16)


def split_first(parts, stage):
    if stage == "z":
        blocks = split_blocks([part.reshape(4, 256, -1) for part in parts], "z", 0)
    else:
        blocks = split_blocks([part.reshape(8, 4, 32, -1) for part in parts], "y", 1)
    return blocks


def x_parts(part, first_stage):
    width = part.shape[-1]
    if first_stage == "z":
        low, high = part[:128], part[128:]
    else:
        blocks = part.reshape(4, 2, 32, width)
        low, high = blocks[:, 0].reshape(128, width), blocks[:, 1].reshape(128, width)
    place = dp_place()["x"]
    return jnp.where(place == 0, low, high), jnp.where(place == 0, high, low)


def send_x(part, first_stage):
    return lax.ppermute(x_parts(part, first_stage)[1], "dp", dp_shift("x", 1))


def add_x(part, other, first_stage):
    kept = x_parts(part, first_stage)[0].astype(jnp.float32)
    return (kept + other.astype(jnp.float32)).astype(jnp.bfloat16)


def send_last(parts, stage):
    blocks = jnp.concatenate(parts, axis=1).reshape(4, 32, -1)
    mine = dp_place()[stage]
    return [lax.dynamic_index_in_dim(blocks, mine, 0, False)] + [
        lax.ppermute(
            lax.dynamic_index_in_dim(blocks, (mine + step) % 4, 0, False),
            "dp",
            dp_shift(stage, step),
        )
        for step in (1, 2, 3)
    ]


def sum_last(sent):
    return sum(block.astype(jnp.float32) for block in sent)


def after(values, *others):
    return lax.optimization_barrier((values, others))[0]


def rms_scale(values, gain):
    return (
        values
        * lax.rsqrt(jnp.mean(values * values, axis=-1, keepdims=True) + NORM_EPS)
        * gain
    )


def rms_backward(values, gain, grad):
    scale = lax.rsqrt(jnp.mean(values * values, axis=-1, keepdims=True) + NORM_EPS)
    unit = values * scale
    scaled = grad * gain
    grad_values = scale * (scaled - unit * jnp.mean(scaled * unit, axis=-1, keepdims=True))
    return grad_values, jnp.sum(grad * unit, axis=0)


def dot(left, right):
    return jnp.dot(left, right, preferred_element_type=jnp.float32)


def dot_nt(left, right):
    return lax.dot_general(left, right, NT, preferred_element_type=jnp.float32)


def dot_tn(left, right):
    return lax.dot_general(left, right, TN, preferred_element_type=jnp.float32).astype(
        jnp.bfloat16
    )


def own_block(rows):
    chip = lax.axis_index("tensor") // 2
    blocks = rows.reshape(2, 128, rows.shape[-1])
    return jnp.where(chip == 0, blocks[0], blocks[1])


def both_blocks(block):
    chip = lax.axis_index("tensor") // 2
    other = lax.ppermute(block, "tensor", chip_pairs())
    return jnp.where(
        chip == 0, jnp.concatenate([block, other]), jnp.concatenate([other, block])
    )


def stand_in(*operands):
    def kernel(*refs):
        refs[-1][...] = jnp.zeros_like(refs[-1])

    return pl.pallas_call(
        kernel,
        out_shape=jax.ShapeDtypeStruct((8, 128), jnp.float32),
        in_specs=[pl.BlockSpec(memory_space=pl.ANY)] * len(operands),
        out_specs=pl.BlockSpec(memory_space=pltpu.VMEM),
        compiler_params=pltpu.CompilerParams(vmem_limit_bytes=64 * 1024),
        cost_estimate=pl.CostEstimate(flops=10**11, bytes_accessed=0, transcendentals=0),
        name="stand_in",
    )(*operands)


def wait_for(clock, values):
    clock[0] = stand_in(after(clock[0], values))
    return clock[0]


def exchange(rows, pairs, clock, *side_work):
    other = lax.ppermute(rows, "tensor", pairs)
    if clock is not None:
        side_work = (*side_work, wait_for(clock, rows))
    return after(other, *side_work) if side_work else other


def with_sibling(rows, clock):
    return jnp.concatenate([rows, exchange(rows, core_pairs(), None)])


def sum_cores(term, clock):
    away = exchange(term(1).astype(jnp.bfloat16), core_pairs(), None)
    return (term(0) + away.astype(jnp.float32)).astype(jnp.bfloat16)


def sum_chips(part, clock, *side_work):
    other = exchange(part, chip_pairs(), clock, *side_work)
    return part.astype(jnp.float32) + other.astype(jnp.float32)


def sum_own_block(part):
    chip = lax.axis_index("tensor") // 2
    part = part.reshape(2, 128, -1)
    keep = jnp.where(chip == 0, part[0], part[1])
    send = jnp.where(chip == 0, part[1], part[0])
    other = lax.ppermute(send, "tensor", chip_pairs())
    return keep.astype(jnp.float32) + other.astype(jnp.float32)


def halves(array):
    return (array[:256], array[256:])


def rotary_tables(segment_ids):
    width = segment_ids.shape[0]
    core = lax.axis_index("tensor") % 2
    column = jnp.arange(width, dtype=jnp.int32)
    doc_starts = jnp.zeros((width,), jnp.int32)
    for doc_number in range(4):
        before = jnp.sum((segment_ids < doc_number).astype(jnp.int32))
        doc_starts = doc_starts + jnp.where(segment_ids == doc_number, before, 0)
    blocks = (column - doc_starts).astype(jnp.float32).reshape(2, 2, 128)
    position = jnp.where(
        core == 0,
        jnp.concatenate([blocks[:, 0], blocks[:, 1]]),
        jnp.concatenate([blocks[:, 1], blocks[:, 0]]),
    ).reshape(width)
    frequency = jnp.exp(
        jnp.arange(HEAD // 2, dtype=jnp.float32) * (-2.0 * math.log(ROPE_BASE) / HEAD)
    )
    angles = position[:, None] * frequency[None, :]
    cosine, sine = jnp.cos(angles), jnp.sin(angles)
    return (
        jnp.concatenate([cosine, cosine], axis=-1),
        jnp.concatenate([-sine, sine], axis=-1),
    )


def send_direct(blocks):
    return lax.all_to_all(blocks, "dp", 0, 0, tiled=True)


def sum_sent(sent):
    return jnp.sum(sent.reshape(32, 32, -1).astype(jnp.float32), axis=0)


def body(
    tokens,
    segment_ids,
    cotangent,
    attn_norm,
    q_weight,
    key_projection,
    value_projection,
    o_weight,
    q_gain,
    k_gain,
    mlp_norm,
    gate_weight,
    up_weight,
    down_weight,
):
    attend = gather_x(
        pack([(q_weight, 0), (key_projection, 0), (value_projection, 0), o_weight[0].T])
    )
    tokens, transposed = after(
        (tokens, [down_weight[0].T, o_weight[1].T, down_weight[1].T]), attend
    )
    token_blocks = both_blocks(tokens)
    qk_part = place_first(ring_gather(attend[..., :768], "y"), "y", [768])[0]
    vo_part = place_first(ring_gather(attend[..., 768:], "z"), "z", [768])[0]
    qk_blocks, vo_blocks = ring_gather(qk_part, "z"), ring_gather(vo_part, "y")
    rest = pack(
        [
            transposed[0],
            (q_weight, 1),
            (key_projection, 1),
            (value_projection, 1),
            transposed[1],
            transposed[2],
            (gate_weight, 0),
            (up_weight, 0),
            (gate_weight, 1),
            (up_weight, 1),
        ]
    )
    segment_ids = after(segment_ids, qk_part, vo_part)
    cosine, sine = rotary_tables(segment_ids)
    segment_rows, segment_columns = segment_ids[:, None], segment_ids[None, :]
    residual = token_blocks.astype(jnp.float32)
    first_normed = rms_scale(residual, attn_norm[0]).astype(jnp.bfloat16)
    rest = gather_x(rest, first_normed)
    (wqk,) = place_last(qk_blocks, "z", [768])
    wv, wo = place_last(vo_blocks, "y", [256, 512])
    y_blocks = ring_gather(rest[..., :3072], "y")
    z_blocks = near_gather(rest[..., 3072:], "z")
    grad_rows = both_blocks(after(cotangent, wqk)).astype(jnp.float32)
    clock = [jnp.zeros((8, 128), jnp.float32)]
    saved_layers = []
    attend_weights, feed_weights = [(wqk, wv, wo), None], [None, None]
    for layer in range(2):
        wqk, wv, wo = attend_weights[layer]
        gains = (q_gain[layer][None], k_gain[layer][None])
        if layer == 1:
            first_normed = rms_scale(residual, attn_norm[1]).astype(jnp.bfloat16)
        normed = with_sibling(first_normed, clock)
        pre_qk, pre_v = dot(normed, wqk), dot(normed, wv)
        rotated, mixed, inverse = attend_forward(
            pre_qk, pre_v, *gains, cosine, sine, segment_rows, segment_columns
        )
        mixed_halves = halves(mixed)
        part = sum_cores(lambda side: dot_nt(mixed_halves[side], wo), clock)
        side_work = []
        if layer == 0:
            z_blocks += far_gather(after(z_blocks[0][0], mixed), "z")
            y_blocks, z_blocks = hold_blocks(y_blocks, mixed), hold_blocks(z_blocks, mixed)
            down_attend_part, next_down_part = place_first(y_blocks, "y", [2304, 768])
            gate_up_part, next_gate_up_part = place_first(z_blocks, "z", [1536, 1536])
            gate_up_near = two_step_near(gate_up_part, "y")
            down_attend_near = two_step_near(down_attend_part, "z")
        else:
            next_gate_up_near, next_down_near = after((next_gate_up_near, next_down_near), part)
            next_gate_up_blocks = two_step_far(next_gate_up_near, "y")
            next_down_blocks = two_step_far(next_down_near, "z")
        middle = residual + sum_chips(part, clock, *side_work)
        normed_two = with_sibling(
            rms_scale(middle, mlp_norm[layer]).astype(jnp.bfloat16), clock
        )
        if layer == 0:
            wg, wu = place_last(two_step_far(gate_up_near, "y"), "y", [768, 768])
        else:
            wg, wu = place_last(next_gate_up_blocks, "y", [768, 768])
            (wd,) = place_last(next_down_blocks, "z", [768])
        gate, up = dot(normed_two, wg), dot(normed_two, wu)
        product = (jax.nn.silu(gate) * up).astype(jnp.bfloat16)
        if layer == 0:
            wd, wqk, wv, wo = place_last(
                two_step_far(down_attend_near, "z"), "z", [768, 768, 256, 512]
            )
            attend_weights[1] = (wqk, wv, wo)
        feed_weights[layer] = (wg, wu, wd)
        product_halves = halves(product)
        saved_layers.append(
            (residual, middle, normed, normed_two, pre_qk, rotated, mixed, inverse, gate, up, product)
        )
        part = sum_cores(
            lambda side: dot_nt(product_halves[side], wd), clock if layer == 0 else None
        )
        if layer == 0:
            next_gate_up_part, next_down_part = after((next_gate_up_part, next_down_part), part)
            next_gate_up_near = two_step_near(next_gate_up_part, "y")
            next_down_near = two_step_near(next_down_part, "z")
            residual = middle + sum_chips(part, clock)
        else:
            output = own_block(middle) + sum_own_block(part)
    output = output.astype(jnp.bfloat16)
    gain_grads = [None, None]
    for layer in (1, 0):
        wqk, wv, wo = attend_weights[layer]
        wg, wu, wd = feed_weights[layer]
        gains = (q_gain[layer][None], k_gain[layer][None])
        residual, middle, normed, normed_two, pre_qk, rotated, mixed, inverse, gate, up, product = (
            saved_layers[layer]
        )
        grad_out = with_sibling(grad_rows.astype(jnp.bfloat16), clock)
        grad_product = dot(grad_out, wd)
        sigmoid = jax.nn.sigmoid(gate)
        grad_gate = grad_product * up * sigmoid * (1.0 + gate * (1.0 - sigmoid))
        grad_gate = grad_gate.astype(jnp.bfloat16)
        grad_up = (grad_product * gate * sigmoid).astype(jnp.bfloat16)
        gate_halves, up_halves = halves(grad_gate), halves(grad_up)
        part = sum_cores(
            lambda side: dot_nt(gate_halves[side], wg) + dot_nt(up_halves[side], wu), clock
        )
        down_grad = dot_tn(after(grad_out, part), product)
        normed_later = after(normed_two, part)
        gate_grad, up_grad = dot_tn(normed_later, grad_gate), dot_tn(normed_later, grad_up)
        if layer == 1:
            feed_blocks = split_first([gate_grad, up_grad, down_grad], "y")
            feed_near = send_near(feed_blocks, "y")
            side_work = feed_blocks
        else:
            gate_up_blocks = split_first([gate_grad, up_grad], "y")
            gate_up_near = send_near(gate_up_blocks, "y")
            feed_sum = far_sum(feed_near, after(feed_far, part))
            attend_sum = far_sum(near_sum(after(attend_near, part)), after(attend_far, part))
            attend_other = send_x(attend_sum, "z")
            side_work = [*gate_up_blocks, down_grad, feed_sum, attend_sum]
        grad_normed_two = sum_chips(part, clock, *side_work)
        grad_middle, mlp_gain_grad = rms_backward(middle, mlp_norm[layer], grad_normed_two)
        grad_middle = grad_rows + grad_middle
        grad_branch = with_sibling(grad_middle.astype(jnp.bfloat16), clock)
        grad_mixed = dot(grad_branch, wo).astype(jnp.bfloat16)
        o_grad = dot_tn(grad_branch, mixed)
        if layer == 0:
            down_blocks = split_first([o_grad, down_grad], "z")
            down_near = send_near(down_blocks, "z")
            grad_mixed = after(grad_mixed, *down_blocks)
        grad_qk, grad_v, gain_grad = attend_backward(
            pre_qk,
            rotated,
            mixed,
            inverse,
            grad_mixed,
            clock[0],
            *gains,
            cosine,
            sine,
            segment_rows,
            segment_columns,
        )
        qk_halves, v_halves = halves(grad_qk), halves(grad_v)
        terms = [dot_nt(qk_halves[side], wqk) + dot_nt(v_halves[side], wv) for side in range(2)]
        part = sum_cores(lambda side: terms[side], clock if layer == 1 else None)
        normed_later = after(normed, part)
        qk_grad, v_grad = dot_tn(normed_later, grad_qk), dot_tn(normed_later, grad_v)
        if layer == 1:
            attend_blocks = split_first([qk_grad, v_grad, o_grad], "z")
            attend_near = send_near(attend_blocks, "z")
            attend_far = send_far(attend_blocks, "z", part)
            feed_near = near_sum(after(feed_near, part))
            feed_far = send_far(feed_blocks, "y", part)
            grad_in, attn_gain_grad = rms_backward(
                residual, attn_norm[1], sum_chips(part, clock, *attend_blocks, feed_near)
            )
            attn_gain_grad = 0.5 * attn_gain_grad
            grad_rows = grad_middle + grad_in
        else:
            normed_halves = halves(normed)
            attn_gain_grad = sum(
                jnp.sum(terms[side] * normed_halves[side].astype(jnp.float32), axis=0)
                for side in range(2)
            )
            attn_gain_grad = attn_gain_grad / attn_norm[0]
        gain_grads[layer] = (attn_gain_grad, gain_grad[0], gain_grad[1], 0.5 * mlp_gain_grad)
    gain_block = jnp.concatenate([*gain_grads[0], *gain_grads[1]]).reshape(36, 128)
    gain_block = jnp.pad(gain_block, ((0, 28), (0, 0))).reshape(32, 256).astype(jnp.bfloat16)
    last = jnp.concatenate([qk_grad, v_grad, jnp.tile(gain_block, (32, 1))], axis=1)
    feed_other = send_x(after(feed_sum, grad_qk), "y")
    gate_up_near = near_sum(after(gate_up_near, grad_qk))
    gate_up_far = send_far(gate_up_blocks, "y", grad_qk)
    down_far = send_far(down_blocks, "z", grad_qk)
    attend_part = add_x(attend_sum, after(attend_other, grad_qk), "z")
    last = after(last, gate_up_near, attend_part)
    last_sent = send_direct(last)
    mark = stand_in(clock[0], last)
    grad_in, _ = rms_backward(own_block(residual), attn_norm[0], sum_own_block(part))
    input_grad = own_block(grad_middle) + grad_in
    feed_other = after(feed_other, mark)
    gate_up_sum = far_sum(gate_up_near, after(gate_up_far, mark))
    down_sum = far_sum(near_sum(after(down_near, mark)), after(down_far, mark))
    gate_up_other, down_other = send_x(gate_up_sum, "y"), send_x(down_sum, "z")
    last = sum_sent(last_sent)
    gain_sums = last[:, 1024:].reshape(64, 128)[:36]
    gain_sums = gain_sums + lax.ppermute(gain_sums, "tensor", core_pairs())
    gain_sums = gain_sums + lax.ppermute(gain_sums, "tensor", chip_pairs())
    gate_up_other, down_other = after((gate_up_other, down_other), gain_sums)
    feed_sent = send_last(
        [add_x(gate_up_sum, gate_up_other, "y"), add_x(feed_sum, feed_other, "y")], "z"
    )
    attend_sent = send_last(
        [add_x(down_sum, down_other, "z"), attend_part], "y"
    )
    feed_sent, attend_sent = after(feed_sent, attend_sent[0]), after(attend_sent, feed_sent[0])
    feed_own, attend_own = sum_last(feed_sent), sum_last(attend_sent)
    gain_sums = gain_sums.reshape(2, 2304)
    first_gate, first_up, gate, up, down = jnp.split(feed_own, 5, axis=1)
    first_o, first_down, qk, v, o = jnp.split(attend_own, [512, 1280, 2048, 2304], axis=1)
    return (
        output,
        input_grad,
        gain_sums[:, :1024],
        jnp.stack([last[:, :512], qk[:, :512]]),
        jnp.stack([last[:, 512:768], qk[:, 512:]]),
        jnp.stack([last[:, 768:1024], v]),
        jnp.stack([first_o.T, o.T]),
        gain_sums[:, 1024:1152],
        gain_sums[:, 1152:1280],
        gain_sums[:, 1280:],
        jnp.stack([first_gate, gate]),
        jnp.stack([first_up, up]),
        jnp.stack([first_down.T, down.T]),
    )


def solution(mesh):
    rows = P(("dp", "tensor"), None)
    in_rows, in_columns = P(None, "dp", "tensor"), P(None, "tensor", "dp")
    return jax.shard_map(
        body,
        mesh=mesh,
        in_specs=(
            rows,
            P("dp"),
            rows,
            P(),
            in_rows,
            in_rows,
            in_rows,
            in_columns,
            P(),
            P(),
            P(),
            in_rows,
            in_rows,
            in_columns,
        ),
        out_specs=(
            rows,
            rows,
            P(),
            in_rows,
            in_rows,
            in_rows,
            in_columns,
            P(),
            P(),
            P(),
            in_rows,
            in_rows,
            in_columns,
        ),
        check_vma=False,
    )
```
